32 devices in a mesh: row: 16 (over z, y, core), col: 2 (over x).
Axes of the slice: x: 2, y: 2, z: 4, core: 2. Of those that a mesh axis runs over, the one named last changes fastest.
Arguments:
- blocks: bfloat16 [160, 72, 128, 128], P('row', 'col')
- slot_cols: int32 [160, 72], P('row', 'col'), may hold values from 0 to 79, as said below
- counts: int32 [160, 2], P('row', 'col'), may hold values from 2 to 36, as said below
- demand: bfloat16 [20480, 128], P('col'), may hold values from 0.1 to 10
- value_added: float32 [20480], P('col'), may hold values from 0.5 to 5
Outputs:
- propagated: bfloat16 [20480, 128], P('row')
The draws below stay inside these ranges and needn't reach their ends.
Inputs may be any that keep to these rules, and one draw needn't show every extreme that they name: `counts`: some block row has all 36 slots live in every column group; live slots come first in each group. `slot_cols`: within one block row and column group the 36 slots name distinct column blocks.
All inputs are finite; a program needn't handle non-finite values.
Results may differ from the reference program's by a relative error of at most 0.0042.
Values may be sent and summed in bfloat16 or wider, within the bound.
No kernel may reach another device: no remote copies, remote signals or barrier semaphores. Data moves between devices by JAX's collectives and lax.ppermute only.
A program may use at most 128 MiB of HBM per device.

```python
import math
import jax
import jax.numpy as jnp
from jax import lax

BS = 128
DC = 128
P_SIZE = 36
NB = 160
CB = 80
N_COL = 2


def pattern(key):
    base = jax.random.fold_in(key, 7)
    key_heavy, key_chosen, key_light, key_order = jax.random.split(base, 4)
    heavy = jax.random.randint(key_heavy, (NB, 1), 0, 6) == 0
    chosen = jax.random.randint(key_chosen, (), 0, NB)
    heavy = heavy | (jnp.arange(NB)[:, None] == chosen)
    light = jax.random.randint(key_light, (NB, N_COL), 2, max(P_SIZE // 3, 2) + 1)
    counts = jnp.where(heavy, P_SIZE, light).astype(jnp.int32)
    scores = jax.random.randint(key_order, (NB, N_COL, CB), 0, 1 << 20) * CB + jnp.arange(CB)[None, None, :]
    order = jnp.argsort(scores, axis=-1, stable=True)[:, :, :P_SIZE]
    return (counts, order.reshape(NB, N_COL * P_SIZE).astype(jnp.int32))


def draw_counts(key, part):
    return pattern(key)[0]


def draw_slot_cols(key, part):
    return pattern(key)[1]


def draw_blocks(key, part):
    base = jax.random.fold_in(key, 11)
    key_entry, key_block, key_column = jax.random.split(base, 3)
    slots = N_COL * P_SIZE
    block_scale = jnp.exp(jax.random.uniform(key_block, (NB, slots, 1, 1), minval=math.log(0.03), maxval=math.log(30.0)))
    column_scale = jnp.exp(jax.random.uniform(key_column, (NB, slots, 1, BS), minval=0.0, maxval=math.log(10.0)))
    factor = 1.0 / (BS * N_COL * P_SIZE)
    uniform_part = jax.random.uniform(key_entry, (NB, slots, BS, BS), minval=0.0, maxval=1.0)
    spread_ratio = 2000.0
    entries = 0.5 / math.log(1.0 + spread_ratio) / (uniform_part + 1.0 / spread_ratio)
    values = entries * block_scale * column_scale * factor
    return values.astype(jnp.bfloat16)


def draw_demand(key, part):
    base = jax.random.fold_in(key, 13)
    key_own, key_shared = jax.random.split(base, 2)
    groups = NB * BS // 16
    own_reach = 1.15
    shared_reach = 1.15
    own_part = jax.random.uniform(key_own, (groups, 16, DC), minval=-own_reach, maxval=own_reach)
    shared_part = jax.random.uniform(key_shared, (groups, 1, DC), minval=-shared_reach, maxval=shared_reach)
    values = jnp.exp(own_part + shared_part).reshape(NB * BS, DC)
    return values.astype(jnp.bfloat16)


def block_levels(stream_key, dims, cuts, smallest, high):
    def one(dim, shards_of):
        steps = jax.random.uniform(jax.random.fold_in(jax.random.fold_in(stream_key, 6), dim), (shards_of,), jnp.float32, smallest / len(cuts), high / len(cuts))
        return jnp.repeat(jnp.exp(steps), dims[dim] // shards_of).reshape((-1,) + (1,) * (len(dims) - dim - 1))

    level = one(*cuts[0])
    for cut in cuts[1:]:
        level = level * one(*cut)
    return level


def setup_inputs(seed: int = 0) -> dict:
    splits = jax.random.split(jax.random.key(seed), 6)
    return {
        "blocks": draw_blocks(jax.random.fold_in(splits[5], 71), 0),
        "slot_cols": draw_slot_cols(jax.random.fold_in(splits[5], 71), 0),
        "counts": draw_counts(jax.random.fold_in(splits[5], 71), 0),
        "demand": draw_demand(jax.random.fold_in(splits[5], 71), 0),
        "value_added": jnp.clip(jnp.exp(math.log(5.0) - 2.3025851 * jax.random.uniform(splits[4], (NB * BS,), jnp.float32) ** block_levels(splits[4], (NB * BS,), ((0, 2),), -0.2, 0.2)), 0.5, 5.0),
    }


def reference(blocks, slot_cols, counts, demand, value_added):
    slots = blocks.shape[1]
    position = jnp.arange(slots, dtype=jnp.int32)
    group_of = position // P_SIZE
    columns = (group_of[None, :] * CB + slot_cols).astype(jnp.int32)
    live_slots = ((position % P_SIZE)[None, :] < counts[:, group_of]).astype(jnp.float32)
    column_sums = lax.map(lambda zblock: jnp.sum(zblock.astype(jnp.float32), axis=1), blocks)
    column_sums = column_sums * live_slots[:, :, None]
    totals = jax.ops.segment_sum(column_sums.reshape(-1, BS), columns.reshape(-1), num_segments=NB)
    totals = totals.reshape(-1) + value_added
    inverse = (1.0 / totals).reshape(NB, BS)

    def layer(source):
        def one_row(items):
            zblock, column_row, live_row = items
            scaling = inverse[column_row] * live_row[:, None]
            coefficients = (zblock.astype(jnp.float32) * scaling[:, None, :]).astype(jnp.bfloat16)
            picked = source[column_row]
            return jnp.einsum("sij,sjk->ik", coefficients.astype(jnp.float32), picked.astype(jnp.float32))
        return lax.map(one_row, (blocks, columns, live_slots))

    layer_one = layer(demand.reshape(NB, BS, DC)).astype(jnp.bfloat16)
    layer_two = layer(layer_one)
    result = (layer_one.astype(jnp.float32) + layer_two).astype(jnp.bfloat16)
    return result.reshape(NB * BS, DC)
```

```python
import functools

import jax
import jax.numpy as jnp
from jax import lax
from jax.experimental import pallas as pl
from jax.experimental.pallas import tpu as pltpu
from jax.sharding import PartitionSpec as P

VMEM_LIMIT = 40 * 1024 * 1024


def chunk_of(slot_count):
    for size in (4, 3, 2):
        if slot_count % size == 0:
            return size
    return 1


def chunk_total(counts_ref, b, chunk):
    return lax.div(counts_ref[b, 0] + (chunk - 1), chunk)


def sums_kernel(cols_ref, counts_ref, blocks_ref, sums_ref, held_ref, acc_ref, sems):
    rows, slots, size, _ = blocks_ref.shape
    groups = sums_ref.shape[0]
    chunk = chunk_of(slots)

    def fetch(b, k):
        part = pl.ds(k * chunk, chunk)
        return pltpu.make_async_copy(blocks_ref.at[b, part], held_ref.at[b, part], sems.at[b])

    for b in range(rows):

        def start(k, carry, b=b):
            fetch(b, k).start()
            return carry

        lax.fori_loop(0, chunk_total(counts_ref, b, chunk), start, 0)
    acc_ref[...] = jnp.zeros_like(acc_ref)
    for b in range(rows):
        total = chunk_total(counts_ref, b, chunk)

        def finish(k, carry, b=b):
            fetch(b, k).wait()
            return carry

        lax.fori_loop(0, total, finish, 0)

        def add(k, carry, b=b):
            for u in range(chunk):
                slot = k * chunk + u
                col = jnp.where(slot < counts_ref[b, 0], cols_ref[b, slot], groups)
                block = held_ref[b, slot].astype(jnp.float32)
                acc_ref[col] += jnp.sum(block.reshape(size // 8, 8, size), axis=0)
            return carry

        lax.fori_loop(0, total, add, 0)
    sums_ref[...] = jnp.sum(acc_ref[:groups], axis=1)


def first_kernel(cols_ref, counts_ref, sums_ref, added_ref, demand_ref, blocks_ref, out_ref, coef_ref, inverse_ref):
    rows, slots, size, _ = blocks_ref.shape
    chunk = chunk_of(slots)
    inverse_ref[...] = (1.0 / (jnp.sum(sums_ref[...], axis=0) + added_ref[...]))[:, None, :]
    for b in range(rows):

        def add(k, acc, b=b):
            left, right = [], []
            for u in range(chunk):
                slot = k * chunk + u
                col = cols_ref[b, slot]
                live = (slot < counts_ref[b, 0]).astype(jnp.float32)
                scale = inverse_ref[col] * live
                coef = (blocks_ref[b, slot].astype(jnp.float32) * scale).astype(jnp.bfloat16)
                coef_ref[b, slot] = coef
                left.append(coef)
                right.append(demand_ref[col])
            return acc + jnp.dot(
                jnp.concatenate(left, axis=1), jnp.concatenate(right, axis=0), preferred_element_type=jnp.float32
            )

        out_ref[b] = lax.fori_loop(
            0, chunk_total(counts_ref, b, chunk), add, jnp.zeros((size, out_ref.shape[2]), jnp.float32)
        ).astype(out_ref.dtype)


def second_kernel(place, cols_ref, counts_ref, source_ref, coef_ref, out_ref):
    rows, slots, size, _ = coef_ref.shape
    chunk = chunk_of(slots)
    for b in range(rows):

        def add(k, acc, b=b):
            left, right = [], []
            for u in range(chunk):
                slot = k * chunk + u
                left.append(coef_ref[b, slot])
                right.append(source_ref[place(cols_ref[b, slot])])
            return acc + jnp.dot(
                jnp.concatenate(left, axis=1), jnp.concatenate(right, axis=0), preferred_element_type=jnp.float32
            )

        out_ref[b] = lax.fori_loop(
            0, chunk_total(counts_ref, b, chunk), add, jnp.zeros((size, out_ref.shape[2]), jnp.float32)
        ).astype(out_ref.dtype)


SMEM = pl.BlockSpec(memory_space=pltpu.SMEM)
VMEM = pl.BlockSpec(memory_space=pltpu.VMEM)
PARAMS = pltpu.CompilerParams(vmem_limit_bytes=VMEM_LIMIT)


def in_vmem(array):
    return pltpu.with_memory_space_constraint(array, pltpu.VMEM)


def body(n_row, n_col, blocks, slot_cols, counts, demand, value_added):
    rows, slots, size, _ = blocks.shape
    width = demand.shape[1]
    groups = demand.shape[0] // size
    group_devices = n_row // n_col
    paired = n_col == 2 and n_row == 16 and rows % 2 == 0
    group = lax.axis_index("col")
    me = lax.axis_index("row")

    sums, held = pl.pallas_call(
        sums_kernel,
        name="column_sums",
        out_shape=(
            jax.ShapeDtypeStruct((groups, size), jnp.float32),
            pltpu.VMEM(blocks.shape, blocks.dtype),
        ),
        in_specs=[SMEM, SMEM, pl.BlockSpec(memory_space=pl.ANY)],
        out_specs=(VMEM, VMEM),
        scratch_shapes=[pltpu.VMEM((groups + 1, 8, size), jnp.float32), pltpu.SemaphoreType.DMA((rows,))],
        compiler_params=PARAMS,
    )(slot_cols, counts, blocks)

    if paired:
        for masks in ((1, 2, 3), (4, 8, 12)):
            parts = [sums] + [lax.ppermute(sums, "row", [(i, i ^ m) for i in range(n_row)]) for m in masks]
            if masks[0] == 1:
                sums = functools.reduce(jnp.add, parts)
        sums = jnp.stack(parts)
    else:
        sums = lax.psum(sums, "row")[None]

    partial, coefs = pl.pallas_call(
        first_kernel,
        name="first_layer",
        out_shape=(
            jax.ShapeDtypeStruct((rows, size, width), jnp.bfloat16 if paired else jnp.float32),
            pltpu.VMEM(blocks.shape, blocks.dtype),
        ),
        in_specs=[SMEM, SMEM, VMEM, VMEM, VMEM, VMEM],
        out_specs=(VMEM, VMEM),
        scratch_shapes=[pltpu.VMEM((groups, 1, size), jnp.float32)],
        input_output_aliases={5: 1},
        compiler_params=PARAMS,
    )(slot_cols, counts, sums, value_added.reshape(groups, size), demand.reshape(groups, size, width), in_vmem(held))

    def exchange(part):
        if paired:
            other = lax.ppermute(part, "col", [(0, 1), (1, 0)])
            return part.astype(jnp.float32) + other.astype(jnp.float32)
        return lax.psum(part, "col")

    layer_one = exchange(partial).astype(jnp.bfloat16)
    if paired:
        half = rows // 2
        across = [(c * group_devices + i, (1 - c) * group_devices + i) for c in range(2) for i in range(group_devices)]
        pairs = []
        for c in range(2):
            for i in range(group_devices):
                pairs.append(((c * group_devices + i) * 2 + c, ((1 - c) * group_devices + i) * 2 + c))
        arrived = lax.ppermute(layer_one[half:], ("row", "col"), pairs)
        mine = jnp.where(me // group_devices == group, layer_one[:half], arrived)
        source = lax.all_gather(mine, "row", axis=0, tiled=True)

        def place(col, group):
            owner, inside = lax.div(col, rows), lax.rem(col, rows)
            near = inside < half
            holder = jnp.where(near, group, 1 - group) * group_devices + owner
            return holder * half + jnp.where(near, inside, inside - half)

        index = place(slot_cols, group)
    else:
        gathered = lax.all_gather(layer_one, "row", axis=0, tiled=True)
        source = lax.dynamic_slice_in_dim(gathered, group * groups, groups, 0)
        index = slot_cols

    partial = pl.pallas_call(
        functools.partial(second_kernel, lambda col: col),
        name="second_layer",
        out_shape=jax.ShapeDtypeStruct((rows, size, width), jnp.bfloat16 if paired else jnp.float32),
        in_specs=[SMEM, SMEM, VMEM, VMEM],
        out_specs=VMEM,
        compiler_params=PARAMS,
    )(index, counts, source, in_vmem(coefs))
    result = layer_one.astype(jnp.float32) + exchange(partial)
    return result.astype(jnp.bfloat16).reshape(rows * size, width)


def solution(mesh):
    return jax.shard_map(
        functools.partial(body, mesh.shape["row"], mesh.shape["col"]),
        mesh=mesh,
        in_specs=(
            P("row", "col", None, None),
            P("row", "col"),
            P("row", "col"),
            P("col", None),
            P("col"),
        ),
        out_specs=P("row", None),
        check_vma=False,
    )
```

```python
import functools

import jax
import jax.numpy as jnp
from jax import lax
from jax.experimental import pallas as pl
from jax.experimental.pallas import tpu as pltpu
from jax.sharding import PartitionSpec as P

VMEM_LIMIT = 12 * 1024 * 1024


def divisor(slot_count, most):
    return max(size for size in range(1, most + 1) if slot_count % size == 0)


def chunk_total(counts_ref, b, chunk):
    return lax.div(counts_ref[b, 0] + (chunk - 1), chunk)


def sums_kernel(cols_ref, counts_ref, blocks_ref, sums_ref, held_ref, acc_ref, sems):
    rows, slots, size, _ = blocks_ref.shape
    groups = sums_ref.shape[0]
    chunk = divisor(slots, 4)

    def fetch(b, k):
        part = pl.ds(k * chunk, chunk)
        return pltpu.make_async_copy(blocks_ref.at[b, part], held_ref.at[b, part], sems.at[b])

    for b in range(rows):

        def start(k, carry, b=b):
            fetch(b, k).start()
            return carry

        lax.fori_loop(0, chunk_total(counts_ref, b, chunk), start, 0)
    acc_ref[...] = jnp.zeros_like(acc_ref)
    for b in range(rows):
        total = chunk_total(counts_ref, b, chunk)

        def finish(k, carry, b=b):
            fetch(b, k).wait()
            return carry

        lax.fori_loop(0, total, finish, 0)

        def add(k, carry, b=b):
            for u in range(chunk):
                slot = k * chunk + u
                col = jnp.where(slot < counts_ref[b, 0], cols_ref[b, slot], groups)
                block = held_ref[b, slot].astype(jnp.float32)
                acc_ref[col] += jnp.sum(block.reshape(size // 8, 8, size), axis=0)
            return carry

        lax.fori_loop(0, total, add, 0)
    sums_ref[...] = jnp.sum(acc_ref[:groups], axis=1)


def first_kernel(base_ref, cols_ref, counts_ref, sums_ref, added_ref, demand_ref, blocks_ref, out_ref, coef_ref, inverse_ref):
    slots = blocks_ref.shape[1]
    size = blocks_ref.shape[2]
    chunk = divisor(slots, 12)
    inverse_ref[...] = (1.0 / (jnp.sum(sums_ref[...], axis=0) + added_ref[...]))[:, None, :]
    for b in range(out_ref.shape[0]):
        row = base_ref[0] + b

        def add(k, acc, row=row):
            left, right = [], []
            for u in range(chunk):
                slot = k * chunk + u
                col = cols_ref[row, slot]
                live = slot < counts_ref[row, 0]
                block = blocks_ref[row, jnp.where(live, slot, 0)].astype(jnp.float32)
                coef = jnp.where(live, block * inverse_ref[col], 0.0).astype(jnp.bfloat16)
                coef_ref[row, slot] = coef
                left.append(coef)
                right.append(demand_ref[col])
            return acc + jnp.dot(
                jnp.concatenate(left, axis=1), jnp.concatenate(right, axis=0), preferred_element_type=jnp.float32
            )

        out_ref[b] = lax.fori_loop(
            0, chunk_total(counts_ref, row, chunk), add, jnp.zeros((size, out_ref.shape[2]), jnp.float32)
        ).astype(out_ref.dtype)


def second_layer(first_row, index_ref, counts_ref, coef_ref, source_ref, own_ref, flag, out_ref):
    slots = coef_ref.shape[1]
    size = coef_ref.shape[2]
    chunk = divisor(slots, 12)
    for b in range(out_ref.shape[0]):
        row = first_row + b

        def add(k, acc, row=row):
            left, right = [], []
            for u in range(chunk):
                slot = k * chunk + u
                left.append(coef_ref[row, slot])
                right.append(source_ref[index_ref[row, slot]])
            return acc + jnp.dot(
                jnp.concatenate(left, axis=1), jnp.concatenate(right, axis=0), preferred_element_type=jnp.float32
            )

        start = jnp.where(flag, own_ref[b].astype(jnp.float32), 0.0)
        out_ref[b] = lax.fori_loop(0, chunk_total(counts_ref, row, chunk), add, start).astype(out_ref.dtype)


def second_kernel_a(group_ref, index_ref, counts_ref, coef_ref, own_ref, *rest):
    pieces, (out_ref, source_ref) = rest[:-2], rest[-2:]
    part = pieces[0].shape[0]
    for i, piece in enumerate(pieces):
        source_ref[i * part : (i + 1) * part] = piece[...]
    second_layer(0, index_ref, counts_ref, coef_ref, source_ref, own_ref, group_ref[0] == 0, out_ref)


def second_kernel_b(group_ref, index_ref, counts_ref, coef_ref, own_ref, source_ref, out_ref):
    second_layer(
        out_ref.shape[0], index_ref, counts_ref, coef_ref, source_ref, own_ref, group_ref[0] == 1, out_ref
    )


def second_kernel(group_ref, index_ref, counts_ref, coef_ref, own_ref, source_ref, out_ref):
    second_layer(0, index_ref, counts_ref, coef_ref, source_ref, own_ref, group_ref[0] == 0, out_ref)


SMEM = pl.BlockSpec(memory_space=pltpu.SMEM)
VMEM = pl.BlockSpec(memory_space=pltpu.VMEM)
PARAMS = pltpu.CompilerParams(vmem_limit_bytes=VMEM_LIMIT)


def in_vmem(array):
    return pltpu.with_memory_space_constraint(array, pltpu.VMEM)


def body(n_row, n_col, blocks, slot_cols, counts, demand, value_added):
    rows, slots, size, _ = blocks.shape
    width = demand.shape[1]
    groups = demand.shape[0] // size
    group_devices = n_row // n_col
    paired = n_col == 2 and n_row == 16 and rows % 2 == 0
    half = rows // 2
    group = lax.axis_index("col")
    me = lax.axis_index("row")
    group_word = group.astype(jnp.int32).reshape(1)

    sums, held = pl.pallas_call(
        sums_kernel,
        name="column_sums",
        out_shape=(
            jax.ShapeDtypeStruct((groups, size), jnp.float32),
            pltpu.VMEM(blocks.shape, blocks.dtype),
        ),
        in_specs=[SMEM, SMEM, pl.BlockSpec(memory_space=pltpu.HBM)],
        out_specs=(VMEM, VMEM),
        scratch_shapes=[pltpu.VMEM((groups + 1, 8, size), jnp.float32), pltpu.SemaphoreType.DMA((rows,))],
        compiler_params=PARAMS,
    )(slot_cols, counts, pltpu.with_memory_space_constraint(blocks, pltpu.HBM))

    def flip(array, mask):
        return lax.ppermute(array, "row", [(i, i ^ mask) for i in range(n_row)])

    def swap(array):
        return lax.ppermute(array, "col", [(0, 1), (1, 0)])

    if paired:
        sums = functools.reduce(jnp.add, [sums] + [flip(sums, m) for m in (1, 2, 3)])
        sums = jnp.stack([sums] + [flip(sums, m) for m in (4, 8, 12)])
    else:
        sums = lax.psum(sums, "row")[None]

    def first_layer(base, count, dtype, held):
        return pl.pallas_call(
            first_kernel,
            name="first_layer",
            out_shape=(
                jax.ShapeDtypeStruct((count, size, width), dtype),
                pltpu.VMEM(blocks.shape, blocks.dtype),
            ),
            in_specs=[SMEM, SMEM, SMEM, VMEM, VMEM, VMEM, VMEM],
            out_specs=(VMEM, VMEM),
            scratch_shapes=[pltpu.VMEM((groups, 1, size), jnp.float32)],
            input_output_aliases={6: 1},
            compiler_params=PARAMS,
        )(
            base,
            slot_cols,
            counts,
            sums,
            value_added.reshape(groups, size),
            demand.reshape(groups, size, width),
            in_vmem(held),
        )

    def second_call(kernel, name, count, index, coefs, own, sources, keep_sources):
        dtype = jnp.bfloat16 if paired else jnp.float32
        out = jax.ShapeDtypeStruct((count, size, width), dtype)
        return pl.pallas_call(
            kernel,
            name=name,
            out_shape=(out, jax.ShapeDtypeStruct((groups, size, width), jnp.bfloat16)) if keep_sources else out,
            in_specs=[SMEM, SMEM, SMEM] + [VMEM] * (2 + len(sources)),
            out_specs=(VMEM, VMEM) if keep_sources else VMEM,
            compiler_params=PARAMS,
        )(group_word, index, counts, in_vmem(coefs), own, *sources)

    if not paired:
        partial, coefs = first_layer(jnp.zeros((1,), jnp.int32), rows, jnp.float32, held)
        layer_one = lax.psum(partial, "col").astype(jnp.bfloat16)
        gathered = lax.all_gather(layer_one, "row", axis=0, tiled=True)
        source = lax.dynamic_slice_in_dim(gathered, group * groups, groups, 0)
        partial = second_call(second_kernel, "second_layer", rows, slot_cols, coefs, layer_one, [source], False)
        return lax.psum(partial, "col").astype(jnp.bfloat16).reshape(rows * size, width)

    sent, coefs = first_layer((1 - group_word) * half, half, jnp.bfloat16, held)
    arrived = swap(sent)
    kept, coefs = first_layer(group_word * half, half, jnp.float32, coefs)
    own = (kept + arrived.astype(jnp.float32)).astype(jnp.bfloat16)

    crossed = flip(own, group_devices)
    at_home = me // group_devices == group
    home = jnp.where(at_home, own, crossed)
    away = swap(jnp.where(at_home, crossed, own))
    home_y, home_z = flip(home, 2), flip(home, 4)
    away_y, away_z = flip(away, 2), flip(away, 4)
    home_yz, away_yz = flip(home_z, 2), flip(away_y, 4)
    near = [home, home_y, home_z, home_yz, away, away_y, away_z, away_yz]
    pieces = []
    for piece in near:
        pieces += [piece, flip(piece, 1)]

    owner, inside = slot_cols // rows, slot_cols % rows
    position = owner ^ (me % group_devices)
    away_piece = ((inside // half) != group).astype(jnp.int32)
    index = ((away_piece * group_devices + position // 2 * 2 + position % 2) * half) + inside % half

    part_a, source = second_call(second_kernel_a, "second_layer", half, index, coefs, own, pieces, True)
    other_a = swap(part_a)
    part_b = second_call(second_kernel_b, "second_layer", half, index, coefs, own, [source], False)
    other_b = swap(part_b)
    parts = [
        (mine.astype(jnp.float32) + other.astype(jnp.float32)).astype(jnp.bfloat16)
        for mine, other in ((part_a, other_a), (part_b, other_b))
    ]
    return jnp.concatenate(parts, axis=0).reshape(rows * size, width)


def solution(mesh):
    return jax.shard_map(
        functools.partial(body, mesh.shape["row"], mesh.shape["col"]),
        mesh=mesh,
        in_specs=(
            P("row", "col", None, None),
            P("row", "col"),
            P("row", "col"),
            P("col", None),
            P("col"),
        ),
        out_specs=P("row", None),
        check_vma=False,
    )
```

```python
import functools

import jax
import jax.numpy as jnp
from jax import lax
from jax.experimental import pallas as pl
from jax.experimental.pallas import tpu as pltpu
from jax.sharding import PartitionSpec as P

VMEM_LIMIT = 12 * 1024 * 1024


def divisor(slot_count, most):
    return max(size for size in range(1, most + 1) if slot_count % size == 0)


def chunk_total(counts_ref, b, chunk):
    return lax.div(counts_ref[b] + (chunk - 1), chunk)


def sums_kernel(cols_ref, counts_ref, blocks_ref, sums_ref, held_ref, acc_ref, sems):
    rows, slots, size, _ = blocks_ref.shape
    groups = sums_ref.shape[0]
    chunk = divisor(slots, 4)

    def fetch(b, k):
        part = pl.ds(k * chunk, chunk)
        return pltpu.make_async_copy(blocks_ref.at[b, part], held_ref.at[b, part], sems.at[b])

    for b in range(rows):

        def start(k, carry, b=b):
            fetch(b, k).start()
            return carry

        lax.fori_loop(0, chunk_total(counts_ref, b, chunk), start, 0)
    acc_ref[...] = jnp.zeros_like(acc_ref)
    for b in range(rows):
        total = chunk_total(counts_ref, b, chunk)

        def finish(k, carry, b=b):
            fetch(b, k).wait()
            return carry

        lax.fori_loop(0, total, finish, 0)

        def add(k, carry, b=b):
            for u in range(chunk):
                slot = k * chunk + u
                col = jnp.where(slot < counts_ref[b], cols_ref[b, slot], groups)
                block = held_ref[b, slot].astype(jnp.float32)
                acc_ref[col] += jnp.sum(block.reshape(size // 8, 8, size), axis=0)
            return carry

        lax.fori_loop(0, total, add, 0)
    sums_ref[...] = jnp.sum(acc_ref[:groups], axis=1)


def multiply_rows(rows, counts_ref, chunk, slots, start, gather, acc_ref):
    def product(row, first):
        left, right = zip(*[gather(row, first + u) for u in range(chunk)])
        return jnp.dot(jnp.concatenate(left, axis=1), jnp.concatenate(right, axis=0), preferred_element_type=jnp.float32)

    for b, row in enumerate(rows):
        acc_ref[b] = start(b) + product(row, 0)
    for b, row in enumerate(rows):

        def add(k, carry, b=b, row=row):
            acc_ref[b] += product(row, k * chunk)
            return carry

        lax.fori_loop(1, chunk_total(counts_ref, row, chunk), add, 0)


def first_kernel(sending, cols_ref, counts_ref, sums_ref, added_ref, demand_ref, blocks_ref, out_ref, coef_ref, inverse_ref, acc_ref):
    slots = blocks_ref.shape[1]
    count = out_ref.shape[0]
    inverse_ref[...] = (1.0 / (jnp.sum(sums_ref[...].astype(jnp.float32), axis=0) + added_ref[...]))[:, None, :]
    base = 0
    if sending is not None:
        side = lax.axis_index("col")
        base = (1 - side if sending else side) * count

    def gather(row, slot):
        col = cols_ref[row, slot]
        live = slot < counts_ref[row]
        block = blocks_ref[row, jnp.where(live, slot, 0)].astype(jnp.float32)
        coef = jnp.where(live, block * inverse_ref[col], 0.0).astype(jnp.bfloat16)
        coef_ref[row, slot] = coef
        return coef, demand_ref[col]

    rows = [base + b for b in range(count)]
    multiply_rows(rows, counts_ref, divisor(slots, 12), slots, lambda b: 0.0, gather, acc_ref)
    out_ref[...] = acc_ref[...].astype(out_ref.dtype)


def second_rows(first_row, place, cols_ref, counts_ref, coef_ref, source_ref, start, out_ref, acc_ref):
    slots = coef_ref.shape[1]

    def gather(row, slot):
        return coef_ref[row, slot], source_ref[place(cols_ref[row, slot])]

    rows = [first_row + b for b in range(out_ref.shape[0])]
    multiply_rows(rows, counts_ref, divisor(slots, 12), slots, start, gather, acc_ref)
    out_ref[...] = acc_ref[...].astype(out_ref.dtype)


def exact_scale(count, part):
    scale = -(-(1 << 16) // part)
    assert all((i * scale) >> 16 == i // part for i in range(count))
    return scale


def second_part_kernel(which, cols_ref, counts_ref, coef_ref, own_ref, *rest):
    if which == 0:
        pieces, (out_ref, source_ref, acc_ref) = rest[:-3], rest[-3:]
        part = pieces[0].shape[0]
        for i, piece in enumerate(pieces):
            source_ref[i * part : (i + 1) * part] = piece[...]
    else:
        source_ref, out_ref, acc_ref = rest
    part = out_ref.shape[0]
    side = lax.axis_index("col")
    near = lax.rem(lax.axis_index("row"), 8) * 2 + side
    scale = exact_scale(source_ref.shape[0], part)

    def place(col):
        piece = lax.shift_right_logical(col * scale, 16)
        return col + part * ((piece ^ near) - piece)

    def start(b):
        return jnp.where(side == which, own_ref[b].astype(jnp.float32), 0.0)

    second_rows(which * part, place, cols_ref, counts_ref, coef_ref, source_ref, start, out_ref, acc_ref)


def second_kernel(cols_ref, counts_ref, coef_ref, own_ref, source_ref, out_ref, acc_ref):
    first = lax.axis_index("col") == 0

    def start(b):
        return jnp.where(first, own_ref[b].astype(jnp.float32), 0.0)

    second_rows(0, lambda col: col, cols_ref, counts_ref, coef_ref, source_ref, start, out_ref, acc_ref)


def sort_kernel(own_ref, crossed_ref, home_ref, away_ref):
    at_home = lax.div(lax.axis_index("row"), 8) == lax.axis_index("col")

    @pl.when(at_home)
    def _():
        home_ref[...] = own_ref[...]
        away_ref[...] = crossed_ref[...]

    @pl.when(jnp.logical_not(at_home))
    def _():
        home_ref[...] = crossed_ref[...]
        away_ref[...] = own_ref[...]


SMEM = pl.BlockSpec(memory_space=pltpu.SMEM)
VMEM = pl.BlockSpec(memory_space=pltpu.VMEM)
PARAMS = pltpu.CompilerParams(vmem_limit_bytes=VMEM_LIMIT)


def in_vmem(array):
    return pltpu.with_memory_space_constraint(array, pltpu.VMEM)


def body(n_row, n_col, blocks, slot_cols, counts, demand, value_added):
    rows, slots, size, _ = blocks.shape
    width = demand.shape[1]
    groups = demand.shape[0] // size
    group_devices = n_row // n_col
    paired = n_col == 2 and n_row == 16 and rows % 2 == 0
    half = rows // 2
    counts = counts.reshape(rows)

    sums, held = pl.pallas_call(
        sums_kernel,
        name="column_sums",
        out_shape=(
            jax.ShapeDtypeStruct((groups, size), jnp.float32),
            pltpu.VMEM(blocks.shape, blocks.dtype),
        ),
        in_specs=[SMEM, SMEM, pl.BlockSpec(memory_space=pltpu.HBM)],
        out_specs=(VMEM, VMEM),
        scratch_shapes=[pltpu.VMEM((groups + 1, 8, size), jnp.float32), pltpu.SemaphoreType.DMA((rows,))],
        compiler_params=PARAMS,
    )(slot_cols, counts, pltpu.with_memory_space_constraint(blocks, pltpu.HBM))

    def flip(array, mask):
        return lax.ppermute(array, "row", [(i, i ^ mask) for i in range(n_row)])

    def swap(array):
        return lax.ppermute(array, "col", [(0, 1), (1, 0)])

    if paired:
        for masks in ((1, 2, 3), (4, 8, 12)):
            sums = sums.astype(jnp.bfloat16)
            parts = [sums] + [flip(sums, m) for m in masks]
            sums = functools.reduce(jnp.add, [part.astype(jnp.float32) for part in parts])
    else:
        sums = lax.psum(sums, "row")

    def first_layer(sending, count, dtype, held):
        return pl.pallas_call(
            functools.partial(first_kernel, sending),
            name="first_layer",
            out_shape=(
                jax.ShapeDtypeStruct((count, size, width), dtype),
                pltpu.VMEM(blocks.shape, blocks.dtype),
            ),
            in_specs=[SMEM, SMEM, VMEM, VMEM, VMEM, VMEM],
            out_specs=(VMEM, VMEM),
            scratch_shapes=[
                pltpu.VMEM((groups, 1, size), jnp.float32),
                pltpu.VMEM((count, size, width), jnp.float32),
            ],
            input_output_aliases={5: 1},
            compiler_params=PARAMS,
        )(
            slot_cols,
            counts,
            sums[None],
            value_added.reshape(groups, size),
            demand.reshape(groups, size, width),
            in_vmem(held),
        )

    def second_call(kernel, count, coefs, own, sources, keep_sources):
        dtype = jnp.bfloat16 if paired else jnp.float32
        out = jax.ShapeDtypeStruct((count, size, width), dtype)
        return pl.pallas_call(
            kernel,
            name="second_layer",
            out_shape=(out, jax.ShapeDtypeStruct((groups, size, width), jnp.bfloat16)) if keep_sources else out,
            in_specs=[SMEM, SMEM] + [VMEM] * (2 + len(sources)),
            out_specs=(VMEM, VMEM) if keep_sources else VMEM,
            scratch_shapes=[pltpu.VMEM((count, size, width), jnp.float32)],
            compiler_params=PARAMS,
        )(slot_cols, counts, in_vmem(coefs), own, *sources)

    if not paired:
        group = lax.axis_index("col")
        partial, coefs = first_layer(None, rows, jnp.float32, held)
        layer_one = lax.psum(partial, "col").astype(jnp.bfloat16)
        gathered = lax.all_gather(layer_one, "row", axis=0, tiled=True)
        source = lax.dynamic_slice_in_dim(gathered, group * groups, groups, 0)
        partial = second_call(second_kernel, rows, coefs, layer_one, [source], False)
        return lax.psum(partial, "col").astype(jnp.bfloat16).reshape(rows * size, width)

    sent, coefs = first_layer(True, half, jnp.bfloat16, held)
    arrived = swap(sent)
    kept, coefs = first_layer(False, half, jnp.float32, coefs)
    own = (kept + arrived.astype(jnp.float32)).astype(jnp.bfloat16)

    crossed = flip(own, group_devices)
    piece = jax.ShapeDtypeStruct(own.shape, own.dtype)
    home, away = pl.pallas_call(
        sort_kernel,
        name="home_and_away",
        out_shape=(piece, piece),
        in_specs=[VMEM, VMEM],
        out_specs=(VMEM, VMEM),
        compiler_params=PARAMS,
    )(own, crossed)
    away = swap(away)
    home_y, home_z = flip(home, 2), flip(home, 4)
    away_y, away_z = flip(away, 2), flip(away, 4)
    home_yz, away_yz = flip(home_z, 2), flip(away_y, 4)
    pieces = []
    for pair in ((home, away), (home_y, away_y), (home_z, away_z), (home_yz, away_yz)):
        pieces += [*pair, flip(pair[0], 1), flip(pair[1], 1)]

    part_a, source = second_call(functools.partial(second_part_kernel, 0), half, coefs, own, pieces, True)
    other_a = swap(part_a)
    part_b = second_call(functools.partial(second_part_kernel, 1), half, coefs, own, [source], False)
    other_b = swap(part_b)
    parts = [
        (mine.astype(jnp.float32) + other.astype(jnp.float32)).astype(jnp.bfloat16)
        for mine, other in ((part_a, other_a), (part_b, other_b))
    ]
    return jnp.concatenate(parts, axis=0).reshape(rows * size, width)


def solution(mesh):
    return jax.shard_map(
        functools.partial(body, mesh.shape["row"], mesh.shape["col"]),
        mesh=mesh,
        in_specs=(
            P("row", "col", None, None),
            P("row", "col"),
            P("row", "col"),
            P("col", None),
            P("col"),
        ),
        out_specs=P("row", None),
        check_vma=False,
    )
```

```python
import functools

import jax
import jax.numpy as jnp
from jax import lax
from jax.experimental import pallas as pl
from jax.experimental.pallas import tpu as pltpu
from jax.sharding import PartitionSpec as P

VMEM_LIMIT = 12 * 1024 * 1024


def divisor(slot_count, most):
    return max(size for size in range(1, most + 1) if slot_count % size == 0)


def chunk_total(counts_ref, b, chunk):
    return lax.div(counts_ref[b] + (chunk - 1), chunk)


def sums_kernel(cols_hbm, counts_hbm, blocks_ref, sums_ref, held_ref, acc_ref, cols_ref, counts_ref, list_sems, sems):
    rows, slots, size, _ = blocks_ref.shape
    groups = sums_ref.shape[0]
    chunk = divisor(slots, 4)

    def fetch(b, k):
        part = pl.ds(k * chunk, chunk)
        return pltpu.make_async_copy(blocks_ref.at[b, part], held_ref.at[b, part], sems.at[b])

    counts_copy = pltpu.make_async_copy(counts_hbm, counts_ref, list_sems.at[0])
    cols_copy = pltpu.make_async_copy(cols_hbm, cols_ref, list_sems.at[1])
    counts_copy.start()
    cols_copy.start()
    for b in range(rows):
        fetch(b, 0).start()
    counts_copy.wait()
    for b in range(rows):

        def start(k, carry, b=b):
            fetch(b, k).start()
            return carry

        lax.fori_loop(1, chunk_total(counts_ref, b, chunk), start, 0)
    acc_ref[...] = jnp.zeros_like(acc_ref)
    cols_copy.wait()
    for b in range(rows):
        total = jnp.maximum(chunk_total(counts_ref, b, chunk), 1)

        def finish(k, carry, b=b):
            fetch(b, k).wait()
            return carry

        lax.fori_loop(0, total, finish, 0)

        def add(k, carry, b=b):
            for u in range(chunk):
                slot = k * chunk + u
                col = jnp.where(slot < counts_ref[b], cols_ref[b, slot], groups)
                block = held_ref[b, slot].astype(jnp.float32)
                acc_ref[col] += jnp.sum(block.reshape(size // 8, 8, size), axis=0)
            return carry

        lax.fori_loop(0, total, add, 0)
    sums_ref[...] = jnp.sum(acc_ref[:groups], axis=1)


def multiply_rows(rows, counts_ref, chunk, slots, start, gather, acc_ref):
    def product(row, first):
        left, right = zip(*[gather(row, first + u) for u in range(chunk)])
        return jnp.dot(jnp.concatenate(left, axis=1), jnp.concatenate(right, axis=0), preferred_element_type=jnp.float32)

    for b, row in enumerate(rows):
        acc_ref[b] = start(b) + product(row, 0)
    for b, row in enumerate(rows):

        def add(k, carry, b=b, row=row):
            acc_ref[b] += product(row, k * chunk)
            return carry

        lax.fori_loop(1, chunk_total(counts_ref, row, chunk), add, 0)


def first_kernel(sending, cols_ref, counts_ref, sums_ref, added_ref, demand_ref, blocks_ref, out_ref, coef_ref, inverse_ref, acc_ref):
    slots = blocks_ref.shape[1]
    count = out_ref.shape[0]
    inverse_ref[...] = (1.0 / (jnp.sum(sums_ref[...].astype(jnp.float32), axis=0) + added_ref[...]))[:, None, :]
    base = 0
    if sending is not None:
        side = lax.axis_index("col")
        base = (1 - side if sending else side) * count

    def gather(row, slot):
        col = cols_ref[row, slot]
        live = slot < counts_ref[row]
        block = blocks_ref[row, jnp.where(live, slot, 0)].astype(jnp.float32)
        coef = jnp.where(live, block * inverse_ref[col], 0.0).astype(jnp.bfloat16)
        coef_ref[row, slot] = coef
        return coef, demand_ref[col]

    rows = [base + b for b in range(count)]
    multiply_rows(rows, counts_ref, divisor(slots, 12), slots, lambda b: 0.0, gather, acc_ref)
    out_ref[...] = acc_ref[...].astype(out_ref.dtype)


def second_rows(first_row, place, cols_ref, counts_ref, coef_ref, source_ref, start, out_ref, acc_ref):
    slots = coef_ref.shape[1]

    def gather(row, slot):
        return coef_ref[row, slot], source_ref[place(cols_ref[row, slot])]

    rows = [first_row + b for b in range(out_ref.shape[0])]
    multiply_rows(rows, counts_ref, divisor(slots, 12), slots, start, gather, acc_ref)
    out_ref[...] = acc_ref[...].astype(out_ref.dtype)


def exact_scale(count, part):
    scale = -(-(1 << 16) // part)
    assert all((i * scale) >> 16 == i // part for i in range(count))
    return scale


def second_part_kernel(which, cols_ref, counts_ref, coef_ref, own_ref, *rest):
    if which == 0:
        pieces, (out_ref, source_ref, acc_ref) = rest[:-3], rest[-3:]
        part = out_ref.shape[0]
        for i, piece in enumerate(pieces):
            for place_yz in range(4):
                at = (place_yz * 4 + i) * part
                source_ref[at : at + part] = piece[place_yz * part : (place_yz + 1) * part]
    else:
        source_ref, out_ref, acc_ref = rest
    part = out_ref.shape[0]
    side = lax.axis_index("col")
    near = lax.rem(lax.axis_index("row"), 8) * 2 + side
    scale = exact_scale(source_ref.shape[0], part)

    def place(col):
        piece = lax.shift_right_logical(col * scale, 16)
        return col + part * ((piece ^ near) - piece)

    def start(b):
        return jnp.where(side == which, own_ref[b].astype(jnp.float32), 0.0)

    second_rows(which * part, place, cols_ref, counts_ref, coef_ref, source_ref, start, out_ref, acc_ref)


def second_kernel(cols_ref, counts_ref, coef_ref, own_ref, source_ref, out_ref, acc_ref):
    first = lax.axis_index("col") == 0

    def start(b):
        return jnp.where(first, own_ref[b].astype(jnp.float32), 0.0)

    second_rows(0, lambda col: col, cols_ref, counts_ref, coef_ref, source_ref, start, out_ref, acc_ref)


def sort_kernel(own_ref, crossed_ref, home_ref, away_ref):
    at_home = lax.div(lax.axis_index("row"), 8) == lax.axis_index("col")

    @pl.when(at_home)
    def _():
        home_ref[...] = own_ref[...]
        away_ref[...] = crossed_ref[...]

    @pl.when(jnp.logical_not(at_home))
    def _():
        home_ref[...] = crossed_ref[...]
        away_ref[...] = own_ref[...]


SMEM = pl.BlockSpec(memory_space=pltpu.SMEM)
VMEM = pl.BlockSpec(memory_space=pltpu.VMEM)
PARAMS = pltpu.CompilerParams(vmem_limit_bytes=VMEM_LIMIT)


def cost(flops, bytes_accessed):
    return pl.CostEstimate(flops=flops, bytes_accessed=bytes_accessed, transcendentals=0)


def in_vmem(array):
    return pltpu.with_memory_space_constraint(array, pltpu.VMEM)


def body(n_row, n_col, blocks, slot_cols, counts, demand, value_added):
    rows, slots, size, _ = blocks.shape
    width = demand.shape[1]
    groups = demand.shape[0] // size
    group_devices = n_row // n_col
    paired = n_col == 2 and n_row == 16 and rows % 2 == 0
    half = rows // 2
    counts = counts.reshape(rows)

    sums, held = pl.pallas_call(
        sums_kernel,
        name="column_sums",
        out_shape=(
            jax.ShapeDtypeStruct((groups, size), jnp.float32),
            pltpu.VMEM(blocks.shape, blocks.dtype),
        ),
        in_specs=[pl.BlockSpec(memory_space=pltpu.HBM)] * 3,
        out_specs=(VMEM, VMEM),
        scratch_shapes=[
            pltpu.VMEM((groups + 1, 8, size), jnp.float32),
            pltpu.SMEM(slot_cols.shape, jnp.int32),
            pltpu.SMEM(counts.shape, jnp.int32),
            pltpu.SemaphoreType.DMA((2,)),
            pltpu.SemaphoreType.DMA((rows,)),
        ],
        compiler_params=PARAMS,
        cost_estimate=cost(0, 4 * rows * size * size * slots),
    )(*[pltpu.with_memory_space_constraint(array, pltpu.HBM) for array in (slot_cols, counts, blocks)])

    def flip(array, mask):
        return lax.ppermute(array, "row", [(i, i ^ mask) for i in range(n_row)])

    def swap(array):
        return lax.ppermute(array, "col", [(0, 1), (1, 0)])

    if paired:
        for masks in ((1, 2, 3), (4, 8, 12)):
            sums = sums.astype(jnp.bfloat16)
            parts = [sums] + [flip(sums, m) for m in masks]
            sums = functools.reduce(jnp.add, [part.astype(jnp.float32) for part in parts])
    else:
        sums = lax.psum(sums, "row")

    def layer_cost(count):
        return cost(2 * count * slots * size * size * width, count * slots * size * size * 2)

    def first_layer(sending, count, dtype, held):
        return pl.pallas_call(
            functools.partial(first_kernel, sending),
            name="first_layer",
            out_shape=(
                jax.ShapeDtypeStruct((count, size, width), dtype),
                pltpu.VMEM(blocks.shape, blocks.dtype),
            ),
            in_specs=[SMEM, SMEM, VMEM, VMEM, VMEM, VMEM],
            out_specs=(VMEM, VMEM),
            scratch_shapes=[
                pltpu.VMEM((groups, 1, size), jnp.float32),
                pltpu.VMEM((count, size, width), jnp.float32),
            ],
            input_output_aliases={5: 1},
            compiler_params=PARAMS,
            cost_estimate=layer_cost(count),
        )(
            slot_cols,
            counts,
            sums[None],
            value_added.reshape(groups, size),
            demand.reshape(groups, size, width),
            in_vmem(held),
        )

    def second_call(kernel, count, coefs, own, sources, keep_sources):
        dtype = jnp.bfloat16 if paired else jnp.float32
        out = jax.ShapeDtypeStruct((count, size, width), dtype)
        return pl.pallas_call(
            kernel,
            name="second_layer",
            out_shape=(out, jax.ShapeDtypeStruct((groups, size, width), jnp.bfloat16)) if keep_sources else out,
            in_specs=[SMEM, SMEM] + [VMEM] * (2 + len(sources)),
            out_specs=(VMEM, VMEM) if keep_sources else VMEM,
            scratch_shapes=[pltpu.VMEM((count, size, width), jnp.float32)],
            compiler_params=PARAMS,
            cost_estimate=layer_cost(count),
        )(slot_cols, counts, in_vmem(coefs), own, *sources)

    if not paired:
        group = lax.axis_index("col")
        partial, coefs = first_layer(None, rows, jnp.float32, held)
        layer_one = lax.psum(partial, "col").astype(jnp.bfloat16)
        gathered = lax.all_gather(layer_one, "row", axis=0, tiled=True)
        source = lax.dynamic_slice_in_dim(gathered, group * groups, groups, 0)
        partial = second_call(second_kernel, rows, coefs, layer_one, [source], False)
        return lax.psum(partial, "col").astype(jnp.bfloat16).reshape(rows * size, width)

    sent, coefs = first_layer(True, half, jnp.bfloat16, held)
    arrived = swap(sent)
    kept, coefs = first_layer(False, half, jnp.float32, coefs)
    own = (kept + arrived.astype(jnp.float32)).astype(jnp.bfloat16)

    crossed = flip(own, group_devices)
    piece = jax.ShapeDtypeStruct(own.shape, own.dtype)
    home, away = pl.pallas_call(
        sort_kernel,
        name="home_and_away",
        out_shape=(piece, piece),
        in_specs=[VMEM, VMEM],
        out_specs=(VMEM, VMEM),
        compiler_params=PARAMS,
    )(own, crossed)
    away = swap(away)
    def spread(piece):
        return jnp.concatenate([piece] + [flip(piece, mask) for mask in (2, 4, 6)], axis=0)

    home, away = spread(home), spread(away)
    pieces = [home, away, flip(home, 1), flip(away, 1)]

    part_a, source = second_call(functools.partial(second_part_kernel, 0), half, coefs, own, pieces, True)
    other_a = swap(part_a)
    part_b = second_call(functools.partial(second_part_kernel, 1), half, coefs, own, [source], False)
    other_b = swap(part_b)
    parts = [
        (mine.astype(jnp.float32) + other.astype(jnp.float32)).astype(jnp.bfloat16)
        for mine, other in ((part_a, other_a), (part_b, other_b))
    ]
    return jnp.concatenate(parts, axis=0).reshape(rows * size, width)


def solution(mesh):
    return jax.shard_map(
        functools.partial(body, mesh.shape["row"], mesh.shape["col"]),
        mesh=mesh,
        in_specs=(
            P("row", "col", None, None),
            P("row", "col"),
            P("row", "col"),
            P("col", None),
            P("col"),
        ),
        out_specs=P("row", None),
        check_vma=False,
    )
```

```python
import functools

import jax
import jax.numpy as jnp
from jax import lax
from jax.experimental import pallas as pl
from jax.experimental.pallas import tpu as pltpu
from jax.sharding import PartitionSpec as P

VMEM_LIMIT = 12 * 1024 * 1024


def divisor(slot_count, most):
    return max(size for size in range(1, most + 1) if slot_count % size == 0)


def chunk_total(counts_ref, b, chunk):
    return lax.div(counts_ref[b] + (chunk - 1), chunk)


def sums_kernel(cols_hbm, counts_hbm, blocks_ref, sums_ref, held_ref, acc_ref, cols_ref, counts_ref, list_sems, sems):
    rows, slots, size, _ = blocks_ref.shape
    groups = sums_ref.shape[0]
    chunk = divisor(slots, 4)

    def fetch(b, k):
        part = pl.ds(k * chunk, chunk)
        return pltpu.make_async_copy(blocks_ref.at[b, part], held_ref.at[b, part], sems.at[b])

    counts_copy = pltpu.make_async_copy(counts_hbm, counts_ref, list_sems.at[0])
    cols_copy = pltpu.make_async_copy(cols_hbm, cols_ref, list_sems.at[1])
    counts_copy.start()
    cols_copy.start()
    for b in range(rows):
        fetch(b, 0).start()
    counts_copy.wait()
    for b in range(rows):

        def start(k, carry, b=b):
            fetch(b, k).start()
            return carry

        lax.fori_loop(1, chunk_total(counts_ref, b, chunk), start, 0)
    acc_ref[...] = jnp.zeros_like(acc_ref)
    cols_copy.wait()
    for b in range(rows):
        total = jnp.maximum(chunk_total(counts_ref, b, chunk), 1)

        def finish(k, carry, b=b):
            fetch(b, k).wait()
            return carry

        lax.fori_loop(0, total, finish, 0)

        def add(k, carry, b=b):
            for u in range(chunk):
                slot = k * chunk + u
                col = jnp.where(slot < counts_ref[b], cols_ref[b, slot], groups)
                block = held_ref[b, slot].astype(jnp.float32)
                acc_ref[col] += jnp.sum(block.reshape(size // 8, 8, size), axis=0)
            return carry

        lax.fori_loop(0, total, add, 0)
    sums_ref[...] = jnp.sum(acc_ref[:groups], axis=1)


def multiply_rows(rows, counts_ref, chunk, start, gather, acc_ref):
    def product(row, first):
        left, right = zip(*[gather(row, first + u) for u in range(chunk)])
        return jnp.dot(jnp.concatenate(left, axis=1), jnp.concatenate(right, axis=0), preferred_element_type=jnp.float32)

    for b, row in enumerate(rows):
        acc_ref[b] = start(b) + product(row, 0)
    for b, row in enumerate(rows):

        def add(k, carry, b=b, row=row):
            acc_ref[b] += product(row, k * chunk)
            return carry

        lax.fori_loop(1, chunk_total(counts_ref, row, chunk), add, 0)


def first_kernel(first_row, cols_ref, counts_ref, sums_ref, added_ref, demand_ref, blocks_ref, out_ref, sent_ref, coef_ref, inverse_ref):
    slots = blocks_ref.shape[1]
    inverse_ref[...] = (1.0 / (sums_ref[...] + added_ref[...]))[:, None, :]

    def gather(row, slot):
        col = cols_ref[row, slot]
        live = slot < counts_ref[row]
        block = blocks_ref[row, jnp.where(live, slot, 0)].astype(jnp.float32)
        coef = jnp.where(live, block * inverse_ref[col], 0.0).astype(jnp.bfloat16)
        coef_ref[row, slot] = coef
        return coef, demand_ref[col]

    rows = [first_row + b for b in range(out_ref.shape[0])]
    multiply_rows(rows, counts_ref, divisor(slots, 12), lambda b: 0.0, gather, out_ref)
    sent_ref[...] = out_ref[...].astype(sent_ref.dtype)


def second_rows(first_row, place, cols_ref, counts_ref, coef_ref, source_ref, start, out_ref, acc_ref):
    slots = coef_ref.shape[1]

    def gather(row, slot):
        return coef_ref[row, slot], source_ref[place(cols_ref[row, slot])]

    rows = [first_row + b for b in range(out_ref.shape[0])]
    multiply_rows(rows, counts_ref, divisor(slots, 12), start, gather, acc_ref)
    out_ref[...] = acc_ref[...].astype(out_ref.dtype)


def exact_scale(count, part):
    scale = -(-(1 << 16) // part)
    assert all((i * scale) >> 16 == i // part for i in range(count))
    return scale


def is_owner():
    return lax.div(lax.axis_index("row"), 8) == lax.axis_index("col")


def second_part_kernel(which, cols_ref, counts_ref, coef_ref, own_ref, *rest):
    part = own_ref.shape[0]
    if which == 0:
        pieces, (out_ref, source_ref, acc_ref) = rest[:-3], rest[-3:]
        for i, piece in enumerate(pieces):
            for place_yz in range(4):
                at = (place_yz * 4 + i) * part
                source_ref[at : at + part] = piece[place_yz * part : (place_yz + 1) * part]
    else:
        source_ref, out_ref, acc_ref = rest
    near = lax.rem(lax.axis_index("row"), 8) * 2
    owner = is_owner()
    scale = exact_scale(source_ref.shape[0], part)

    def place(col):
        piece = lax.shift_right_logical(col * scale, 16)
        return col + part * ((piece ^ near) - piece)

    def start(b):
        return jnp.where(owner, own_ref[b].astype(jnp.float32), 0.0)

    second_rows(which * part, place, cols_ref, counts_ref, coef_ref, source_ref, start, out_ref, acc_ref)


def second_kernel(cols_ref, counts_ref, coef_ref, own_ref, source_ref, out_ref, acc_ref):
    first = lax.axis_index("col") == 0

    def start(b):
        return jnp.where(first, own_ref[b].astype(jnp.float32), 0.0)

    second_rows(0, lambda col: col, cols_ref, counts_ref, coef_ref, source_ref, start, out_ref, acc_ref)


def reduce_kernel(kept_ref, arrived_ref, *rest):
    own_ref = rest[-1]
    own_ref[...] = (kept_ref[...] + arrived_ref[...].astype(jnp.float32)).astype(own_ref.dtype)


def choose_kernel(own_ref, crossed_ref, *rest):
    home_ref = rest[-1]
    owner = is_owner()

    @pl.when(owner)
    def _():
        home_ref[...] = own_ref[...]

    @pl.when(jnp.logical_not(owner))
    def _():
        home_ref[...] = crossed_ref[...]


def result_kernel(first_row, mine_ref, other_ref, *rest):
    out_ref, sum_ref, sem = rest[-3:]
    sum_ref[...] = (mine_ref[...].astype(jnp.float32) + other_ref[...].astype(jnp.float32)).astype(sum_ref.dtype)
    copy = pltpu.make_async_copy(sum_ref, out_ref.at[pl.ds(first_row, sum_ref.shape[0])], sem)
    copy.start()
    copy.wait()


SMEM = pl.BlockSpec(memory_space=pltpu.SMEM)
VMEM = pl.BlockSpec(memory_space=pltpu.VMEM)
PARAMS = pltpu.CompilerParams(vmem_limit_bytes=VMEM_LIMIT)


def cost(flops, bytes_accessed):
    return pl.CostEstimate(flops=flops, bytes_accessed=bytes_accessed, transcendentals=0)


def in_vmem(array):
    return pltpu.with_memory_space_constraint(array, pltpu.VMEM)


def body(n_row, n_col, blocks, slot_cols, counts, demand, value_added):
    rows, slots, size, _ = blocks.shape
    width = demand.shape[1]
    groups = demand.shape[0] // size
    group_devices = n_row // n_col
    paired = n_col == 2 and n_row == 16 and rows % 2 == 0
    half = rows // 2
    counts = counts.reshape(rows)

    sums, held = pl.pallas_call(
        sums_kernel,
        name="column_sums",
        out_shape=(
            jax.ShapeDtypeStruct((groups, size), jnp.float32),
            pltpu.VMEM(blocks.shape, blocks.dtype),
        ),
        in_specs=[pl.BlockSpec(memory_space=pltpu.HBM)] * 3,
        out_specs=(VMEM, VMEM),
        scratch_shapes=[
            pltpu.VMEM((groups + 1, 8, size), jnp.float32),
            pltpu.SMEM(slot_cols.shape, jnp.int32),
            pltpu.SMEM(counts.shape, jnp.int32),
            pltpu.SemaphoreType.DMA((2,)),
            pltpu.SemaphoreType.DMA((rows,)),
        ],
        compiler_params=PARAMS,
        cost_estimate=cost(0, 4 * rows * size * size * slots),
    )(*[pltpu.with_memory_space_constraint(array, pltpu.HBM) for array in (slot_cols, counts, blocks)])

    def flip(array, mask):
        return lax.ppermute(array, "row", [(i, i ^ mask) for i in range(n_row)])

    def swap(array):
        return lax.ppermute(array, "col", [(0, 1), (1, 0)])

    if paired:
        for masks in ((1, 2, 3), (4, 8, 12)):
            sums = sums.astype(jnp.bfloat16)
            parts = [sums] + [flip(sums, m) for m in masks]
            sums = functools.reduce(jnp.add, [part.astype(jnp.float32) for part in parts])
    else:
        sums = lax.psum(sums, "row")

    def layer_cost(count):
        return cost(2 * count * slots * size * size * width, count * slots * size * size * 2)

    def first_layer(first_row, count, held):
        return pl.pallas_call(
            functools.partial(first_kernel, first_row),
            name="first_layer",
            out_shape=(
                jax.ShapeDtypeStruct((count, size, width), jnp.float32),
                jax.ShapeDtypeStruct((count, size, width), jnp.bfloat16),
                pltpu.VMEM(blocks.shape, blocks.dtype),
            ),
            in_specs=[SMEM, SMEM, VMEM, VMEM, VMEM, VMEM],
            out_specs=(VMEM, VMEM, VMEM),
            scratch_shapes=[pltpu.VMEM((groups, 1, size), jnp.float32)],
            input_output_aliases={5: 2},
            compiler_params=PARAMS,
            cost_estimate=layer_cost(count),
        )(
            slot_cols,
            counts,
            sums,
            value_added.reshape(groups, size),
            demand.reshape(groups, size, width),
            in_vmem(held),
        )

    def second_call(kernel, count, coefs, own, sources, keep_sources):
        dtype = jnp.bfloat16 if paired else jnp.float32
        out = jax.ShapeDtypeStruct((count, size, width), dtype)
        return pl.pallas_call(
            kernel,
            name="second_layer",
            out_shape=(out, jax.ShapeDtypeStruct((groups, size, width), jnp.bfloat16)) if keep_sources else out,
            in_specs=[SMEM, SMEM] + [VMEM] * (2 + len(sources)),
            out_specs=(VMEM, VMEM) if keep_sources else VMEM,
            scratch_shapes=[pltpu.VMEM((count, size, width), jnp.float32)],
            compiler_params=PARAMS,
            cost_estimate=layer_cost(count),
        )(slot_cols, counts, in_vmem(coefs), own, *sources)

    if not paired:
        group = lax.axis_index("col")
        partial, _, coefs = first_layer(0, rows, held)
        layer_one = lax.psum(partial, "col").astype(jnp.bfloat16)
        gathered = lax.all_gather(layer_one, "row", axis=0, tiled=True)
        source = lax.dynamic_slice_in_dim(gathered, group * groups, groups, 0)
        partial = second_call(second_kernel, rows, coefs, layer_one, [source], False)
        return lax.psum(partial, "col").astype(jnp.bfloat16).reshape(rows * size, width)

    owners = [(c * group_devices + i, c) for c in range(2) for i in range(group_devices)]

    def send(array, target):
        pairs = [(source[0] * 2 + source[1], sink[0] * 2 + sink[1]) for source, sink in map(target, owners)]
        return lax.ppermute(array, ("row", "col"), pairs)

    def to_owner(array):
        return send(array, lambda owner: ((owner[0], 1 - owner[1]), owner))

    def across(array):
        return send(array, lambda owner: (owner, (owner[0] ^ group_devices, owner[1])))

    piece = jax.ShapeDtypeStruct((half, size, width), jnp.bfloat16)

    def small_call(kernel, name, inputs, earlier):
        return pl.pallas_call(
            kernel,
            name=name,
            out_shape=piece,
            in_specs=[VMEM] * len(inputs) + [pl.BlockSpec(memory_space=pl.ANY)] * len(earlier),
            out_specs=VMEM,
            compiler_params=PARAMS,
        )(*inputs, *earlier)

    kept_a, sent_a, coefs = first_layer(0, half, held)
    kept_b, sent_b, coefs = first_layer(half, half, coefs)
    own_a = small_call(reduce_kernel, "own_rows", [kept_a, to_owner(sent_a)], [sent_b])
    own_b = small_call(reduce_kernel, "own_rows", [kept_b, to_owner(sent_b)], [own_a])
    home_a = small_call(choose_kernel, "own_or_crossed", [own_a, across(own_a)], [])
    a_y, a_z = flip(home_a, 2), flip(home_a, 4)
    home_b = small_call(choose_kernel, "own_or_crossed", [own_b, across(own_b)], [a_y, a_z])
    near_a = jnp.concatenate([home_a, a_y, a_z, flip(a_z, 2)], axis=0)
    near_b = jnp.concatenate([home_b] + [flip(home_b, mask) for mask in (2, 4, 6)], axis=0)
    pieces = [near_a, near_b, flip(near_a, 1), flip(near_b, 1)]

    part_a, source = second_call(functools.partial(second_part_kernel, 0), half, coefs, own_a, pieces, True)
    other_a = swap(part_a)
    part_b = second_call(functools.partial(second_part_kernel, 1), half, coefs, own_b, [source], False)
    other_b = swap(part_b)

    def result(first_row, inputs):
        return pl.pallas_call(
            functools.partial(result_kernel, first_row),
            name="result",
            out_shape=jax.ShapeDtypeStruct((rows, size, width), jnp.bfloat16),
            in_specs=[VMEM, VMEM] + [pl.BlockSpec(memory_space=pltpu.HBM)] * (len(inputs) - 2),
            out_specs=pl.BlockSpec(memory_space=pltpu.HBM),
            scratch_shapes=[pltpu.VMEM(piece.shape, piece.dtype), pltpu.SemaphoreType.DMA],
            input_output_aliases={2: 0} if len(inputs) > 2 else {},
            compiler_params=PARAMS,
        )(*inputs)

    out = result(0, [part_a, other_a])
    return result(half, [part_b, other_b, out]).reshape(rows * size, width)


def solution(mesh):
    return jax.shard_map(
        functools.partial(body, mesh.shape["row"], mesh.shape["col"]),
        mesh=mesh,
        in_specs=(
            P("row", "col", None, None),
            P("row", "col"),
            P("row", "col"),
            P("col", None),
            P("col"),
        ),
        out_specs=P("row", None),
        check_vma=False,
    )
```

```python
import functools

import jax
import jax.numpy as jnp
from jax import lax
from jax.experimental import pallas as pl
from jax.experimental.pallas import tpu as pltpu
from jax.sharding import PartitionSpec as P

VMEM_LIMIT = 12 * 1024 * 1024


def divisor(slot_count, most):
    return max(size for size in range(1, most + 1) if slot_count % size == 0)


def chunk_total(counts_ref, b, chunk):
    return lax.div(counts_ref[b] + (chunk - 1), chunk)


def sums_kernel(cols_hbm, counts_hbm, blocks_ref, sums_ref, held_ref, acc_ref, cols_ref, counts_ref, list_sems, sems):
    rows, slots, size, _ = blocks_ref.shape
    groups = sums_ref.shape[0]
    chunk = divisor(slots, 4)

    def fetch(b, k):
        part = pl.ds(k * chunk, chunk)
        return pltpu.make_async_copy(blocks_ref.at[b, part], held_ref.at[b, part], sems.at[b])

    counts_copy = pltpu.make_async_copy(counts_hbm, counts_ref, list_sems.at[0])
    cols_copy = pltpu.make_async_copy(cols_hbm, cols_ref, list_sems.at[1])
    counts_copy.start()
    cols_copy.start()
    for b in range(rows):
        fetch(b, 0).start()
    counts_copy.wait()
    for b in range(rows):

        def start(k, carry, b=b):
            fetch(b, k).start()
            return carry

        lax.fori_loop(1, chunk_total(counts_ref, b, chunk), start, 0)
    acc_ref[...] = jnp.zeros_like(acc_ref)
    cols_copy.wait()
    for b in range(rows):
        total = jnp.maximum(chunk_total(counts_ref, b, chunk), 1)

        def finish(k, carry, b=b):
            fetch(b, k).wait()
            return carry

        lax.fori_loop(0, total, finish, 0)

        def add(k, carry, b=b):
            for u in range(chunk):
                slot = k * chunk + u
                col = jnp.where(slot < counts_ref[b], cols_ref[b, slot], groups)
                block = held_ref[b, slot].astype(jnp.float32)
                acc_ref[col] += jnp.sum(block.reshape(size // 8, 8, size), axis=0)
            return carry

        lax.fori_loop(0, total, add, 0)
    sums_ref[...] = jnp.sum(acc_ref[:groups], axis=1)


def multiply_rows(rows, counts_ref, chunk, start, gather, acc_ref):
    def product(row, first):
        left, right = zip(*[gather(row, first + u) for u in range(chunk)])
        return jnp.dot(jnp.concatenate(left, axis=1), jnp.concatenate(right, axis=0), preferred_element_type=jnp.float32)

    for b, row in enumerate(rows):
        acc_ref[b] = start(b) + product(row, 0)
    for b, row in enumerate(rows):

        def add(k, carry, b=b, row=row):
            acc_ref[b] += product(row, k * chunk)
            return carry

        lax.fori_loop(1, chunk_total(counts_ref, row, chunk), add, 0)


def first_kernel(sending, cols_ref, counts_ref, sums_ref, added_ref, demand_ref, blocks_ref, out_ref, coef_ref, inverse_ref, acc_ref):
    slots = blocks_ref.shape[1]
    count = out_ref.shape[0]
    base = 0
    if sending is not None:
        side = lax.axis_index("col")
        base = (1 - side if sending else side) * count
    inverse_ref[...] = (1.0 / (sums_ref[...] + added_ref[...]))[:, None, :]

    def gather(row, slot):
        col = cols_ref[row, slot]
        live = slot < counts_ref[row]
        block = blocks_ref[row, jnp.where(live, slot, 0)].astype(jnp.float32)
        coef = jnp.where(live, block * inverse_ref[col], 0.0).astype(jnp.bfloat16)
        coef_ref[row, slot] = coef
        return coef, demand_ref[col]

    rows = [base + b for b in range(count)]
    multiply_rows(rows, counts_ref, divisor(slots, 12), lambda b: 0.0, gather, acc_ref)
    out_ref[...] = acc_ref[...].astype(out_ref.dtype)


def second_rows(first_row, place, cols_ref, counts_ref, coef_ref, source_ref, start, out_ref, acc_ref):
    slots = coef_ref.shape[1]

    def gather(row, slot):
        return coef_ref[row, slot], source_ref[place(cols_ref[row, slot])]

    rows = [first_row + b for b in range(out_ref.shape[0])]
    multiply_rows(rows, counts_ref, divisor(slots, 12), start, gather, acc_ref)
    out_ref[...] = acc_ref[...].astype(out_ref.dtype)


def exact_scale(count, part):
    scale = -(-(1 << 16) // part)
    assert all((i * scale) >> 16 == i // part for i in range(count))
    return scale


NEAR = ((0, 0, 0), (0, 1, 0), (0, 0, 1), (1, 0, 1))
FAR = ((1, 0, 0), (1, 1, 0), (0, 1, 1), (1, 1, 1))


def second_part_kernel(which, cols_ref, counts_ref, coef_ref, own_ref, *rest):
    part = own_ref.shape[0]
    if which == 0:
        near_ref, far_ref, near_core_ref, far_core_ref, out_ref, source_ref, acc_ref = rest
        for core, arrays in enumerate(((near_ref, far_ref), (near_core_ref, far_core_ref))):
            for array, places in zip(arrays, (NEAR, FAR)):
                for i, (z, y, away) in enumerate(places):
                    at = ((z * 4 + y * 2 + core) * 2 + away) * part
                    source_ref[at : at + part] = array[i * part : (i + 1) * part]
    else:
        source_ref, out_ref, acc_ref = rest
    side = lax.axis_index("col")
    near = lax.rem(lax.axis_index("row"), 8) * 2 + side
    scale = exact_scale(source_ref.shape[0], part)

    def place(col):
        piece = lax.shift_right_logical(col * scale, 16)
        return col + part * ((piece ^ near) - piece)

    def start(b):
        return jnp.where(side == which, own_ref[b].astype(jnp.float32), 0.0)

    second_rows(which * part, place, cols_ref, counts_ref, coef_ref, source_ref, start, out_ref, acc_ref)


def second_kernel(cols_ref, counts_ref, coef_ref, own_ref, source_ref, out_ref, acc_ref):
    first = lax.axis_index("col") == 0

    def start(b):
        return jnp.where(first, own_ref[b].astype(jnp.float32), 0.0)

    second_rows(0, lambda col: col, cols_ref, counts_ref, coef_ref, source_ref, start, out_ref, acc_ref)


def choose_kernel(own_ref, first_ref, second_ref, home_ref, away_ref):
    owner = lax.div(lax.axis_index("row"), 8) == lax.axis_index("col")

    @pl.when(owner)
    def _():
        home_ref[...] = own_ref[...]
        away_ref[...] = first_ref[...]

    @pl.when(jnp.logical_not(owner))
    def _():
        home_ref[...] = first_ref[...]
        away_ref[...] = second_ref[...]


def result_kernel(first_row, mine_ref, other_ref, *rest):
    out_ref, sum_ref, sem = rest[-3:]
    sum_ref[...] = (mine_ref[...].astype(jnp.float32) + other_ref[...].astype(jnp.float32)).astype(sum_ref.dtype)
    copy = pltpu.make_async_copy(sum_ref, out_ref.at[pl.ds(first_row, sum_ref.shape[0])], sem)
    copy.start()
    copy.wait()


SMEM = pl.BlockSpec(memory_space=pltpu.SMEM)
VMEM = pl.BlockSpec(memory_space=pltpu.VMEM)
PARAMS = pltpu.CompilerParams(vmem_limit_bytes=VMEM_LIMIT)


def cost(flops, bytes_accessed):
    return pl.CostEstimate(flops=flops, bytes_accessed=bytes_accessed, transcendentals=0)


def in_vmem(array):
    return pltpu.with_memory_space_constraint(array, pltpu.VMEM)


def body(n_row, n_col, blocks, slot_cols, counts, demand, value_added):
    rows, slots, size, _ = blocks.shape
    width = demand.shape[1]
    groups = demand.shape[0] // size
    group_devices = n_row // n_col
    paired = n_col == 2 and n_row == 16 and rows % 2 == 0
    half = rows // 2
    counts = counts.reshape(rows)

    sums, held = pl.pallas_call(
        sums_kernel,
        name="column_sums",
        out_shape=(
            jax.ShapeDtypeStruct((groups, size), jnp.float32),
            pltpu.VMEM(blocks.shape, blocks.dtype),
        ),
        in_specs=[pl.BlockSpec(memory_space=pltpu.HBM)] * 3,
        out_specs=(VMEM, VMEM),
        scratch_shapes=[
            pltpu.VMEM((groups + 1, 8, size), jnp.float32),
            pltpu.SMEM(slot_cols.shape, jnp.int32),
            pltpu.SMEM(counts.shape, jnp.int32),
            pltpu.SemaphoreType.DMA((2,)),
            pltpu.SemaphoreType.DMA((rows,)),
        ],
        compiler_params=PARAMS,
        cost_estimate=cost(0, 4 * rows * size * size * slots),
    )(*[pltpu.with_memory_space_constraint(array, pltpu.HBM) for array in (slot_cols, counts, blocks)])

    def flip(array, mask):
        return lax.ppermute(array, "row", [(i, i ^ mask) for i in range(n_row)])

    def swap(array):
        return lax.ppermute(array, "col", [(0, 1), (1, 0)])

    if paired:
        for masks in ((1, 2, 3), (4, 8, 12)):
            sums = sums.astype(jnp.bfloat16)
            parts = [sums] + [flip(sums, m) for m in masks]
            sums = functools.reduce(jnp.add, [part.astype(jnp.float32) for part in parts])
    else:
        sums = lax.psum(sums, "row")

    def layer_cost(count):
        return cost(2 * count * slots * size * size * width, count * slots * size * size * 2)

    def first_layer(sending, count, dtype, held):
        return pl.pallas_call(
            functools.partial(first_kernel, sending),
            name="first_layer",
            out_shape=(
                jax.ShapeDtypeStruct((count, size, width), dtype),
                pltpu.VMEM(blocks.shape, blocks.dtype),
            ),
            in_specs=[SMEM, SMEM, VMEM, VMEM, VMEM, VMEM],
            out_specs=(VMEM, VMEM),
            scratch_shapes=[
                pltpu.VMEM((groups, 1, size), jnp.float32),
                pltpu.VMEM((count, size, width), jnp.float32),
            ],
            input_output_aliases={5: 1},
            compiler_params=PARAMS,
            cost_estimate=layer_cost(count),
        )(
            slot_cols,
            counts,
            sums,
            value_added.reshape(groups, size),
            demand.reshape(groups, size, width),
            in_vmem(held),
        )

    def second_call(kernel, count, coefs, own, sources, keep_sources):
        dtype = jnp.bfloat16 if paired else jnp.float32
        out = jax.ShapeDtypeStruct((count, size, width), dtype)
        return pl.pallas_call(
            kernel,
            name="second_layer",
            out_shape=(out, jax.ShapeDtypeStruct((groups, size, width), jnp.bfloat16)) if keep_sources else out,
            in_specs=[SMEM, SMEM] + [VMEM] * (2 + len(sources)),
            out_specs=(VMEM, VMEM) if keep_sources else VMEM,
            scratch_shapes=[pltpu.VMEM((count, size, width), jnp.float32)],
            compiler_params=PARAMS,
            cost_estimate=layer_cost(count),
        )(slot_cols, counts, in_vmem(coefs), own, *sources)

    if not paired:
        group = lax.axis_index("col")
        partial, coefs = first_layer(None, rows, jnp.float32, held)
        layer_one = lax.psum(partial, "col").astype(jnp.bfloat16)
        gathered = lax.all_gather(layer_one, "row", axis=0, tiled=True)
        source = lax.dynamic_slice_in_dim(gathered, group * groups, groups, 0)
        partial = second_call(second_kernel, rows, coefs, layer_one, [source], False)
        return lax.psum(partial, "col").astype(jnp.bfloat16).reshape(rows * size, width)

    sent, coefs = first_layer(True, half, jnp.bfloat16, held)
    arrived = swap(sent)
    kept, coefs = first_layer(False, half, jnp.float32, coefs)
    own = (kept + arrived.astype(jnp.float32)).astype(jnp.bfloat16)

    first_pairs, second_pairs = [], []
    for i in range(n_row):
        for c in range(2):
            me, crossed = i * 2 + c, (i ^ group_devices) * 2
            if i // group_devices == c:
                first_pairs.append((me, crossed + c))
                second_pairs.append((me, me))
            else:
                first_pairs.append((me, i * 2 + 1 - c))
                second_pairs.append((me, crossed + 1 - c))
    first, second = [lax.ppermute(own, ("row", "col"), pairs) for pairs in (first_pairs, second_pairs)]
    piece = jax.ShapeDtypeStruct(own.shape, own.dtype)
    home, away = pl.pallas_call(
        choose_kernel,
        name="home_and_away",
        out_shape=(piece, piece),
        in_specs=[VMEM] * 3,
        out_specs=(VMEM, VMEM),
        compiler_params=PARAMS,
    )(own, first, second)
    home = jnp.concatenate([home, flip(home, 2)], axis=0)
    away = jnp.concatenate([away, flip(away, 4)], axis=0)
    near = jnp.concatenate([home, away], axis=0)
    far = jnp.concatenate([flip(home, 4), flip(away, 2)], axis=0)
    pieces = [near, far, flip(near, 1), flip(far, 1)]

    part_a, source = second_call(functools.partial(second_part_kernel, 0), half, coefs, own, pieces, True)
    other_a = swap(part_a)
    part_b = second_call(functools.partial(second_part_kernel, 1), half, coefs, own, [source], False)
    other_b = swap(part_b)

    def result(first_row, inputs):
        return pl.pallas_call(
            functools.partial(result_kernel, first_row),
            name="result",
            out_shape=jax.ShapeDtypeStruct((rows, size, width), jnp.bfloat16),
            in_specs=[VMEM, VMEM] + [pl.BlockSpec(memory_space=pltpu.HBM)] * (len(inputs) - 2),
            out_specs=pl.BlockSpec(memory_space=pltpu.HBM),
            scratch_shapes=[pltpu.VMEM(piece.shape, piece.dtype), pltpu.SemaphoreType.DMA],
            input_output_aliases={2: 0} if len(inputs) > 2 else {},
            compiler_params=PARAMS,
        )(*inputs)

    out = result(0, [part_a, other_a])
    return result(half, [part_b, other_b, out]).reshape(rows * size, width)


def solution(mesh):
    return jax.shard_map(
        functools.partial(body, mesh.shape["row"], mesh.shape["col"]),
        mesh=mesh,
        in_specs=(
            P("row", "col", None, None),
            P("row", "col"),
            P("row", "col"),
            P("col", None),
            P("col"),
        ),
        out_specs=P("row", None),
        check_vma=False,
    )
```

```python
import functools

import jax
import jax.numpy as jnp
from jax import lax
from jax.experimental import pallas as pl
from jax.experimental.pallas import tpu as pltpu
from jax.sharding import PartitionSpec as P

VMEM_LIMIT = 12 * 1024 * 1024


def divisor(slot_count, most):
    return max(size for size in range(1, most + 1) if slot_count % size == 0)


def chunk_total(counts_ref, b, chunk):
    return lax.div(counts_ref[b] + (chunk - 1), chunk)


def sums_kernel(cols_hbm, counts_hbm, blocks_ref, sums_ref, held_ref, acc_ref, cols_ref, counts_ref, list_sems, sems):
    rows, slots, size, _ = blocks_ref.shape
    groups = acc_ref.shape[0] - 1
    chunk = divisor(slots, 4)

    def fetch(b, k):
        part = pl.ds(k * chunk, chunk)
        return pltpu.make_async_copy(blocks_ref.at[b, part], held_ref.at[b, part], sems.at[b])

    counts_copy = pltpu.make_async_copy(counts_hbm, counts_ref, list_sems.at[0])
    cols_copy = pltpu.make_async_copy(cols_hbm, cols_ref, list_sems.at[1])
    counts_copy.start()
    cols_copy.start()
    for b in range(rows):
        fetch(b, 0).start()
    counts_copy.wait()
    for b in range(rows):

        def start(k, carry, b=b):
            fetch(b, k).start()
            return carry

        lax.fori_loop(1, chunk_total(counts_ref, b, chunk), start, 0)
    acc_ref[...] = jnp.zeros_like(acc_ref)
    cols_copy.wait()
    for b in range(rows):
        total = jnp.maximum(chunk_total(counts_ref, b, chunk), 1)

        def finish(k, carry, b=b):
            fetch(b, k).wait()
            return carry

        lax.fori_loop(0, total, finish, 0)

        def add(k, carry, b=b):
            for u in range(chunk):
                slot = k * chunk + u
                col = jnp.where(slot < counts_ref[b], cols_ref[b, slot], groups)
                block = held_ref[b, slot].astype(jnp.float32)
                acc_ref[col] += jnp.sum(block.reshape(size // 8, 8, size), axis=0)
            return carry

        lax.fori_loop(0, total, add, 0)
    sums = jnp.sum(acc_ref[:groups], axis=1)
    if len(sums_ref.shape) == 2:
        sums_ref[...] = sums
    else:
        share = groups // sums_ref.shape[0]
        sums_ref[...] = jnp.zeros_like(sums_ref)
        for i in range(sums_ref.shape[0]):
            sums_ref[i, :share] = sums[i * share : (i + 1) * share]


def multiply_rows(rows, counts_ref, chunk, start, gather, acc_ref):
    def product(row, first):
        left, right = zip(*[gather(row, first + u) for u in range(chunk)])
        return jnp.dot(jnp.concatenate(left, axis=1), jnp.concatenate(right, axis=0), preferred_element_type=jnp.float32)

    for b, row in enumerate(rows):
        acc_ref[b] = start(b) + product(row, 0)
    for b, row in enumerate(rows):

        def add(k, carry, b=b, row=row):
            acc_ref[b] += product(row, k * chunk)
            return carry

        lax.fori_loop(1, chunk_total(counts_ref, row, chunk), add, 0)


def first_kernel(sending, cols_ref, counts_ref, sums_ref, added_ref, demand_ref, blocks_ref, out_ref, coef_ref, inverse_ref, acc_ref):
    slots = blocks_ref.shape[1]
    count = out_ref.shape[0]
    base = 0
    if sending is not None:
        side = lax.axis_index("col")
        base = (1 - side if sending else side) * count
    if len(sums_ref.shape) == 2:
        sums = sums_ref[...]
    else:
        share = added_ref.shape[0] // sums_ref.shape[0]
        sums = jnp.concatenate([sums_ref[i, :share] for i in range(sums_ref.shape[0])], axis=0)
    inverse_ref[...] = (1.0 / (sums + added_ref[...]))[:, None, :]

    def gather(row, slot):
        col = cols_ref[row, slot]
        live = slot < counts_ref[row]
        block = blocks_ref[row, jnp.where(live, slot, 0)].astype(jnp.float32)
        coef = (block * jnp.where(live, inverse_ref[col], 0.0)).astype(jnp.bfloat16)
        coef_ref[row, slot] = coef
        return coef, demand_ref[col]

    rows = [base + b for b in range(count)]
    multiply_rows(rows, counts_ref, divisor(slots, 12), lambda b: 0.0, gather, acc_ref)
    out_ref[...] = acc_ref[...].astype(out_ref.dtype)


def second_rows(first_row, place, cols_ref, counts_ref, coef_ref, source_ref, start, out_ref, acc_ref):
    slots = coef_ref.shape[1]

    def gather(row, slot):
        return coef_ref[row, slot], source_ref[place(cols_ref[row, slot])]

    rows = [first_row + b for b in range(out_ref.shape[0])]
    multiply_rows(rows, counts_ref, divisor(slots, 12), start, gather, acc_ref)
    out_ref[...] = acc_ref[...].astype(out_ref.dtype)


def exact_scale(count, part):
    scale = -(-(1 << 16) // part)
    assert all((i * scale) >> 16 == i // part for i in range(count))
    return scale


PLACES = ((0, 0), (0, 1), (1, 0), (1, 1))


def second_part_kernel(which, cols_ref, counts_ref, coef_ref, own_ref, *rest):
    part = own_ref.shape[0]
    if which == 0:
        pieces, (out_ref, source_ref, acc_ref) = rest[:-3], rest[-3:]
        for array, (core, away) in zip(pieces, ((0, 0), (0, 1), (1, 0), (1, 1))):
            for i, (z, y) in enumerate(PLACES):
                at = ((z * 4 + y * 2 + core) * 2 + away) * part
                source_ref[at : at + part] = array[i * part : (i + 1) * part]
    else:
        source_ref, out_ref, acc_ref = rest
    side = lax.axis_index("col")
    near = lax.rem(lax.axis_index("row"), 8) * 2 + side
    scale = exact_scale(source_ref.shape[0], part)

    def place(col):
        piece = lax.shift_right_logical(col * scale, 16)
        return col + part * ((piece ^ near) - piece)

    def start(b):
        return jnp.where(side == which, own_ref[b].astype(jnp.float32), 0.0)

    second_rows(which * part, place, cols_ref, counts_ref, coef_ref, source_ref, start, out_ref, acc_ref)


def second_kernel(cols_ref, counts_ref, coef_ref, own_ref, source_ref, out_ref, acc_ref):
    first = lax.axis_index("col") == 0

    def start(b):
        return jnp.where(first, own_ref[b].astype(jnp.float32), 0.0)

    second_rows(0, lambda col: col, cols_ref, counts_ref, coef_ref, source_ref, start, out_ref, acc_ref)


def choose_kernel(own_ref, crossed_ref, home_ref, away_ref):
    owner = lax.div(lax.axis_index("row"), 8) == lax.axis_index("col")

    @pl.when(owner)
    def _():
        home_ref[...] = own_ref[...]
        away_ref[...] = crossed_ref[...]

    @pl.when(jnp.logical_not(owner))
    def _():
        home_ref[...] = crossed_ref[...]
        away_ref[...] = own_ref[...]


def join_kernel(*refs):
    out_ref, pieces = refs[-1], refs[:4]
    part = pieces[0].shape[0]
    for i, piece in enumerate(pieces):
        out_ref[i * part : (i + 1) * part] = piece[...]


def result_kernel(first_row, mine_ref, other_ref, *rest):
    out_ref, sum_ref, sem = rest[-3:]
    sum_ref[...] = (mine_ref[...].astype(jnp.float32) + other_ref[...].astype(jnp.float32)).astype(sum_ref.dtype)
    copy = pltpu.make_async_copy(sum_ref, out_ref.at[pl.ds(first_row, sum_ref.shape[0])], sem)
    copy.start()
    copy.wait()


SMEM = pl.BlockSpec(memory_space=pltpu.SMEM)
VMEM = pl.BlockSpec(memory_space=pltpu.VMEM)
PARAMS = pltpu.CompilerParams(vmem_limit_bytes=VMEM_LIMIT)


def cost(flops, bytes_accessed):
    return pl.CostEstimate(flops=flops, bytes_accessed=bytes_accessed, transcendentals=0)


def in_vmem(array):
    return pltpu.with_memory_space_constraint(array, pltpu.VMEM)


def body(n_row, n_col, blocks, slot_cols, counts, demand, value_added):
    rows, slots, size, _ = blocks.shape
    width = demand.shape[1]
    groups = demand.shape[0] // size
    group_devices = n_row // n_col
    paired = n_col == 2 and n_row == 16 and rows % 2 == 0 and groups % n_row == 0 and groups // n_row <= 8
    half = rows // 2
    counts = counts.reshape(rows)

    sums, held = pl.pallas_call(
        sums_kernel,
        name="column_sums",
        out_shape=(
            jax.ShapeDtypeStruct((n_row, 8, size) if paired else (groups, size), jnp.float32),
            pltpu.VMEM(blocks.shape, blocks.dtype),
        ),
        in_specs=[pl.BlockSpec(memory_space=pltpu.HBM)] * 3,
        out_specs=(VMEM, VMEM),
        scratch_shapes=[
            pltpu.VMEM((groups + 1, 8, size), jnp.float32),
            pltpu.SMEM(slot_cols.shape, jnp.int32),
            pltpu.SMEM(counts.shape, jnp.int32),
            pltpu.SemaphoreType.DMA((2,)),
            pltpu.SemaphoreType.DMA((rows,)),
        ],
        compiler_params=PARAMS,
        cost_estimate=cost(0, 4 * rows * size * size * slots),
    )(*[pltpu.with_memory_space_constraint(array, pltpu.HBM) for array in (slot_cols, counts, blocks)])

    def flip(array, mask):
        return lax.ppermute(array, "row", [(i, i ^ mask) for i in range(n_row)])

    def swap(array):
        return lax.ppermute(array, "col", [(0, 1), (1, 0)])

    if paired:
        shares = lax.all_to_all(sums, "row", 0, 0)
        share = jnp.broadcast_to(jnp.sum(shares, axis=0), sums.shape)
        sums = lax.all_to_all(share, "row", 0, 0)
    else:
        sums = lax.psum(sums, "row")

    def layer_cost(count):
        return cost(2 * count * slots * size * size * width, count * slots * size * size * 2)

    def first_layer(sending, count, dtype, held):
        return pl.pallas_call(
            functools.partial(first_kernel, sending),
            name="first_layer",
            out_shape=(
                jax.ShapeDtypeStruct((count, size, width), dtype),
                pltpu.VMEM(blocks.shape, blocks.dtype),
            ),
            in_specs=[SMEM, SMEM, VMEM, VMEM, VMEM, VMEM],
            out_specs=(VMEM, VMEM),
            scratch_shapes=[
                pltpu.VMEM((groups, 1, size), jnp.float32),
                pltpu.VMEM((count, size, width), jnp.float32),
            ],
            input_output_aliases={5: 1},
            compiler_params=PARAMS,
            cost_estimate=layer_cost(count),
        )(
            slot_cols,
            counts,
            sums,
            value_added.reshape(groups, size),
            demand.reshape(groups, size, width),
            in_vmem(held),
        )

    def second_call(kernel, count, coefs, own, sources, keep_sources):
        dtype = jnp.bfloat16 if paired else jnp.float32
        out = jax.ShapeDtypeStruct((count, size, width), dtype)
        return pl.pallas_call(
            kernel,
            name="second_layer",
            out_shape=(out, jax.ShapeDtypeStruct((groups, size, width), jnp.bfloat16)) if keep_sources else out,
            in_specs=[SMEM, SMEM] + [VMEM] * (2 + len(sources)),
            out_specs=(VMEM, VMEM) if keep_sources else VMEM,
            scratch_shapes=[pltpu.VMEM((count, size, width), jnp.float32)],
            compiler_params=PARAMS,
            cost_estimate=layer_cost(count),
        )(slot_cols, counts, in_vmem(coefs), own, *sources)

    if not paired:
        group = lax.axis_index("col")
        partial, coefs = first_layer(None, rows, jnp.float32, held)
        layer_one = lax.psum(partial, "col").astype(jnp.bfloat16)
        gathered = lax.all_gather(layer_one, "row", axis=0, tiled=True)
        source = lax.dynamic_slice_in_dim(gathered, group * groups, groups, 0)
        partial = second_call(second_kernel, rows, coefs, layer_one, [source], False)
        return lax.psum(partial, "col").astype(jnp.bfloat16).reshape(rows * size, width)

    sent, coefs = first_layer(True, half, jnp.bfloat16, held)
    arrived = swap(sent)
    kept, coefs = first_layer(False, half, jnp.float32, coefs)
    own = (kept + arrived.astype(jnp.float32)).astype(jnp.bfloat16)

    piece = jax.ShapeDtypeStruct(own.shape, own.dtype)
    home, away = pl.pallas_call(
        choose_kernel,
        name="home_and_away",
        out_shape=(piece, piece),
        in_specs=[VMEM] * 2,
        out_specs=(VMEM, VMEM),
        compiler_params=PARAMS,
    )(own, flip(own, group_devices))

    def join(pieces, earlier):
        return pl.pallas_call(
            join_kernel,
            name="own_joined",
            out_shape=jax.ShapeDtypeStruct((4 * half, size, width), own.dtype),
            in_specs=[VMEM] * 4 + [pl.BlockSpec(memory_space=pl.ANY)] * len(earlier),
            out_specs=VMEM,
            compiler_params=PARAMS,
        )(*pieces, *earlier)

    away = swap(away)
    home_z, home_y = flip(home, 4), flip(home, 2)
    away_y, away_z, away_yz = flip(away, 2), flip(away, 4), flip(away, 6)
    home = join([home, home_y, home_z, flip(home_z, 2)], [away_y])
    away = join([away, away_y, away_z, away_yz], [])
    pieces = [home, away, flip(home, 1), flip(away, 1)]

    part_a, source = second_call(functools.partial(second_part_kernel, 0), half, coefs, own, pieces, True)
    other_a = swap(part_a)
    part_b = second_call(functools.partial(second_part_kernel, 1), half, coefs, own, [source], False)
    other_b = swap(part_b)

    def result(first_row, inputs):
        return pl.pallas_call(
            functools.partial(result_kernel, first_row),
            name="result",
            out_shape=jax.ShapeDtypeStruct((rows, size, width), jnp.bfloat16),
            in_specs=[VMEM, VMEM] + [pl.BlockSpec(memory_space=pltpu.HBM)] * (len(inputs) - 2),
            out_specs=pl.BlockSpec(memory_space=pltpu.HBM),
            scratch_shapes=[pltpu.VMEM(piece.shape, piece.dtype), pltpu.SemaphoreType.DMA],
            input_output_aliases={2: 0} if len(inputs) > 2 else {},
            compiler_params=PARAMS,
        )(*inputs)

    out = result(0, [part_a, other_a])
    return result(half, [part_b, other_b, out]).reshape(rows * size, width)


def solution(mesh):
    return jax.shard_map(
        functools.partial(body, mesh.shape["row"], mesh.shape["col"]),
        mesh=mesh,
        in_specs=(
            P("row", "col", None, None),
            P("row", "col"),
            P("row", "col"),
            P("col", None),
            P("col"),
        ),
        out_specs=P("row", None),
        check_vma=False,
    )
```

```python
import functools

import jax
import jax.numpy as jnp
from jax import lax
from jax.experimental import pallas as pl
from jax.experimental.pallas import tpu as pltpu
from jax.sharding import PartitionSpec as P

VMEM_LIMIT = 12 * 1024 * 1024


def divisor(slot_count, most):
    return max(size for size in range(1, most + 1) if slot_count % size == 0)


def chunk_total(counts_ref, b, chunk):
    return lax.div(counts_ref[b] + (chunk - 1), chunk)


def sums_kernel(cols_hbm, counts_hbm, blocks_ref, sums_ref, held_ref, acc_ref, cols_ref, counts_ref, list_sems, sems):
    rows, slots, size, _ = blocks_ref.shape
    groups = acc_ref.shape[0] - 1
    chunk = divisor(slots, 4)

    def fetch(b, k):
        part = pl.ds(k * chunk, chunk)
        return pltpu.make_async_copy(blocks_ref.at[b, part], held_ref.at[b, part], sems.at[b])

    counts_copy = pltpu.make_async_copy(counts_hbm, counts_ref, list_sems.at[0])
    cols_copy = pltpu.make_async_copy(cols_hbm, cols_ref, list_sems.at[1])
    counts_copy.start()
    cols_copy.start()
    for b in range(rows):
        fetch(b, 0).start()
    counts_copy.wait()
    for b in range(rows):

        def start(k, carry, b=b):
            fetch(b, k).start()
            return carry

        lax.fori_loop(1, chunk_total(counts_ref, b, chunk), start, 0)
    acc_ref[...] = jnp.zeros_like(acc_ref)
    cols_copy.wait()
    for b in range(rows):
        total = jnp.maximum(chunk_total(counts_ref, b, chunk), 1)

        def finish(k, carry, b=b):
            fetch(b, k).wait()
            return carry

        lax.fori_loop(0, total, finish, 0)

        def add(k, carry, b=b):
            for u in range(chunk):
                slot = k * chunk + u
                col = jnp.where(slot < counts_ref[b], cols_ref[b, slot], groups)
                block = held_ref[b, slot].astype(jnp.float32)
                acc_ref[col] += jnp.sum(block.reshape(size // 8, 8, size), axis=0)
            return carry

        lax.fori_loop(0, total, add, 0)
    sums_ref[...] = jnp.sum(acc_ref[:groups], axis=1)


def multiply_rows(rows, counts_ref, chunk, start, gather, acc_ref):
    def product(row, first):
        left, right = zip(*[gather(row, first + u) for u in range(chunk)])
        return jnp.dot(jnp.concatenate(left, axis=1), jnp.concatenate(right, axis=0), preferred_element_type=jnp.float32)

    for b, row in enumerate(rows):
        acc_ref[b] = start(b) + product(row, 0)
    for b, row in enumerate(rows):

        def add(k, carry, b=b, row=row):
            acc_ref[b] += product(row, k * chunk)
            return carry

        lax.fori_loop(1, chunk_total(counts_ref, row, chunk), add, 0)


def first_kernel(sending, cols_ref, counts_ref, sums_ref, added_ref, demand_ref, blocks_ref, out_ref, coef_ref, inverse_ref, acc_ref):
    slots = blocks_ref.shape[1]
    count = out_ref.shape[0]
    base = 0
    if sending is not None:
        side = lax.axis_index("col")
        base = (1 - side if sending else side) * count
    inverse_ref[...] = (1.0 / (sums_ref[...] + added_ref[...]))[:, None, :]

    def gather(row, slot):
        col = cols_ref[row, slot]
        live = slot < counts_ref[row]
        block = blocks_ref[row, jnp.where(live, slot, 0)].astype(jnp.float32)
        coef = (block * jnp.where(live, inverse_ref[col], 0.0)).astype(jnp.bfloat16)
        coef_ref[row, slot] = coef
        return coef, demand_ref[col]

    rows = [base + b for b in range(count)]
    multiply_rows(rows, counts_ref, divisor(slots, 12), lambda b: 0.0, gather, acc_ref)
    out_ref[...] = acc_ref[...].astype(out_ref.dtype)


def second_rows(first_row, place, cols_ref, counts_ref, coef_ref, source_ref, start, out_ref, acc_ref):
    slots = coef_ref.shape[1]

    def gather(row, slot):
        return coef_ref[row, slot], source_ref[place(cols_ref[row, slot])]

    rows = [first_row + b for b in range(out_ref.shape[0])]
    multiply_rows(rows, counts_ref, divisor(slots, 12), start, gather, acc_ref)
    out_ref[...] = acc_ref[...].astype(out_ref.dtype)


def exact_scale(count, part):
    scale = -(-(1 << 16) // part)
    assert all((i * scale) >> 16 == i // part for i in range(count))
    return scale


FIRST = ((0, 0, 0), (0, 1, 0), (1, 0, 0), (0, 0, 1), (0, 1, 1), (1, 0, 1))
LAST = ((1, 1, 0), (1, 1, 1))


def second_part_kernel(which, cols_ref, counts_ref, coef_ref, own_ref, *rest):
    part = own_ref.shape[0]
    if which == 0:
        pieces, (out_ref, source_ref, acc_ref) = rest[:-3], rest[-3:]
        for number, array in enumerate(pieces):
            core = number // 2
            for i, (z, y, away) in enumerate((FIRST, LAST)[number % 2]):
                at = ((z * 4 + y * 2 + core) * 2 + away) * part
                source_ref[at : at + part] = array[i * part : (i + 1) * part]
    else:
        source_ref, out_ref, acc_ref = rest
    side = lax.axis_index("col")
    near = lax.rem(lax.axis_index("row"), 8) * 2 + side
    scale = exact_scale(source_ref.shape[0], part)

    def place(col):
        piece = lax.shift_right_logical(col * scale, 16)
        return col + part * ((piece ^ near) - piece)

    def start(b):
        return jnp.where(side == which, own_ref[b].astype(jnp.float32), 0.0)

    second_rows(which * part, place, cols_ref, counts_ref, coef_ref, source_ref, start, out_ref, acc_ref)


def second_kernel(cols_ref, counts_ref, coef_ref, own_ref, source_ref, out_ref, acc_ref):
    first = lax.axis_index("col") == 0

    def start(b):
        return jnp.where(first, own_ref[b].astype(jnp.float32), 0.0)

    second_rows(0, lambda col: col, cols_ref, counts_ref, coef_ref, source_ref, start, out_ref, acc_ref)


def choose_kernel(own_ref, crossed_ref, home_ref, away_ref):
    owner = lax.div(lax.axis_index("row"), 8) == lax.axis_index("col")

    @pl.when(owner)
    def _():
        home_ref[...] = own_ref[...]
        away_ref[...] = crossed_ref[...]

    @pl.when(jnp.logical_not(owner))
    def _():
        home_ref[...] = crossed_ref[...]
        away_ref[...] = own_ref[...]


def join_kernel(copies, *refs):
    pieces, joined_ref, copy_refs = refs[: -1 - len(copies)], refs[-1 - len(copies)], refs[len(refs) - len(copies) :]
    part = pieces[0].shape[0]
    for i, piece in enumerate(pieces):
        joined_ref[i * part : (i + 1) * part] = piece[...]
    for i, copy_ref in zip(copies, copy_refs):
        copy_ref[...] = pieces[i][...]


def result_kernel(first_row, mine_ref, other_ref, *rest):
    out_ref, sum_ref, sem = rest[-3:]
    sum_ref[...] = (mine_ref[...].astype(jnp.float32) + other_ref[...].astype(jnp.float32)).astype(sum_ref.dtype)
    copy = pltpu.make_async_copy(sum_ref, out_ref.at[pl.ds(first_row, sum_ref.shape[0])], sem)
    copy.start()
    copy.wait()


SMEM = pl.BlockSpec(memory_space=pltpu.SMEM)
VMEM = pl.BlockSpec(memory_space=pltpu.VMEM)
PARAMS = pltpu.CompilerParams(vmem_limit_bytes=VMEM_LIMIT)


def cost(flops, bytes_accessed):
    return pl.CostEstimate(flops=flops, bytes_accessed=bytes_accessed, transcendentals=0)


def in_vmem(array):
    return pltpu.with_memory_space_constraint(array, pltpu.VMEM)


def body(n_row, n_col, blocks, slot_cols, counts, demand, value_added):
    rows, slots, size, _ = blocks.shape
    width = demand.shape[1]
    groups = demand.shape[0] // size
    group_devices = n_row // n_col
    paired = n_col == 2 and n_row == 16 and rows % 2 == 0
    half = rows // 2
    counts = counts.reshape(rows)

    sums, held = pl.pallas_call(
        sums_kernel,
        name="column_sums",
        out_shape=(
            jax.ShapeDtypeStruct((groups, size), jnp.float32),
            pltpu.VMEM(blocks.shape, blocks.dtype),
        ),
        in_specs=[pl.BlockSpec(memory_space=pltpu.HBM)] * 3,
        out_specs=(VMEM, VMEM),
        scratch_shapes=[
            pltpu.VMEM((groups + 1, 8, size), jnp.float32),
            pltpu.SMEM(slot_cols.shape, jnp.int32),
            pltpu.SMEM(counts.shape, jnp.int32),
            pltpu.SemaphoreType.DMA((2,)),
            pltpu.SemaphoreType.DMA((rows,)),
        ],
        compiler_params=PARAMS,
        cost_estimate=cost(0, 4 * rows * size * size * slots),
    )(*[pltpu.with_memory_space_constraint(array, pltpu.HBM) for array in (slot_cols, counts, blocks)])

    def flip(array, mask):
        return lax.ppermute(array, "row", [(i, i ^ mask) for i in range(n_row)])

    def swap(array):
        return lax.ppermute(array, "col", [(0, 1), (1, 0)])

    if paired:
        for mask in (1, 2, 4, 8):
            sums = sums + flip(sums.astype(jnp.bfloat16), mask).astype(jnp.float32)
    else:
        sums = lax.psum(sums, "row")

    def layer_cost(count):
        return cost(2 * count * slots * size * size * width, count * slots * size * size * 2)

    def first_layer(sending, count, dtype, held):
        return pl.pallas_call(
            functools.partial(first_kernel, sending),
            name="first_layer",
            out_shape=(
                jax.ShapeDtypeStruct((count, size, width), dtype),
                pltpu.VMEM(blocks.shape, blocks.dtype),
            ),
            in_specs=[SMEM, SMEM, VMEM, VMEM, VMEM, VMEM],
            out_specs=(VMEM, VMEM),
            scratch_shapes=[
                pltpu.VMEM((groups, 1, size), jnp.float32),
                pltpu.VMEM((count, size, width), jnp.float32),
            ],
            input_output_aliases={5: 1},
            compiler_params=PARAMS,
            cost_estimate=layer_cost(count),
        )(
            slot_cols,
            counts,
            sums,
            value_added.reshape(groups, size),
            demand.reshape(groups, size, width),
            in_vmem(held),
        )

    def second_call(kernel, count, coefs, own, sources, keep_sources):
        dtype = jnp.bfloat16 if paired else jnp.float32
        out = jax.ShapeDtypeStruct((count, size, width), dtype)
        return pl.pallas_call(
            kernel,
            name="second_layer",
            out_shape=(out, jax.ShapeDtypeStruct((groups, size, width), jnp.bfloat16)) if keep_sources else out,
            in_specs=[SMEM, SMEM] + [VMEM] * (2 + len(sources)),
            out_specs=(VMEM, VMEM) if keep_sources else VMEM,
            scratch_shapes=[pltpu.VMEM((count, size, width), jnp.float32)],
            compiler_params=PARAMS,
            cost_estimate=layer_cost(count),
        )(slot_cols, counts, in_vmem(coefs), own, *sources)

    if not paired:
        group = lax.axis_index("col")
        partial, coefs = first_layer(None, rows, jnp.float32, held)
        layer_one = lax.psum(partial, "col").astype(jnp.bfloat16)
        gathered = lax.all_gather(layer_one, "row", axis=0, tiled=True)
        source = lax.dynamic_slice_in_dim(gathered, group * groups, groups, 0)
        partial = second_call(second_kernel, rows, coefs, layer_one, [source], False)
        return lax.psum(partial, "col").astype(jnp.bfloat16).reshape(rows * size, width)

    sent, coefs = first_layer(True, half, jnp.bfloat16, held)
    arrived = swap(sent)
    kept, coefs = first_layer(False, half, jnp.float32, coefs)
    own = (kept + arrived.astype(jnp.float32)).astype(jnp.bfloat16)

    piece = jax.ShapeDtypeStruct(own.shape, own.dtype)
    home, away = pl.pallas_call(
        choose_kernel,
        name="home_and_away",
        out_shape=(piece, piece),
        in_specs=[VMEM] * 2,
        out_specs=(VMEM, VMEM),
        compiler_params=PARAMS,
    )(own, flip(own, group_devices))

    def join(pieces, copies):
        return pl.pallas_call(
            functools.partial(join_kernel, copies),
            name="own_joined",
            out_shape=[jax.ShapeDtypeStruct((len(pieces) * half, size, width), own.dtype)] + [piece] * len(copies),
            in_specs=[VMEM] * len(pieces),
            out_specs=[VMEM] * (1 + len(copies)),
            compiler_params=PARAMS,
        )(*pieces)

    away = swap(away)
    home_y, home_z = flip(home, 2), flip(home, 4)
    away_y, away_z = flip(away, 2), flip(away, 4)
    first, home_z, away_y = join([home, home_y, home_z, away, away_y, away_z], (2, 4))
    (last,) = join([flip(home_z, 2), flip(away_y, 4)], ())
    pieces = [first, last, flip(first, 1), flip(last, 1)]

    part_a, source = second_call(functools.partial(second_part_kernel, 0), half, coefs, own, pieces, True)
    other_a = swap(part_a)
    part_b = second_call(functools.partial(second_part_kernel, 1), half, coefs, own, [source], False)
    other_b = swap(part_b)

    def result(first_row, inputs):
        return pl.pallas_call(
            functools.partial(result_kernel, first_row),
            name="result",
            out_shape=jax.ShapeDtypeStruct((rows, size, width), jnp.bfloat16),
            in_specs=[VMEM, VMEM] + [pl.BlockSpec(memory_space=pltpu.HBM)] * (len(inputs) - 2),
            out_specs=pl.BlockSpec(memory_space=pltpu.HBM),
            scratch_shapes=[pltpu.VMEM(piece.shape, piece.dtype), pltpu.SemaphoreType.DMA],
            input_output_aliases={2: 0} if len(inputs) > 2 else {},
            compiler_params=PARAMS,
        )(*inputs)

    out = result(0, [part_a, other_a])
    return result(half, [part_b, other_b, out]).reshape(rows * size, width)


def solution(mesh):
    return jax.shard_map(
        functools.partial(body, mesh.shape["row"], mesh.shape["col"]),
        mesh=mesh,
        in_specs=(
            P("row", "col", None, None),
            P("row", "col"),
            P("row", "col"),
            P("col", None),
            P("col"),
        ),
        out_specs=P("row", None),
        check_vma=False,
    )
```

```python
import functools

import jax
import jax.numpy as jnp
from jax import lax
from jax.experimental import pallas as pl
from jax.experimental.pallas import tpu as pltpu
from jax.sharding import PartitionSpec as P

VMEM_LIMIT = 12 * 1024 * 1024


def divisor(slot_count, most):
    return max(size for size in range(1, most + 1) if slot_count % size == 0)


def chunk_total(counts_ref, b, chunk):
    return lax.div(counts_ref[b] + (chunk - 1), chunk)


def sums_kernel(cols_hbm, counts_hbm, blocks_ref, sums_ref, held_ref, acc_ref, cols_ref, counts_ref, list_sems, sems):
    rows, slots, size, _ = blocks_ref.shape
    groups = acc_ref.shape[0] - 1
    chunk = divisor(slots, 4)

    def fetch(b, k):
        part = pl.ds(k * chunk, chunk)
        return pltpu.make_async_copy(blocks_ref.at[b, part], held_ref.at[b, part], sems.at[b])

    counts_copy = pltpu.make_async_copy(counts_hbm, counts_ref, list_sems.at[0])
    cols_copy = pltpu.make_async_copy(cols_hbm, cols_ref, list_sems.at[1])
    counts_copy.start()
    cols_copy.start()
    for b in range(rows):
        fetch(b, 0).start()
    counts_copy.wait()
    for b in range(rows):

        def start(k, carry, b=b):
            fetch(b, k).start()
            return carry

        lax.fori_loop(1, chunk_total(counts_ref, b, chunk), start, 0)
    acc_ref[...] = jnp.zeros_like(acc_ref)
    cols_copy.wait()
    for b in range(rows):
        total = jnp.maximum(chunk_total(counts_ref, b, chunk), 1)

        def finish(k, carry, b=b):
            fetch(b, k).wait()
            return carry

        lax.fori_loop(0, total, finish, 0)

        def add(k, carry, b=b):
            for u in range(chunk):
                slot = k * chunk + u
                col = jnp.where(slot < counts_ref[b], cols_ref[b, slot], groups)
                block = held_ref[b, slot].astype(jnp.float32)
                acc_ref[col] += jnp.sum(block.reshape(size // 8, 8, size), axis=0)
            return carry

        lax.fori_loop(0, total, add, 0)
    sums_ref[...] = jnp.sum(acc_ref[:groups], axis=1)


def multiply_rows(rows, counts_ref, chunk, start, gather, acc_ref):
    def product(row, first):
        left, right = zip(*[gather(row, first + u) for u in range(chunk)])
        return jnp.dot(jnp.concatenate(left, axis=1), jnp.concatenate(right, axis=0), preferred_element_type=jnp.float32)

    for b, row in enumerate(rows):
        acc_ref[b] = start(b) + product(row, 0)
    for b, row in enumerate(rows):

        def add(k, carry, b=b, row=row):
            acc_ref[b] += product(row, k * chunk)
            return carry

        lax.fori_loop(1, chunk_total(counts_ref, row, chunk), add, 0)


def first_kernel(sending, cols_ref, counts_ref, sums_ref, added_ref, demand_ref, blocks_ref, out_ref, coef_ref, inverse_ref, acc_ref):
    slots = blocks_ref.shape[1]
    count = out_ref.shape[0]
    base = 0
    if sending is not None:
        side = lax.axis_index("col")
        base = (1 - side if sending else side) * count
    inverse_ref[...] = (1.0 / (sums_ref[...] + added_ref[...]))[:, None, :]

    def gather(row, slot):
        col = cols_ref[row, slot]
        live = slot < counts_ref[row]
        block = blocks_ref[row, jnp.where(live, slot, 0)].astype(jnp.float32)
        coef = (block * jnp.where(live, inverse_ref[col], 0.0)).astype(jnp.bfloat16)
        coef_ref[row, slot] = coef
        return coef, demand_ref[col]

    rows = [base + b for b in range(count)]
    multiply_rows(rows, counts_ref, divisor(slots, 12), lambda b: 0.0, gather, acc_ref)
    out_ref[...] = acc_ref[...].astype(out_ref.dtype)


def second_rows(first_row, place, cols_ref, counts_ref, coef_ref, source_ref, start, out_ref, acc_ref):
    slots = coef_ref.shape[1]

    def gather(row, slot):
        return coef_ref[row, slot], source_ref[place(cols_ref[row, slot])]

    rows = [first_row + b for b in range(out_ref.shape[0])]
    multiply_rows(rows, counts_ref, divisor(slots, 12), start, gather, acc_ref)
    out_ref[...] = acc_ref[...].astype(out_ref.dtype)


def exact_scale(count, part):
    scale = -(-(1 << 16) // part)
    assert all((i * scale) >> 16 == i // part for i in range(count))
    return scale


PLACES = ((0, 0), (0, 1), (1, 0), (1, 1))


def second_part_kernel(which, cols_ref, counts_ref, coef_ref, own_ref, *rest):
    part = own_ref.shape[0]
    if which == 0:
        pieces, (out_ref, source_ref, acc_ref) = rest[:-3], rest[-3:]
        for array, (core, away) in zip(pieces, ((0, 0), (0, 1), (1, 0), (1, 1))):
            for i, (z, y) in enumerate(PLACES):
                at = ((z * 4 + y * 2 + core) * 2 + away) * part
                source_ref[at : at + part] = array[i * part : (i + 1) * part]
    else:
        source_ref, out_ref, acc_ref = rest
    side = lax.axis_index("col")
    near = lax.rem(lax.axis_index("row"), 8) * 2 + side
    scale = exact_scale(source_ref.shape[0], part)

    def place(col):
        piece = lax.shift_right_logical(col * scale, 16)
        return col + part * ((piece ^ near) - piece)

    def start(b):
        return jnp.where(side == which, own_ref[b].astype(jnp.float32), 0.0)

    second_rows(which * part, place, cols_ref, counts_ref, coef_ref, source_ref, start, out_ref, acc_ref)


def second_kernel(cols_ref, counts_ref, coef_ref, own_ref, source_ref, out_ref, acc_ref):
    first = lax.axis_index("col") == 0

    def start(b):
        return jnp.where(first, own_ref[b].astype(jnp.float32), 0.0)

    second_rows(0, lambda col: col, cols_ref, counts_ref, coef_ref, source_ref, start, out_ref, acc_ref)


def choose_kernel(own_ref, crossed_ref, home_ref, away_ref):
    owner = lax.div(lax.axis_index("row"), 8) == lax.axis_index("col")

    @pl.when(owner)
    def _():
        home_ref[...] = own_ref[...]
        away_ref[...] = crossed_ref[...]

    @pl.when(jnp.logical_not(owner))
    def _():
        home_ref[...] = crossed_ref[...]
        away_ref[...] = own_ref[...]


def join_kernel(*refs):
    pieces, joined_ref = refs[:-1], refs[-1]
    part = pieces[0].shape[0]
    for i, piece in enumerate(pieces):
        joined_ref[i * part : (i + 1) * part] = piece[...]


def result_kernel(first_row, mine_ref, other_ref, *rest):
    out_ref, sum_ref, sem = rest[-3:]
    sum_ref[...] = (mine_ref[...].astype(jnp.float32) + other_ref[...].astype(jnp.float32)).astype(sum_ref.dtype)
    copy = pltpu.make_async_copy(sum_ref, out_ref.at[pl.ds(first_row, sum_ref.shape[0])], sem)
    copy.start()
    copy.wait()


SMEM = pl.BlockSpec(memory_space=pltpu.SMEM)
VMEM = pl.BlockSpec(memory_space=pltpu.VMEM)
PARAMS = pltpu.CompilerParams(vmem_limit_bytes=VMEM_LIMIT)


def cost(flops, bytes_accessed):
    return pl.CostEstimate(flops=flops, bytes_accessed=bytes_accessed, transcendentals=0)


def in_vmem(array):
    return pltpu.with_memory_space_constraint(array, pltpu.VMEM)


def body(n_row, n_col, blocks, slot_cols, counts, demand, value_added):
    rows, slots, size, _ = blocks.shape
    width = demand.shape[1]
    groups = demand.shape[0] // size
    group_devices = n_row // n_col
    paired = n_col == 2 and n_row == 16 and rows % 2 == 0
    half = rows // 2
    counts = counts.reshape(rows)

    sums, held = pl.pallas_call(
        sums_kernel,
        name="column_sums",
        out_shape=(
            jax.ShapeDtypeStruct((groups, size), jnp.float32),
            pltpu.VMEM(blocks.shape, blocks.dtype),
        ),
        in_specs=[pl.BlockSpec(memory_space=pltpu.HBM)] * 3,
        out_specs=(VMEM, VMEM),
        scratch_shapes=[
            pltpu.VMEM((groups + 1, 8, size), jnp.float32),
            pltpu.SMEM(slot_cols.shape, jnp.int32),
            pltpu.SMEM(counts.shape, jnp.int32),
            pltpu.SemaphoreType.DMA((2,)),
            pltpu.SemaphoreType.DMA((rows,)),
        ],
        compiler_params=PARAMS,
        cost_estimate=cost(0, 4 * rows * size * size * slots),
    )(*[pltpu.with_memory_space_constraint(array, pltpu.HBM) for array in (slot_cols, counts, blocks)])

    def flip(array, mask):
        return lax.ppermute(array, "row", [(i, i ^ mask) for i in range(n_row)])

    def swap(array):
        return lax.ppermute(array, "col", [(0, 1), (1, 0)])

    if paired:
        sums = sums + flip(sums.astype(jnp.bfloat16), 1).astype(jnp.float32)
        shared = sums.astype(jnp.bfloat16)
        for part in [flip(shared, mask) for mask in (12, 14, 8, 10, 4, 6, 2)]:
            sums = sums + part.astype(jnp.float32)
    else:
        sums = lax.psum(sums, "row")

    def layer_cost(count):
        return cost(2 * count * slots * size * size * width, count * slots * size * size * 2)

    def first_layer(sending, count, dtype, held):
        return pl.pallas_call(
            functools.partial(first_kernel, sending),
            name="first_layer",
            out_shape=(
                jax.ShapeDtypeStruct((count, size, width), dtype),
                pltpu.VMEM(blocks.shape, blocks.dtype),
            ),
            in_specs=[SMEM, SMEM, VMEM, VMEM, VMEM, VMEM],
            out_specs=(VMEM, VMEM),
            scratch_shapes=[
                pltpu.VMEM((groups, 1, size), jnp.float32),
                pltpu.VMEM((count, size, width), jnp.float32),
            ],
            input_output_aliases={5: 1},
            compiler_params=PARAMS,
            cost_estimate=layer_cost(count),
        )(
            slot_cols,
            counts,
            sums,
            value_added.reshape(groups, size),
            demand.reshape(groups, size, width),
            in_vmem(held),
        )

    def second_call(kernel, count, coefs, own, sources, keep_sources):
        dtype = jnp.bfloat16 if paired else jnp.float32
        out = jax.ShapeDtypeStruct((count, size, width), dtype)
        return pl.pallas_call(
            kernel,
            name="second_layer",
            out_shape=(out, jax.ShapeDtypeStruct((groups, size, width), jnp.bfloat16)) if keep_sources else out,
            in_specs=[SMEM, SMEM] + [VMEM] * (2 + len(sources)),
            out_specs=(VMEM, VMEM) if keep_sources else VMEM,
            scratch_shapes=[pltpu.VMEM((count, size, width), jnp.float32)],
            compiler_params=PARAMS,
            cost_estimate=layer_cost(count),
        )(slot_cols, counts, in_vmem(coefs), own, *sources)

    if not paired:
        group = lax.axis_index("col")
        partial, coefs = first_layer(None, rows, jnp.float32, held)
        layer_one = lax.psum(partial, "col").astype(jnp.bfloat16)
        gathered = lax.all_gather(layer_one, "row", axis=0, tiled=True)
        source = lax.dynamic_slice_in_dim(gathered, group * groups, groups, 0)
        partial = second_call(second_kernel, rows, coefs, layer_one, [source], False)
        return lax.psum(partial, "col").astype(jnp.bfloat16).reshape(rows * size, width)

    sent, coefs = first_layer(True, half, jnp.bfloat16, held)
    arrived = swap(sent)
    kept, coefs = first_layer(False, half, jnp.float32, coefs)
    own = (kept + arrived.astype(jnp.float32)).astype(jnp.bfloat16)

    piece = jax.ShapeDtypeStruct(own.shape, own.dtype)
    home, away = pl.pallas_call(
        choose_kernel,
        name="home_and_away",
        out_shape=(piece, piece),
        in_specs=[VMEM] * 2,
        out_specs=(VMEM, VMEM),
        compiler_params=PARAMS,
    )(own, flip(own, group_devices))

    def join(pieces):
        return pl.pallas_call(
            join_kernel,
            name="own_joined",
            out_shape=jax.ShapeDtypeStruct((len(pieces) * half, size, width), own.dtype),
            in_specs=[VMEM] * len(pieces),
            out_specs=VMEM,
            compiler_params=PARAMS,
        )(*pieces)

    def move(array, mask):
        pairs = [(i * 2 + c, (i ^ mask) * 2 + 1 - c) for i in range(n_row) for c in range(2)]
        return lax.ppermute(array, ("row", "col"), pairs)

    away = join([move(away, mask) for mask in (0, 2, 4, 6)])
    home = join([home] + [flip(home, mask) for mask in (2, 4, 6)])
    pieces = [home, away, flip(home, 1), flip(away, 1)]

    part_a, source = second_call(functools.partial(second_part_kernel, 0), half, coefs, own, pieces, True)
    other_a = swap(part_a)
    part_b = second_call(functools.partial(second_part_kernel, 1), half, coefs, own, [source], False)
    other_b = swap(part_b)

    def result(first_row, inputs):
        return pl.pallas_call(
            functools.partial(result_kernel, first_row),
            name="result",
            out_shape=jax.ShapeDtypeStruct((rows, size, width), jnp.bfloat16),
            in_specs=[VMEM, VMEM] + [pl.BlockSpec(memory_space=pltpu.HBM)] * (len(inputs) - 2),
            out_specs=pl.BlockSpec(memory_space=pltpu.HBM),
            scratch_shapes=[pltpu.VMEM(piece.shape, piece.dtype), pltpu.SemaphoreType.DMA],
            input_output_aliases={2: 0} if len(inputs) > 2 else {},
            compiler_params=PARAMS,
        )(*inputs)

    out = result(0, [part_a, other_a])
    return result(half, [part_b, other_b, out]).reshape(rows * size, width)


def solution(mesh):
    return jax.shard_map(
        functools.partial(body, mesh.shape["row"], mesh.shape["col"]),
        mesh=mesh,
        in_specs=(
            P("row", "col", None, None),
            P("row", "col"),
            P("row", "col"),
            P("col", None),
            P("col"),
        ),
        out_specs=P("row", None),
        check_vma=False,
    )
```

```python
import functools

import jax
import jax.numpy as jnp
from jax import lax
from jax.experimental import pallas as pl
from jax.experimental.pallas import tpu as pltpu
from jax.sharding import PartitionSpec as P

VMEM_LIMIT = 12 * 1024 * 1024


def divisor(slot_count, most):
    return max(size for size in range(1, most + 1) if slot_count % size == 0)


def chunk_total(counts_ref, b, chunk):
    return lax.div(counts_ref[b] + (chunk - 1), chunk)


def sums_kernel(cols_hbm, counts_hbm, blocks_ref, sums_ref, held_ref, acc_ref, cols_ref, counts_ref, list_sems, sems):
    rows, slots, size, _ = blocks_ref.shape
    groups = acc_ref.shape[0] - 1
    chunk = divisor(slots, 12)

    def fetch(b, k):
        part = pl.ds(k * chunk, chunk)
        return pltpu.make_async_copy(blocks_ref.at[b, part], held_ref.at[b, part], sems.at[b, k])

    counts_copy = pltpu.make_async_copy(counts_hbm, counts_ref, list_sems.at[0])
    cols_copy = pltpu.make_async_copy(cols_hbm, cols_ref, list_sems.at[1])
    counts_copy.start()
    cols_copy.start()
    for b in range(rows):
        fetch(b, 0).start()
    acc_ref[...] = jnp.zeros_like(acc_ref)
    counts_copy.wait()
    cols_copy.wait()
    for b in range(rows):
        for k in range(1, slots // chunk):

            @pl.when(counts_ref[b] > k * chunk)
            def _(b=b, k=k):
                fetch(b, k).start()

    def add(b, k):
        fetch(b, k).wait()
        for slot in range(k * chunk, (k + 1) * chunk):
            col = jnp.where(slot < counts_ref[b], cols_ref[b, slot], groups)
            block = held_ref[b, slot].astype(jnp.float32)
            acc_ref[col] += jnp.sum(block.reshape(size // 8, 8, size), axis=0)

    for b in range(rows):
        add(b, 0)
    for b in range(rows):
        for k in range(1, slots // chunk):

            @pl.when(counts_ref[b] > k * chunk)
            def _(b=b, k=k):
                add(b, k)

    sums_ref[...] = jnp.sum(acc_ref[:groups], axis=1)


def multiply_rows(rows, counts_ref, chunk, start, gather, acc_ref):
    def product(row, first):
        left, right = zip(*[gather(row, first + u) for u in range(chunk)])
        return jnp.dot(jnp.concatenate(left, axis=1), jnp.concatenate(right, axis=0), preferred_element_type=jnp.float32)

    for b, row in enumerate(rows):
        acc_ref[b] = start(b) + product(row, 0)
    for b, row in enumerate(rows):

        def add(k, carry, b=b, row=row):
            acc_ref[b] += product(row, k * chunk)
            return carry

        lax.fori_loop(1, chunk_total(counts_ref, row, chunk), add, 0)


def first_kernel(sending, cols_ref, counts_ref, sums_ref, added_ref, demand_ref, blocks_ref, out_ref, coef_ref, inverse_ref, acc_ref):
    slots, size = blocks_ref.shape[1:3]
    count = out_ref.shape[0]
    base = 0
    if sending is not None:
        side = lax.axis_index("col")
        base = (1 - side if sending else side) * count
    inverse_ref[...] = (1.0 / (sums_ref[...] + added_ref[...]))[:, None, :]

    def gather(row, slot):
        col = cols_ref[row, slot]
        scale = jnp.where(slot < counts_ref[row], inverse_ref[col], 0.0)
        scale = jnp.broadcast_to(scale, (16, size)).astype(jnp.bfloat16)
        coef = (blocks_ref[row, slot].reshape(size // 16, 16, size) * scale).reshape(size, size)
        coef_ref[row, slot] = coef
        return coef, demand_ref[col]

    rows = [base + b for b in range(count)]
    multiply_rows(rows, counts_ref, divisor(slots, 12), lambda b: 0.0, gather, acc_ref)
    out_ref[...] = acc_ref[...].astype(out_ref.dtype)


def second_rows(first_row, place, cols_ref, counts_ref, coef_ref, source_ref, start, out_ref, acc_ref):
    slots = coef_ref.shape[1]

    def gather(row, slot):
        return coef_ref[row, slot], source_ref[place(cols_ref[row, slot])]

    rows = [first_row + b for b in range(out_ref.shape[0])]
    multiply_rows(rows, counts_ref, divisor(slots, 12), start, gather, acc_ref)
    out_ref[...] = acc_ref[...].astype(out_ref.dtype)


def exact_scale(count, part):
    scale = -(-(1 << 16) // part)
    assert all((i * scale) >> 16 == i // part for i in range(count))
    return scale


GATHERED = (
    ((0, 0, 0), (0, 1, 0), (1, 0, 0), (1, 1, 0)),
    ((0, 0, 1), (0, 1, 1), (1, 0, 1)),
    ((1, 1, 1),),
)


def second_part_kernel(which, cols_ref, counts_ref, coef_ref, own_ref, *rest):
    part = own_ref.shape[0]
    if which == 0:
        pieces, (out_ref, source_ref, acc_ref) = rest[:-3], rest[-3:]
        for number, array in enumerate(pieces):
            core = number // len(GATHERED)
            for i, (z, y, away) in enumerate(GATHERED[number % len(GATHERED)]):
                at = ((z * 4 + y * 2 + core) * 2 + away) * part
                source_ref[at : at + part] = array[i * part : (i + 1) * part]
    else:
        source_ref, out_ref, acc_ref = rest
    side = lax.axis_index("col")
    near = lax.rem(lax.axis_index("row"), 8) * 2 + side
    scale = exact_scale(source_ref.shape[0], part)

    def place(col):
        piece = lax.shift_right_logical(col * scale, 16)
        return col + part * ((piece ^ near) - piece)

    def start(b):
        return jnp.where(side == which, own_ref[b].astype(jnp.float32), 0.0)

    second_rows(which * part, place, cols_ref, counts_ref, coef_ref, source_ref, start, out_ref, acc_ref)


def second_kernel(cols_ref, counts_ref, coef_ref, own_ref, source_ref, out_ref, acc_ref):
    first = lax.axis_index("col") == 0

    def start(b):
        return jnp.where(first, own_ref[b].astype(jnp.float32), 0.0)

    second_rows(0, lambda col: col, cols_ref, counts_ref, coef_ref, source_ref, start, out_ref, acc_ref)


def choose_kernel(own_ref, crossed_ref, home_ref, away_ref):
    owner = lax.div(lax.axis_index("row"), 8) == lax.axis_index("col")

    @pl.when(owner)
    def _():
        home_ref[...] = own_ref[...]
        away_ref[...] = crossed_ref[...]

    @pl.when(jnp.logical_not(owner))
    def _():
        home_ref[...] = crossed_ref[...]
        away_ref[...] = own_ref[...]


def join_kernel(*refs):
    pieces, joined_ref = refs[:-1], refs[-1]
    part = pieces[0].shape[0]
    for i, piece in enumerate(pieces):
        joined_ref[i * part : (i + 1) * part] = piece[...]


def result_kernel(first_row, mine_ref, other_ref, *rest):
    out_ref, sum_ref, sem = rest[-3:]
    sum_ref[...] = (mine_ref[...].astype(jnp.float32) + other_ref[...].astype(jnp.float32)).astype(sum_ref.dtype)
    copy = pltpu.make_async_copy(sum_ref, out_ref.at[pl.ds(first_row, sum_ref.shape[0])], sem)
    copy.start()
    copy.wait()


SMEM = pl.BlockSpec(memory_space=pltpu.SMEM)
VMEM = pl.BlockSpec(memory_space=pltpu.VMEM)
PARAMS = pltpu.CompilerParams(vmem_limit_bytes=VMEM_LIMIT)


def cost(flops, bytes_accessed):
    return pl.CostEstimate(flops=flops, bytes_accessed=bytes_accessed, transcendentals=0)


def in_vmem(array):
    return pltpu.with_memory_space_constraint(array, pltpu.VMEM)


def body(n_row, n_col, blocks, slot_cols, counts, demand, value_added):
    rows, slots, size, _ = blocks.shape
    width = demand.shape[1]
    groups = demand.shape[0] // size
    group_devices = n_row // n_col
    paired = n_col == 2 and n_row == 16 and rows % 2 == 0
    half = rows // 2
    counts = counts.reshape(rows)

    sums, held = pl.pallas_call(
        sums_kernel,
        name="column_sums",
        out_shape=(
            jax.ShapeDtypeStruct((groups, size), jnp.float32),
            pltpu.VMEM(blocks.shape, blocks.dtype),
        ),
        in_specs=[pl.BlockSpec(memory_space=pltpu.HBM)] * 3,
        out_specs=(VMEM, VMEM),
        scratch_shapes=[
            pltpu.VMEM((groups + 1, 8, size), jnp.float32),
            pltpu.SMEM(slot_cols.shape, jnp.int32),
            pltpu.SMEM(counts.shape, jnp.int32),
            pltpu.SemaphoreType.DMA((2,)),
            pltpu.SemaphoreType.DMA((rows, slots // divisor(slots, 12))),
        ],
        compiler_params=PARAMS,
        cost_estimate=cost(0, 4 * rows * size * size * slots),
    )(*[pltpu.with_memory_space_constraint(array, pltpu.HBM) for array in (slot_cols, counts, blocks)])

    def flip(array, mask):
        return lax.ppermute(array, "row", [(i, i ^ mask) for i in range(n_row)])

    def swap(array):
        return lax.ppermute(array, "col", [(0, 1), (1, 0)])

    if paired:
        for masks in ((1, 2, 3), (4, 8, 12)):
            sums = sums.astype(jnp.bfloat16)
            parts = [sums] + [flip(sums, m) for m in masks]
            sums = functools.reduce(jnp.add, [part.astype(jnp.float32) for part in parts])
    else:
        sums = lax.psum(sums, "row")

    def layer_cost(count):
        return cost(2 * count * slots * size * size * width, count * slots * size * size * 2)

    def first_layer(sending, count, dtype, held):
        return pl.pallas_call(
            functools.partial(first_kernel, sending),
            name="first_layer",
            out_shape=(
                jax.ShapeDtypeStruct((count, size, width), dtype),
                pltpu.VMEM(blocks.shape, blocks.dtype),
            ),
            in_specs=[SMEM, SMEM, VMEM, VMEM, VMEM, VMEM],
            out_specs=(VMEM, VMEM),
            scratch_shapes=[
                pltpu.VMEM((groups, 1, size), jnp.float32),
                pltpu.VMEM((count, size, width), jnp.float32),
            ],
            input_output_aliases={5: 1},
            compiler_params=PARAMS,
            cost_estimate=layer_cost(count),
        )(
            slot_cols,
            counts,
            sums,
            value_added.reshape(groups, size),
            demand.reshape(groups, size, width),
            in_vmem(held),
        )

    def second_call(kernel, count, coefs, own, sources, keep_sources):
        dtype = jnp.bfloat16 if paired else jnp.float32
        out = jax.ShapeDtypeStruct((count, size, width), dtype)
        return pl.pallas_call(
            kernel,
            name="second_layer",
            out_shape=(out, jax.ShapeDtypeStruct((groups, size, width), jnp.bfloat16)) if keep_sources else out,
            in_specs=[SMEM, SMEM] + [VMEM] * (2 + len(sources)),
            out_specs=(VMEM, VMEM) if keep_sources else VMEM,
            scratch_shapes=[pltpu.VMEM((count, size, width), jnp.float32)],
            compiler_params=PARAMS,
            cost_estimate=layer_cost(count),
        )(slot_cols, counts, in_vmem(coefs), own, *sources)

    if not paired:
        group = lax.axis_index("col")
        partial, coefs = first_layer(None, rows, jnp.float32, held)
        layer_one = lax.psum(partial, "col").astype(jnp.bfloat16)
        gathered = lax.all_gather(layer_one, "row", axis=0, tiled=True)
        source = lax.dynamic_slice_in_dim(gathered, group * groups, groups, 0)
        partial = second_call(second_kernel, rows, coefs, layer_one, [source], False)
        return lax.psum(partial, "col").astype(jnp.bfloat16).reshape(rows * size, width)

    sent, coefs = first_layer(True, half, jnp.bfloat16, held)
    arrived = swap(sent)
    kept, coefs = first_layer(False, half, jnp.float32, coefs)
    own = (kept + arrived.astype(jnp.float32)).astype(jnp.bfloat16)

    piece = jax.ShapeDtypeStruct(own.shape, own.dtype)
    home, away = pl.pallas_call(
        choose_kernel,
        name="home_and_away",
        out_shape=(piece, piece),
        in_specs=[VMEM] * 2,
        out_specs=(VMEM, VMEM),
        compiler_params=PARAMS,
    )(own, flip(own, group_devices))

    def join(pieces):
        return pl.pallas_call(
            join_kernel,
            name="own_joined",
            out_shape=jax.ShapeDtypeStruct((len(pieces) * half, size, width), own.dtype),
            in_specs=[VMEM] * len(pieces),
            out_specs=VMEM,
            compiler_params=PARAMS,
        )(*pieces)

    away = swap(away)
    home_y, home_z = flip(home, 2), flip(home, 4)
    away_y, away_z = flip(away, 2), flip(away, 4)
    gathered = [join([home, home_y, home_z, flip(home_z, 2)]), join([away, away_y, away_z]), flip(away_y, 4)]
    pieces = gathered + [flip(part, 1) for part in gathered]

    part_a, source = second_call(functools.partial(second_part_kernel, 0), half, coefs, own, pieces, True)
    other_a = swap(part_a)
    part_b = second_call(functools.partial(second_part_kernel, 1), half, coefs, own, [source], False)
    other_b = swap(part_b)

    def result(first_row, inputs):
        return pl.pallas_call(
            functools.partial(result_kernel, first_row),
            name="result",
            out_shape=jax.ShapeDtypeStruct((rows, size, width), jnp.bfloat16),
            in_specs=[VMEM, VMEM] + [pl.BlockSpec(memory_space=pltpu.HBM)] * (len(inputs) - 2),
            out_specs=pl.BlockSpec(memory_space=pltpu.HBM),
            scratch_shapes=[pltpu.VMEM(piece.shape, piece.dtype), pltpu.SemaphoreType.DMA],
            input_output_aliases={2: 0} if len(inputs) > 2 else {},
            compiler_params=PARAMS,
        )(*inputs)

    out = result(0, [part_a, other_a])
    return result(half, [part_b, other_b, out]).reshape(rows * size, width)


def solution(mesh):
    return jax.shard_map(
        functools.partial(body, mesh.shape["row"], mesh.shape["col"]),
        mesh=mesh,
        in_specs=(
            P("row", "col", None, None),
            P("row", "col"),
            P("row", "col"),
            P("col", None),
            P("col"),
        ),
        out_specs=P("row", None),
        check_vma=False,
    )
```

```python
import functools

import jax
import jax.numpy as jnp
from jax import lax
from jax.experimental import pallas as pl
from jax.experimental.pallas import tpu as pltpu
from jax.sharding import PartitionSpec as P

VMEM_LIMIT = 12 * 1024 * 1024


def divisor(slot_count, most):
    return max(size for size in range(1, most + 1) if slot_count % size == 0)


def chunk_total(counts_ref, b, chunk):
    return lax.div(counts_ref[b] + (chunk - 1), chunk)


def sums_kernel(cols_hbm, counts_hbm, blocks_ref, sums_ref, held_ref, acc_ref, cols_ref, counts_ref, list_sems, sems):
    rows, slots, size, _ = blocks_ref.shape
    groups = acc_ref.shape[0] - 1
    chunk = divisor(slots, 12)

    def fetch(b, k):
        part = pl.ds(k * chunk, chunk)
        return pltpu.make_async_copy(blocks_ref.at[b, part], held_ref.at[b, part], sems.at[b, k])

    counts_copy = pltpu.make_async_copy(counts_hbm, counts_ref, list_sems.at[0])
    cols_copy = pltpu.make_async_copy(cols_hbm, cols_ref, list_sems.at[1])
    counts_copy.start()
    cols_copy.start()
    for b in range(rows):
        fetch(b, 0).start()
    acc_ref[...] = jnp.zeros_like(acc_ref)
    counts_copy.wait()
    cols_copy.wait()
    for b in range(rows):
        for k in range(1, slots // chunk):

            @pl.when(counts_ref[b] > k * chunk)
            def _(b=b, k=k):
                fetch(b, k).start()

    def add(b, k):
        fetch(b, k).wait()
        for slot in range(k * chunk, (k + 1) * chunk):
            col = jnp.where(slot < counts_ref[b], cols_ref[b, slot], groups)
            block = held_ref[b, slot].astype(jnp.float32)
            acc_ref[col] += jnp.sum(block.reshape(size // 8, 8, size), axis=0)

    for b in range(rows):
        add(b, 0)
    for b in range(rows):
        for k in range(1, slots // chunk):

            @pl.when(counts_ref[b] > k * chunk)
            def _(b=b, k=k):
                add(b, k)

    sums_ref[...] = jnp.sum(acc_ref[:groups], axis=1)


def multiply_rows(rows, counts_ref, chunk, start, gather, acc_ref):
    def product(row, first):
        left, right = zip(*[gather(row, first + u) for u in range(chunk)])
        return jnp.dot(jnp.concatenate(left, axis=1), jnp.concatenate(right, axis=0), preferred_element_type=jnp.float32)

    for b, row in enumerate(rows):
        acc_ref[b] = start(b) + product(row, 0)
    for b, row in enumerate(rows):

        def add(k, carry, b=b, row=row):
            acc_ref[b] += product(row, k * chunk)
            return carry

        lax.fori_loop(1, chunk_total(counts_ref, row, chunk), add, 0)


def first_kernel(sending, cols_ref, counts_ref, sums_ref, added_ref, demand_ref, blocks_ref, out_ref, coef_ref, inverse_ref, acc_ref):
    slots, size = blocks_ref.shape[1:3]
    count = out_ref.shape[0]
    base = 0
    if sending is not None:
        side = lax.axis_index("col")
        base = (1 - side if sending else side) * count
    inverse_ref[...] = (1.0 / (sums_ref[...] + added_ref[...]))[:, None, :]

    def gather(row, slot):
        col = cols_ref[row, slot]
        scale = jnp.where(slot < counts_ref[row], inverse_ref[col], 0.0)
        scale = jnp.broadcast_to(scale, (16, size)).astype(jnp.bfloat16)
        coef = (blocks_ref[row, slot].reshape(size // 16, 16, size) * scale).reshape(size, size)
        coef_ref[row, slot] = coef
        return coef, demand_ref[col]

    rows = [base + b for b in range(count)]
    multiply_rows(rows, counts_ref, divisor(slots, 12), lambda b: 0.0, gather, acc_ref)
    out_ref[...] = acc_ref[...].astype(out_ref.dtype)


def second_rows(first_row, place, cols_ref, counts_ref, coef_ref, source_ref, start, out_ref, acc_ref):
    slots = coef_ref.shape[1]

    def gather(row, slot):
        return coef_ref[row, slot], source_ref[place(cols_ref[row, slot])]

    rows = [first_row + b for b in range(out_ref.shape[0])]
    multiply_rows(rows, counts_ref, divisor(slots, 12), start, gather, acc_ref)
    out_ref[...] = acc_ref[...].astype(out_ref.dtype)


def exact_scale(count, part):
    scale = -(-(1 << 16) // part)
    assert all((i * scale) >> 16 == i // part for i in range(count))
    return scale


PLACES = ((0, 0), (0, 1), (1, 0), (1, 1))


def second_part_kernel(which, cols_ref, counts_ref, coef_ref, own_ref, *rest):
    part = own_ref.shape[0]
    if which == 0:
        pieces, (out_ref, source_ref, acc_ref) = rest[:-3], rest[-3:]
        for array, (core, away) in zip(pieces, ((0, 0), (0, 1), (1, 0), (1, 1))):
            for i, (z, y) in enumerate(PLACES):
                at = ((z * 4 + y * 2 + core) * 2 + away) * part
                source_ref[at : at + part] = array[i * part : (i + 1) * part]
    else:
        source_ref, out_ref, acc_ref = rest
    side = lax.axis_index("col")
    near = lax.rem(lax.axis_index("row"), 8) * 2 + side
    scale = exact_scale(source_ref.shape[0], part)

    def place(col):
        piece = lax.shift_right_logical(col * scale, 16)
        return col + part * ((piece ^ near) - piece)

    def start(b):
        return jnp.where(side == which, own_ref[b].astype(jnp.float32), 0.0)

    second_rows(which * part, place, cols_ref, counts_ref, coef_ref, source_ref, start, out_ref, acc_ref)


def second_kernel(cols_ref, counts_ref, coef_ref, own_ref, source_ref, out_ref, acc_ref):
    first = lax.axis_index("col") == 0

    def start(b):
        return jnp.where(first, own_ref[b].astype(jnp.float32), 0.0)

    second_rows(0, lambda col: col, cols_ref, counts_ref, coef_ref, source_ref, start, out_ref, acc_ref)


def choose_kernel(own_ref, crossed_ref, home_ref, away_ref):
    owner = lax.div(lax.axis_index("row"), 8) == lax.axis_index("col")

    @pl.when(owner)
    def _():
        home_ref[...] = own_ref[...]
        away_ref[...] = crossed_ref[...]

    @pl.when(jnp.logical_not(owner))
    def _():
        home_ref[...] = crossed_ref[...]
        away_ref[...] = own_ref[...]


def join_kernel(*refs):
    pieces, joined_ref = refs[:-1], refs[-1]
    part = pieces[0].shape[0]
    for i, piece in enumerate(pieces):
        joined_ref[i * part : (i + 1) * part] = piece[...]


def result_kernel(first_row, mine_ref, other_ref, *rest):
    out_ref, sum_ref, sem = rest[-3:]
    sum_ref[...] = (mine_ref[...].astype(jnp.float32) + other_ref[...].astype(jnp.float32)).astype(sum_ref.dtype)
    copy = pltpu.make_async_copy(sum_ref, out_ref.at[pl.ds(first_row, sum_ref.shape[0])], sem)
    copy.start()
    copy.wait()


SMEM = pl.BlockSpec(memory_space=pltpu.SMEM)
VMEM = pl.BlockSpec(memory_space=pltpu.VMEM)
PARAMS = pltpu.CompilerParams(vmem_limit_bytes=VMEM_LIMIT)


def cost(flops, bytes_accessed):
    return pl.CostEstimate(flops=flops, bytes_accessed=bytes_accessed, transcendentals=0)


def in_vmem(array):
    return pltpu.with_memory_space_constraint(array, pltpu.VMEM)


def body(n_row, n_col, blocks, slot_cols, counts, demand, value_added):
    rows, slots, size, _ = blocks.shape
    width = demand.shape[1]
    groups = demand.shape[0] // size
    group_devices = n_row // n_col
    paired = n_col == 2 and n_row == 16 and rows % 2 == 0
    half = rows // 2
    counts = counts.reshape(rows)

    sums, held = pl.pallas_call(
        sums_kernel,
        name="column_sums",
        out_shape=(
            jax.ShapeDtypeStruct((groups, size), jnp.float32),
            pltpu.VMEM(blocks.shape, blocks.dtype),
        ),
        in_specs=[pl.BlockSpec(memory_space=pltpu.HBM)] * 3,
        out_specs=(VMEM, VMEM),
        scratch_shapes=[
            pltpu.VMEM((groups + 1, 8, size), jnp.float32),
            pltpu.SMEM(slot_cols.shape, jnp.int32),
            pltpu.SMEM(counts.shape, jnp.int32),
            pltpu.SemaphoreType.DMA((2,)),
            pltpu.SemaphoreType.DMA((rows, slots // divisor(slots, 12))),
        ],
        compiler_params=PARAMS,
        cost_estimate=cost(0, 4 * rows * size * size * slots),
    )(*[pltpu.with_memory_space_constraint(array, pltpu.HBM) for array in (slot_cols, counts, blocks)])

    def flip(array, mask):
        return lax.ppermute(array, "row", [(i, i ^ mask) for i in range(n_row)])

    def swap(array):
        return lax.ppermute(array, "col", [(0, 1), (1, 0)])

    if paired:
        for masks in ((1, 2, 3), (4, 8, 12)):
            sums = sums.astype(jnp.bfloat16)
            parts = [sums] + [flip(sums, m) for m in masks]
            sums = functools.reduce(jnp.add, [part.astype(jnp.float32) for part in parts])
    else:
        sums = lax.psum(sums, "row")

    def layer_cost(count):
        return cost(2 * count * slots * size * size * width, count * slots * size * size * 2)

    def first_layer(sending, count, dtype, held):
        return pl.pallas_call(
            functools.partial(first_kernel, sending),
            name="first_layer",
            out_shape=(
                jax.ShapeDtypeStruct((count, size, width), dtype),
                pltpu.VMEM(blocks.shape, blocks.dtype),
            ),
            in_specs=[SMEM, SMEM, VMEM, VMEM, VMEM, VMEM],
            out_specs=(VMEM, VMEM),
            scratch_shapes=[
                pltpu.VMEM((groups, 1, size), jnp.float32),
                pltpu.VMEM((count, size, width), jnp.float32),
            ],
            input_output_aliases={5: 1},
            compiler_params=PARAMS,
            cost_estimate=layer_cost(count),
        )(
            slot_cols,
            counts,
            sums,
            value_added.reshape(groups, size),
            demand.reshape(groups, size, width),
            in_vmem(held),
        )

    def second_call(kernel, count, coefs, own, sources, keep_sources):
        dtype = jnp.bfloat16 if paired else jnp.float32
        out = jax.ShapeDtypeStruct((count, size, width), dtype)
        return pl.pallas_call(
            kernel,
            name="second_layer",
            out_shape=(out, jax.ShapeDtypeStruct((groups, size, width), jnp.bfloat16)) if keep_sources else out,
            in_specs=[SMEM, SMEM] + [VMEM] * (2 + len(sources)),
            out_specs=(VMEM, VMEM) if keep_sources else VMEM,
            scratch_shapes=[pltpu.VMEM((count, size, width), jnp.float32)],
            compiler_params=PARAMS,
            cost_estimate=layer_cost(count),
        )(slot_cols, counts, in_vmem(coefs), own, *sources)

    if not paired:
        group = lax.axis_index("col")
        partial, coefs = first_layer(None, rows, jnp.float32, held)
        layer_one = lax.psum(partial, "col").astype(jnp.bfloat16)
        gathered = lax.all_gather(layer_one, "row", axis=0, tiled=True)
        source = lax.dynamic_slice_in_dim(gathered, group * groups, groups, 0)
        partial = second_call(second_kernel, rows, coefs, layer_one, [source], False)
        return lax.psum(partial, "col").astype(jnp.bfloat16).reshape(rows * size, width)

    sent, coefs = first_layer(True, half, jnp.bfloat16, held)
    arrived = swap(sent)
    kept, coefs = first_layer(False, half, jnp.float32, coefs)
    own = (kept + arrived.astype(jnp.float32)).astype(jnp.bfloat16)

    piece = jax.ShapeDtypeStruct(own.shape, own.dtype)
    home, away = pl.pallas_call(
        choose_kernel,
        name="home_and_away",
        out_shape=(piece, piece),
        in_specs=[VMEM] * 2,
        out_specs=(VMEM, VMEM),
        compiler_params=PARAMS,
    )(own, flip(own, group_devices))

    def join(pieces):
        return pl.pallas_call(
            join_kernel,
            name="own_joined",
            out_shape=jax.ShapeDtypeStruct((len(pieces) * half, size, width), own.dtype),
            in_specs=[VMEM] * len(pieces),
            out_specs=VMEM,
            compiler_params=PARAMS,
        )(*pieces)

    gathered = [join([part] + [flip(part, mask) for mask in (2, 4, 6)]) for part in (home, swap(away))]
    pieces = gathered + [flip(part, 1) for part in gathered]

    part_a, source = second_call(functools.partial(second_part_kernel, 0), half, coefs, own, pieces, True)
    other_a = swap(part_a)
    part_b = second_call(functools.partial(second_part_kernel, 1), half, coefs, own, [source], False)
    other_b = swap(part_b)

    def result(first_row, inputs):
        return pl.pallas_call(
            functools.partial(result_kernel, first_row),
            name="result",
            out_shape=jax.ShapeDtypeStruct((rows, size, width), jnp.bfloat16),
            in_specs=[VMEM, VMEM] + [pl.BlockSpec(memory_space=pltpu.HBM)] * (len(inputs) - 2),
            out_specs=pl.BlockSpec(memory_space=pltpu.HBM),
            scratch_shapes=[pltpu.VMEM(piece.shape, piece.dtype), pltpu.SemaphoreType.DMA],
            input_output_aliases={2: 0} if len(inputs) > 2 else {},
            compiler_params=PARAMS,
        )(*inputs)

    out = result(0, [part_a, other_a])
    return result(half, [part_b, other_b, out]).reshape(rows * size, width)


def solution(mesh):
    return jax.shard_map(
        functools.partial(body, mesh.shape["row"], mesh.shape["col"]),
        mesh=mesh,
        in_specs=(
            P("row", "col", None, None),
            P("row", "col"),
            P("row", "col"),
            P("col", None),
            P("col"),
        ),
        out_specs=P("row", None),
        check_vma=False,
    )
```

```python
import functools

import jax
import jax.numpy as jnp
from jax import lax
from jax.experimental import pallas as pl
from jax.experimental.pallas import tpu as pltpu
from jax.sharding import PartitionSpec as P

VMEM_LIMIT = 12 * 1024 * 1024


def divisor(slot_count, most):
    return max(size for size in range(1, most + 1) if slot_count % size == 0)


def sums_kernel(cols_hbm, counts_hbm, blocks_ref, sums_ref, held_ref, acc_ref, cols_ref, counts_ref, list_sems, sems):
    rows, slots, size, _ = blocks_ref.shape
    groups = acc_ref.shape[0] - 1
    chunk = divisor(slots, 12)

    def fetch(b, k):
        part = pl.ds(k * chunk, chunk)
        return pltpu.make_async_copy(blocks_ref.at[b, part], held_ref.at[b, part], sems.at[b, k])

    counts_copy = pltpu.make_async_copy(counts_hbm, counts_ref, list_sems.at[0])
    cols_copy = pltpu.make_async_copy(cols_hbm, cols_ref, list_sems.at[1])
    counts_copy.start()
    cols_copy.start()
    for b in range(rows):
        fetch(b, 0).start()
    acc_ref[...] = jnp.zeros_like(acc_ref)
    counts_copy.wait()
    cols_copy.wait()
    for b in range(rows):
        for k in range(1, slots // chunk):

            @pl.when(counts_ref[b] > k * chunk)
            def _(b=b, k=k):
                fetch(b, k).start()

    def add(b, k):
        fetch(b, k).wait()
        for slot in range(k * chunk, (k + 1) * chunk):
            col = jnp.where(slot < counts_ref[b], cols_ref[b, slot], groups)
            block = held_ref[b, slot].astype(jnp.float32)
            acc_ref[col] += jnp.sum(block.reshape(size // 8, 8, size), axis=0)

    for b in range(rows):
        add(b, 0)
    for b in range(rows):
        for k in range(1, slots // chunk):

            @pl.when(counts_ref[b] > k * chunk)
            def _(b=b, k=k):
                add(b, k)

    sums_ref[...] = jnp.sum(acc_ref[:groups], axis=1)


def multiply_rows(rows, totals, chunk, start, gather, acc_ref):
    def product(row, first):
        left, right = zip(*[gather(row, first + u) for u in range(chunk)])
        return jnp.dot(jnp.concatenate(left, axis=1), jnp.concatenate(right, axis=0), preferred_element_type=jnp.float32)

    for b, row in enumerate(rows):
        acc_ref[b] = start(b) + product(row, 0)
    for b, row in enumerate(rows):

        def add(k, carry, b=b, row=row):
            acc_ref[b] += product(row, k * chunk)
            return carry

        lax.fori_loop(1, lax.div(totals[b] + (chunk - 1), chunk), add, 0)


def first_kernel(sending, cols_ref, counts_ref, sums_ref, added_ref, demand_ref, blocks_ref, *rest):
    out_ref, coef_ref, inverse_ref, acc_ref = rest[-4:]
    slots, size = blocks_ref.shape[1:3]
    count = out_ref.shape[0]
    base = 0
    if sending is not None:
        side = lax.axis_index("col")
        base = (1 - side if sending else side) * count
    inverse_ref[...] = (1.0 / (sums_ref[...] + added_ref[...]))[:, None, :]

    def gather(row, slot):
        col = cols_ref[row, slot]
        scale = jnp.where(slot < counts_ref[row], inverse_ref[col], 0.0)
        scale = jnp.broadcast_to(scale, (16, size)).astype(jnp.bfloat16)
        coef = (blocks_ref[row, slot].reshape(size // 16, 16, size) * scale).reshape(size, size)
        coef_ref[row, slot] = coef
        return coef, demand_ref[col]

    rows = [base + b for b in range(count)]
    multiply_rows(rows, [counts_ref[row] for row in rows], divisor(slots, 12), lambda b: 0.0, gather, acc_ref)
    out_ref[...] = acc_ref[...].astype(out_ref.dtype)


def second_rows(first_row, place, cols_ref, counts_ref, coef_ref, source_ref, start, out_ref, acc_ref):
    slots = coef_ref.shape[1]

    def gather(row, slot):
        return coef_ref[row, slot], source_ref[place(cols_ref[row, slot])]

    rows = [first_row + b for b in range(out_ref.shape[0])]
    multiply_rows(rows, [counts_ref[row] for row in rows], divisor(slots, 12), start, gather, acc_ref)
    out_ref[...] = acc_ref[...].astype(out_ref.dtype)


def exact_scale(count, part):
    scale = -(-(1 << 16) // part)
    assert all((i * scale) >> 16 == i // part for i in range(count))
    return scale


FIRST_CHUNK, LAST_CHUNK = 8, 4


def plan_kernel(part, cols_ref, counts_ref, _, first_ref, last_ref, totals_ref):
    rows, slots = cols_ref.shape
    near = lax.rem(lax.axis_index("row"), 8) * 2 + lax.axis_index("col")
    scale = exact_scale(16 * part, part)
    for b in range(rows):

        def add(slot, ends, b=b):
            first, last = ends
            col = cols_ref[b, slot]
            piece = lax.shift_right_logical(col * scale, 16)
            place = piece ^ near
            group = place & 3
            entry = slot * 256 + lax.shift_right_logical(place, 2) * part + col - part * piece
            is_last = (group == 3).astype(jnp.int32)
            first_ref[b, first] = entry + group * (4 * part)
            last_ref[b, last] = entry
            return first + 1 - is_last, last + is_last

        first, last = lax.fori_loop(0, counts_ref[b], add, (0, 0))
        totals_ref[0, b] = first
        totals_ref[1, b] = last
        for ref, end, chunk in ((first_ref, first, FIRST_CHUNK), (last_ref, last, LAST_CHUNK)):
            for u in range(chunk):
                ref[b, end + u] = 0


def list_gather(list_ref, totals_ref, which, coef_ref, source_ref):
    def gather(row, i):
        entry = list_ref[row, i]
        coef = coef_ref[row, lax.shift_right_logical(entry, 8)]
        return jnp.where(i < totals_ref[which, row], coef, jnp.zeros_like(coef)), source_ref[entry & 255]

    return gather


def second_first_kernel(list_ref, totals_ref, coef_ref, *rest):
    pieces, (out_ref, source_ref) = rest[:-2], rest[-2:]
    length = pieces[0].shape[0]
    for i, piece in enumerate(pieces):
        source_ref[i * length : (i + 1) * length] = piece[...]
    gather = list_gather(list_ref, totals_ref, 0, coef_ref, source_ref)
    rows = list(range(out_ref.shape[0]))
    totals = [totals_ref[0, row] for row in rows]
    multiply_rows(rows, totals, FIRST_CHUNK, lambda b: 0.0, gather, out_ref)


def second_last_kernel(which, list_ref, totals_ref, coef_ref, sum_ref, own_ref, source_ref, out_ref, acc_ref):
    count = out_ref.shape[0]
    side = lax.axis_index("col")
    gather = list_gather(list_ref, totals_ref, 1, coef_ref, source_ref)
    rows = [which * count + b for b in range(count)]
    totals = [totals_ref[1, row] for row in rows]

    def start(b):
        return sum_ref[rows[b]] + jnp.where(side == which, own_ref[b].astype(jnp.float32), 0.0)

    multiply_rows(rows, totals, LAST_CHUNK, start, gather, acc_ref)
    out_ref[...] = acc_ref[...].astype(out_ref.dtype)


def second_kernel(cols_ref, counts_ref, coef_ref, own_ref, source_ref, out_ref, acc_ref):
    first = lax.axis_index("col") == 0

    def start(b):
        return jnp.where(first, own_ref[b].astype(jnp.float32), 0.0)

    second_rows(0, lambda col: col, cols_ref, counts_ref, coef_ref, source_ref, start, out_ref, acc_ref)


def choose_kernel(own_ref, crossed_ref, home_ref, away_ref):
    owner = lax.div(lax.axis_index("row"), 8) == lax.axis_index("col")

    @pl.when(owner)
    def _():
        home_ref[...] = own_ref[...]
        away_ref[...] = crossed_ref[...]

    @pl.when(jnp.logical_not(owner))
    def _():
        home_ref[...] = crossed_ref[...]
        away_ref[...] = own_ref[...]


def join_kernel(*refs):
    pieces, joined_ref = refs[:-1], refs[-1]
    part = pieces[0].shape[0]
    for i, piece in zip((0, 3, 2, 1), pieces):
        joined_ref[i * part : (i + 1) * part] = piece[...]


def result_kernel(first_row, mine_ref, other_ref, *rest):
    out_ref, sum_ref, sem = rest[-3:]
    sum_ref[...] = (mine_ref[...].astype(jnp.float32) + other_ref[...].astype(jnp.float32)).astype(sum_ref.dtype)
    copy = pltpu.make_async_copy(sum_ref, out_ref.at[pl.ds(first_row, sum_ref.shape[0])], sem)
    copy.start()
    copy.wait()


SMEM = pl.BlockSpec(memory_space=pltpu.SMEM)
VMEM = pl.BlockSpec(memory_space=pltpu.VMEM)
PARAMS = pltpu.CompilerParams(vmem_limit_bytes=VMEM_LIMIT)


def cost(flops, bytes_accessed):
    return pl.CostEstimate(flops=flops, bytes_accessed=bytes_accessed, transcendentals=0)


def in_vmem(array):
    return pltpu.with_memory_space_constraint(array, pltpu.VMEM)


def body(n_row, n_col, blocks, slot_cols, counts, demand, value_added):
    rows, slots, size, _ = blocks.shape
    width = demand.shape[1]
    groups = demand.shape[0] // size
    group_devices = n_row // n_col
    paired = n_col == 2 and n_row == 16 and rows % 2 == 0 and rows <= 12
    half = rows // 2
    counts = counts.reshape(rows)

    sums, held = pl.pallas_call(
        sums_kernel,
        name="column_sums",
        out_shape=(
            jax.ShapeDtypeStruct((groups, size), jnp.float32),
            pltpu.VMEM(blocks.shape, blocks.dtype),
        ),
        in_specs=[pl.BlockSpec(memory_space=pltpu.HBM)] * 3,
        out_specs=(VMEM, VMEM),
        scratch_shapes=[
            pltpu.VMEM((groups + 1, 8, size), jnp.float32),
            pltpu.SMEM(slot_cols.shape, jnp.int32),
            pltpu.SMEM(counts.shape, jnp.int32),
            pltpu.SemaphoreType.DMA((2,)),
            pltpu.SemaphoreType.DMA((rows, slots // divisor(slots, 12))),
        ],
        compiler_params=PARAMS,
        cost_estimate=cost(0, 4 * rows * size * size * slots),
    )(*[pltpu.with_memory_space_constraint(array, pltpu.HBM) for array in (slot_cols, counts, blocks)])

    def flip(array, mask):
        return lax.ppermute(array, "row", [(i, i ^ mask) for i in range(n_row)])

    def swap(array):
        return lax.ppermute(array, "col", [(0, 1), (1, 0)])

    if paired:
        for masks in ((1, 2, 3), (12, 8, 4)):
            sums = sums.astype(jnp.bfloat16)
            parts = [sums] + [flip(sums, m) for m in masks]
            if masks[0] == 12:
                plan = pl.pallas_call(
                    functools.partial(plan_kernel, half),
                    name="slot_plan",
                    out_shape=(
                        jax.ShapeDtypeStruct((rows, slots + FIRST_CHUNK), jnp.int32),
                        jax.ShapeDtypeStruct((rows, slots + FIRST_CHUNK), jnp.int32),
                        jax.ShapeDtypeStruct((2, rows), jnp.int32),
                    ),
                    in_specs=[SMEM, SMEM, pl.BlockSpec(memory_space=pl.ANY)],
                    out_specs=(SMEM, SMEM, SMEM),
                    compiler_params=PARAMS,
                    cost_estimate=cost(10**9, 10**6),
                )(slot_cols, counts, sums)
            sums = functools.reduce(jnp.add, [part.astype(jnp.float32) for part in parts])
    else:
        sums = lax.psum(sums, "row")

    def layer_cost(count):
        return cost(2 * count * slots * size * size * width, count * slots * size * size * 2)

    def first_layer(sending, count, dtype, held, earlier=()):
        return pl.pallas_call(
            functools.partial(first_kernel, sending),
            name="first_layer",
            out_shape=(
                jax.ShapeDtypeStruct((count, size, width), dtype),
                pltpu.VMEM(blocks.shape, blocks.dtype),
            ),
            in_specs=[SMEM, SMEM, VMEM, VMEM, VMEM, VMEM] + [pl.BlockSpec(memory_space=pl.ANY)] * len(earlier),
            out_specs=(VMEM, VMEM),
            scratch_shapes=[
                pltpu.VMEM((groups, 1, size), jnp.float32),
                pltpu.VMEM((count, size, width), jnp.float32),
            ],
            input_output_aliases={5: 1},
            compiler_params=PARAMS,
            cost_estimate=layer_cost(count),
        )(
            slot_cols,
            counts,
            sums,
            value_added.reshape(groups, size),
            demand.reshape(groups, size, width),
            in_vmem(held),
            *earlier,
        )

    def second_call(kernel, count, lists, inputs, scratch_shapes, dtype):
        return pl.pallas_call(
            kernel,
            name="second_layer",
            out_shape=jax.ShapeDtypeStruct((count, size, width), dtype),
            in_specs=[SMEM] * 2 + [VMEM] * len(inputs),
            out_specs=VMEM,
            scratch_shapes=scratch_shapes,
            compiler_params=PARAMS,
            cost_estimate=layer_cost(count),
        )(*lists, in_vmem(inputs[0]), *inputs[1:])

    if not paired:
        group = lax.axis_index("col")
        partial, coefs = first_layer(None, rows, jnp.float32, held)
        layer_one = lax.psum(partial, "col").astype(jnp.bfloat16)
        gathered = lax.all_gather(layer_one, "row", axis=0, tiled=True)
        source = lax.dynamic_slice_in_dim(gathered, group * groups, groups, 0)
        sums_shape = pltpu.VMEM((rows, size, width), jnp.float32)
        lists, inputs = [slot_cols, counts], [coefs, layer_one, source]
        partial = second_call(second_kernel, rows, lists, inputs, [sums_shape], jnp.float32)
        return lax.psum(partial, "col").astype(jnp.bfloat16).reshape(rows * size, width)

    sent, coefs = first_layer(True, half, jnp.bfloat16, held, plan)
    arrived = swap(sent)
    kept, coefs = first_layer(False, half, jnp.float32, coefs)
    own = (kept + arrived.astype(jnp.float32)).astype(jnp.bfloat16)

    piece = jax.ShapeDtypeStruct(own.shape, own.dtype)
    home, away = pl.pallas_call(
        choose_kernel,
        name="home_and_away",
        out_shape=(piece, piece),
        in_specs=[VMEM] * 2,
        out_specs=(VMEM, VMEM),
        compiler_params=PARAMS,
    )(own, flip(own, group_devices))

    def join(pieces):
        return pl.pallas_call(
            join_kernel,
            name="own_joined",
            out_shape=jax.ShapeDtypeStruct((len(pieces) * half, size, width), own.dtype),
            in_specs=[VMEM] * len(pieces),
            out_specs=VMEM,
            compiler_params=PARAMS,
        )(*pieces)

    def spread(part):
        return join([part, flip(part, 6), flip(part, 4), flip(part, 2)])

    home, away = spread(home), spread(swap(away))
    home_core, away_core = flip(home, 1), flip(away, 1)
    first_list, last_list, totals = plan
    sources = pltpu.VMEM((3 * home.shape[0], size, width), jnp.bfloat16)
    lists, inputs = [first_list, totals], [coefs, home, away, home_core]
    total = second_call(second_first_kernel, rows, lists, inputs, [sources], jnp.float32)

    def last_pass(which):
        kernel = functools.partial(second_last_kernel, which)
        sums_shape = pltpu.VMEM((half, size, width), jnp.float32)
        lists, inputs = [last_list, totals], [coefs, total, own, away_core]
        return second_call(kernel, half, lists, inputs, [sums_shape], jnp.bfloat16)

    part_a = last_pass(0)
    other_a = swap(part_a)
    part_b = last_pass(1)
    other_b = swap(part_b)

    def result(first_row, inputs):
        return pl.pallas_call(
            functools.partial(result_kernel, first_row),
            name="result",
            out_shape=jax.ShapeDtypeStruct((rows, size, width), jnp.bfloat16),
            in_specs=[VMEM, VMEM] + [pl.BlockSpec(memory_space=pltpu.HBM)] * (len(inputs) - 2),
            out_specs=pl.BlockSpec(memory_space=pltpu.HBM),
            scratch_shapes=[pltpu.VMEM(piece.shape, piece.dtype), pltpu.SemaphoreType.DMA],
            input_output_aliases={2: 0} if len(inputs) > 2 else {},
            compiler_params=PARAMS,
        )(*inputs)

    out = result(0, [part_a, other_a])
    return result(half, [part_b, other_b, out]).reshape(rows * size, width)


def solution(mesh):
    return jax.shard_map(
        functools.partial(body, mesh.shape["row"], mesh.shape["col"]),
        mesh=mesh,
        in_specs=(
            P("row", "col", None, None),
            P("row", "col"),
            P("row", "col"),
            P("col", None),
            P("col"),
        ),
        out_specs=P("row", None),
        check_vma=False,
    )
```

```python
import functools

import jax
import jax.numpy as jnp
from jax import lax
from jax.experimental import pallas as pl
from jax.experimental.pallas import tpu as pltpu
from jax.sharding import PartitionSpec as P

VMEM_LIMIT = 12 * 1024 * 1024


def slot_ranges(slots):
    first = min(12, slots)
    return [range(first)] + ([range(first, slots)] if slots > first else [])


def sums_kernel(cols_hbm, counts_hbm, blocks_ref, sums_ref, held_ref, acc_ref, cols_ref, counts_ref, list_sems, sems):
    rows, slots, size, _ = blocks_ref.shape
    groups = acc_ref.shape[0] - 1
    first, *others = slot_ranges(slots)

    def fetch(b, part):
        span = pl.ds(part.start, len(part))
        return pltpu.make_async_copy(blocks_ref.at[b, span], held_ref.at[b, span], sems.at[b, min(part.start, 1)])

    counts_copy = pltpu.make_async_copy(counts_hbm, counts_ref, list_sems.at[0])
    cols_copy = pltpu.make_async_copy(cols_hbm, cols_ref, list_sems.at[1])
    counts_copy.start()
    cols_copy.start()
    for b in range(rows):
        fetch(b, first).start()
    acc_ref[...] = jnp.zeros_like(acc_ref)
    counts_copy.wait()
    cols_copy.wait()
    for b in range(rows):
        for part in others:

            @pl.when(counts_ref[b] > part.start)
            def _(b=b, part=part):
                fetch(b, part).start()

    def add(b, part):
        fetch(b, part).wait()
        for slot in part:
            col = jnp.where(slot < counts_ref[b], cols_ref[b, slot], groups)
            block = held_ref[b, slot].astype(jnp.float32)
            acc_ref[col] += jnp.sum(block.reshape(size // 8, 8, size), axis=0)

    for b in range(rows):
        add(b, first)
    for b in range(rows):
        for part in others:

            @pl.when(counts_ref[b] > part.start)
            def _(b=b, part=part):
                add(b, part)

    sums_ref[...] = jnp.sum(acc_ref[:groups], axis=1)


def multiply_rows(rows, counts_ref, slots, start, gather, acc_ref):
    first, *others = slot_ranges(slots)

    def product(row, part):
        left, right = zip(*[gather(row, slot) for slot in part])
        return jnp.dot(jnp.concatenate(left, axis=1), jnp.concatenate(right, axis=0), preferred_element_type=jnp.float32)

    for b, row in enumerate(rows):
        acc_ref[b] = start(b) + product(row, first)
    for b, row in enumerate(rows):
        for part in others:

            @pl.when(counts_ref[row] > part.start)
            def _(b=b, row=row, part=part):
                acc_ref[b] += product(row, part)


def first_kernel(sending, cols_ref, counts_ref, sums_ref, added_ref, demand_ref, blocks_ref, out_ref, coef_ref, inverse_ref, acc_ref):
    slots, size = blocks_ref.shape[1:3]
    count = out_ref.shape[0]
    base = 0
    if sending is not None:
        side = lax.axis_index("col")
        base = (1 - side if sending else side) * count
    inverse_ref[...] = (1.0 / (sums_ref[...] + added_ref[...]))[:, None, :]

    def gather(row, slot):
        col = cols_ref[row, slot]
        scale = jnp.where(slot < counts_ref[row], inverse_ref[col], 0.0)
        scale = jnp.broadcast_to(scale, (16, size)).astype(jnp.bfloat16)
        coef = (blocks_ref[row, slot].reshape(size // 16, 16, size) * scale).reshape(size, size)
        coef_ref[row, slot] = coef
        return coef, demand_ref[col]

    rows = [base + b for b in range(count)]
    multiply_rows(rows, counts_ref, slots, lambda b: 0.0, gather, acc_ref)
    out_ref[...] = acc_ref[...].astype(out_ref.dtype)


def second_rows(first_row, place, cols_ref, counts_ref, coef_ref, source_ref, start, out_ref, acc_ref):
    slots = coef_ref.shape[1]

    def gather(row, slot):
        return coef_ref[row, slot], source_ref[place(cols_ref[row, slot])]

    rows = [first_row + b for b in range(out_ref.shape[0])]
    multiply_rows(rows, counts_ref, slots, start, gather, acc_ref)
    out_ref[...] = acc_ref[...].astype(out_ref.dtype)


def exact_scale(count, part):
    scale = -(-(1 << 16) // part)
    assert all((i * scale) >> 16 == i // part for i in range(count))
    return scale


GATHERED = (
    ((0, 0, 0), (1, 0, 0), (1, 1, 0), (0, 1, 0)),
    ((0, 0, 1), (0, 1, 1), (1, 0, 1), (1, 1, 1)),
)


def second_part_kernel(which, cols_ref, counts_ref, coef_ref, own_ref, *rest):
    part = own_ref.shape[0]
    if which == 0:
        pieces, (out_ref, source_ref, acc_ref) = rest[:-3], rest[-3:]
        for number, array in enumerate(pieces):
            core = number // len(GATHERED)
            for i, (z, y, away) in enumerate(GATHERED[number % len(GATHERED)]):
                at = ((z * 4 + y * 2 + core) * 2 + away) * part
                source_ref[at : at + part] = array[i * part : (i + 1) * part]
    else:
        source_ref, out_ref, acc_ref = rest
    side = lax.axis_index("col")
    near = lax.rem(lax.axis_index("row"), 8) * 2 + side
    scale = exact_scale(source_ref.shape[0], part)

    def place(col):
        piece = lax.shift_right_logical(col * scale, 16)
        return col + part * ((piece ^ near) - piece)

    def start(b):
        return jnp.where(side == which, own_ref[b].astype(jnp.float32), 0.0)

    second_rows(which * part, place, cols_ref, counts_ref, coef_ref, source_ref, start, out_ref, acc_ref)


def second_kernel(cols_ref, counts_ref, coef_ref, own_ref, source_ref, out_ref, acc_ref):
    first = lax.axis_index("col") == 0

    def start(b):
        return jnp.where(first, own_ref[b].astype(jnp.float32), 0.0)

    second_rows(0, lambda col: col, cols_ref, counts_ref, coef_ref, source_ref, start, out_ref, acc_ref)


def choose_kernel(own_ref, crossed_ref, home_ref, away_ref):
    owner = lax.div(lax.axis_index("row"), 8) == lax.axis_index("col")

    @pl.when(owner)
    def _():
        home_ref[...] = own_ref[...]
        away_ref[...] = crossed_ref[...]

    @pl.when(jnp.logical_not(owner))
    def _():
        home_ref[...] = crossed_ref[...]
        away_ref[...] = own_ref[...]


def join_kernel(*refs):
    pieces, joined_ref = refs[:-1], refs[-1]
    part = pieces[0].shape[0]
    for i, piece in enumerate(pieces):
        joined_ref[i * part : (i + 1) * part] = piece[...]


def result_kernel(first_row, mine_ref, other_ref, *rest):
    out_ref, sum_ref, sem = rest[-3:]
    sum_ref[...] = (mine_ref[...].astype(jnp.float32) + other_ref[...].astype(jnp.float32)).astype(sum_ref.dtype)
    copy = pltpu.make_async_copy(sum_ref, out_ref.at[pl.ds(first_row, sum_ref.shape[0])], sem)
    copy.start()
    copy.wait()


SMEM = pl.BlockSpec(memory_space=pltpu.SMEM)
VMEM = pl.BlockSpec(memory_space=pltpu.VMEM)
PARAMS = pltpu.CompilerParams(vmem_limit_bytes=VMEM_LIMIT)


def cost(flops, bytes_accessed):
    return pl.CostEstimate(flops=flops, bytes_accessed=bytes_accessed, transcendentals=0)


def in_vmem(array):
    return pltpu.with_memory_space_constraint(array, pltpu.VMEM)


def body(n_row, n_col, blocks, slot_cols, counts, demand, value_added):
    rows, slots, size, _ = blocks.shape
    width = demand.shape[1]
    groups = demand.shape[0] // size
    group_devices = n_row // n_col
    paired = n_col == 2 and n_row == 16 and rows % 2 == 0
    half = rows // 2
    counts = counts.reshape(rows)

    sums, held = pl.pallas_call(
        sums_kernel,
        name="column_sums",
        out_shape=(
            jax.ShapeDtypeStruct((groups, size), jnp.float32),
            pltpu.VMEM(blocks.shape, blocks.dtype),
        ),
        in_specs=[pl.BlockSpec(memory_space=pltpu.HBM)] * 3,
        out_specs=(VMEM, VMEM),
        scratch_shapes=[
            pltpu.VMEM((groups + 1, 8, size), jnp.float32),
            pltpu.SMEM(slot_cols.shape, jnp.int32),
            pltpu.SMEM(counts.shape, jnp.int32),
            pltpu.SemaphoreType.DMA((2,)),
            pltpu.SemaphoreType.DMA((rows, 2)),
        ],
        compiler_params=PARAMS,
        cost_estimate=cost(0, 4 * rows * size * size * slots),
    )(*[pltpu.with_memory_space_constraint(array, pltpu.HBM) for array in (slot_cols, counts, blocks)])

    def flip(array, mask):
        return lax.ppermute(array, "row", [(i, i ^ mask) for i in range(n_row)])

    def swap(array):
        return lax.ppermute(array, "col", [(0, 1), (1, 0)])

    if paired:
        for masks in ((1, 2, 3), (4, 8, 12)):
            sums = sums.astype(jnp.bfloat16)
            parts = [sums] + [flip(sums, m) for m in masks]
            sums = functools.reduce(jnp.add, [part.astype(jnp.float32) for part in parts])
    else:
        sums = lax.psum(sums, "row")

    def layer_cost(count):
        return cost(2 * count * slots * size * size * width, count * slots * size * size * 2)

    def first_layer(sending, count, dtype, held):
        return pl.pallas_call(
            functools.partial(first_kernel, sending),
            name="first_layer",
            out_shape=(
                jax.ShapeDtypeStruct((count, size, width), dtype),
                pltpu.VMEM(blocks.shape, blocks.dtype),
            ),
            in_specs=[SMEM, SMEM, VMEM, VMEM, VMEM, VMEM],
            out_specs=(VMEM, VMEM),
            scratch_shapes=[
                pltpu.VMEM((groups, 1, size), jnp.float32),
                pltpu.VMEM((count, size, width), jnp.float32),
            ],
            input_output_aliases={5: 1},
            compiler_params=PARAMS,
            cost_estimate=layer_cost(count),
        )(
            slot_cols,
            counts,
            sums,
            value_added.reshape(groups, size),
            demand.reshape(groups, size, width),
            in_vmem(held),
        )

    def second_call(kernel, count, coefs, own, sources, keep_sources):
        dtype = jnp.bfloat16 if paired else jnp.float32
        out = jax.ShapeDtypeStruct((count, size, width), dtype)
        return pl.pallas_call(
            kernel,
            name="second_layer",
            out_shape=(out, jax.ShapeDtypeStruct((groups, size, width), jnp.bfloat16)) if keep_sources else out,
            in_specs=[SMEM, SMEM] + [VMEM] * (2 + len(sources)),
            out_specs=(VMEM, VMEM) if keep_sources else VMEM,
            scratch_shapes=[pltpu.VMEM((count, size, width), jnp.float32)],
            compiler_params=PARAMS,
            cost_estimate=layer_cost(count),
        )(slot_cols, counts, in_vmem(coefs), own, *sources)

    if not paired:
        group = lax.axis_index("col")
        partial, coefs = first_layer(None, rows, jnp.float32, held)
        layer_one = lax.psum(partial, "col").astype(jnp.bfloat16)
        gathered = lax.all_gather(layer_one, "row", axis=0, tiled=True)
        source = lax.dynamic_slice_in_dim(gathered, group * groups, groups, 0)
        partial = second_call(second_kernel, rows, coefs, layer_one, [source], False)
        return lax.psum(partial, "col").astype(jnp.bfloat16).reshape(rows * size, width)

    sent, coefs = first_layer(True, half, jnp.bfloat16, held)
    arrived = swap(sent)
    kept, coefs = first_layer(False, half, jnp.float32, coefs)
    own = (kept + arrived.astype(jnp.float32)).astype(jnp.bfloat16)

    piece = jax.ShapeDtypeStruct(own.shape, own.dtype)
    home, away = pl.pallas_call(
        choose_kernel,
        name="home_and_away",
        out_shape=(piece, piece),
        in_specs=[VMEM] * 2,
        out_specs=(VMEM, VMEM),
        compiler_params=PARAMS,
    )(own, flip(own, group_devices))

    def join(pieces):
        return pl.pallas_call(
            join_kernel,
            name="own_joined",
            out_shape=jax.ShapeDtypeStruct((len(pieces) * half, size, width), own.dtype),
            in_specs=[VMEM] * len(pieces),
            out_specs=VMEM,
            compiler_params=PARAMS,
        )(*pieces)

    away = swap(away)
    near_home = join([home, flip(home, 4), flip(home, 6), flip(home, 2)])
    near_away = join([away, flip(away, 2), flip(away, 4), flip(away, 6)])
    gathered = [near_home, near_away]
    pieces = gathered + [flip(part, 1) for part in gathered]

    part_a, source = second_call(functools.partial(second_part_kernel, 0), half, coefs, own, pieces, True)
    other_a = swap(part_a)
    part_b = second_call(functools.partial(second_part_kernel, 1), half, coefs, own, [source], False)
    other_b = swap(part_b)

    def result(first_row, inputs):
        return pl.pallas_call(
            functools.partial(result_kernel, first_row),
            name="result",
            out_shape=jax.ShapeDtypeStruct((rows, size, width), jnp.bfloat16),
            in_specs=[VMEM, VMEM] + [pl.BlockSpec(memory_space=pltpu.HBM)] * (len(inputs) - 2),
            out_specs=pl.BlockSpec(memory_space=pltpu.HBM),
            scratch_shapes=[pltpu.VMEM(piece.shape, piece.dtype), pltpu.SemaphoreType.DMA],
            input_output_aliases={2: 0} if len(inputs) > 2 else {},
            compiler_params=PARAMS,
        )(*inputs)

    out = result(0, [part_a, other_a])
    return result(half, [part_b, other_b, out]).reshape(rows * size, width)


def solution(mesh):
    return jax.shard_map(
        functools.partial(body, mesh.shape["row"], mesh.shape["col"]),
        mesh=mesh,
        in_specs=(
            P("row", "col", None, None),
            P("row", "col"),
            P("row", "col"),
            P("col", None),
            P("col"),
        ),
        out_specs=P("row", None),
        check_vma=False,
    )
```

```python
import functools

import jax
import jax.numpy as jnp
from jax import lax
from jax.experimental import pallas as pl
from jax.experimental.pallas import tpu as pltpu
from jax.sharding import PartitionSpec as P

VMEM_LIMIT = 12 * 1024 * 1024


def slot_ranges(slots):
    first = min(12, slots)
    return [range(first)] + ([range(first, slots)] if slots > first else [])


def sums_kernel(cols_hbm, counts_hbm, blocks_ref, sums_ref, held_ref, acc_ref, cols_ref, counts_ref, list_sems, sems):
    rows, slots, size, _ = blocks_ref.shape
    groups = acc_ref.shape[0] - 1
    first, *others = slot_ranges(slots)

    def fetch(b, part):
        span = pl.ds(part.start, len(part))
        return pltpu.make_async_copy(blocks_ref.at[b, span], held_ref.at[b, span], sems.at[b, min(part.start, 1)])

    counts_copy = pltpu.make_async_copy(counts_hbm, counts_ref, list_sems.at[0])
    cols_copy = pltpu.make_async_copy(cols_hbm, cols_ref, list_sems.at[1])
    counts_copy.start()
    cols_copy.start()
    for b in range(rows):
        fetch(b, first).start()
    acc_ref[...] = jnp.zeros_like(acc_ref)
    counts_copy.wait()
    cols_copy.wait()
    for b in range(rows):
        for part in others:

            @pl.when(counts_ref[b] > part.start)
            def _(b=b, part=part):
                fetch(b, part).start()

    def add(b, part):
        fetch(b, part).wait()
        for slot in part:
            col = jnp.where(slot < counts_ref[b], cols_ref[b, slot], groups)
            block = held_ref[b, slot].astype(jnp.float32)
            acc_ref[col] += jnp.sum(block.reshape(size // 8, 8, size), axis=0)

    for b in range(rows):
        add(b, first)
    for b in range(rows):
        for part in others:

            @pl.when(counts_ref[b] > part.start)
            def _(b=b, part=part):
                add(b, part)

    sums = jnp.sum(acc_ref[:groups], axis=1).astype(sums_ref.dtype)
    sums_ref[...] = jnp.broadcast_to(sums, sums_ref.shape)


def add_kernel(parts_ref, out_ref):
    sums = sum(parts_ref[i].astype(jnp.float32) for i in range(parts_ref.shape[0]))
    out_ref[...] = jnp.broadcast_to(sums.astype(out_ref.dtype), out_ref.shape)


def multiply_rows(rows, counts_ref, slots, start, gather, acc_ref):
    first, *others = slot_ranges(slots)

    def product(row, part):
        left, right = zip(*[gather(row, slot) for slot in part])
        return jnp.dot(jnp.concatenate(left, axis=1), jnp.concatenate(right, axis=0), preferred_element_type=jnp.float32)

    for b, row in enumerate(rows):
        acc_ref[b] = start(b) + product(row, first)
    for b, row in enumerate(rows):
        for part in others:

            @pl.when(counts_ref[row] > part.start)
            def _(b=b, row=row, part=part):
                acc_ref[b] += product(row, part)


def first_kernel(sending, cols_ref, counts_ref, sums_ref, added_ref, demand_ref, blocks_ref, out_ref, coef_ref, inverse_ref, acc_ref):
    slots, size = blocks_ref.shape[1:3]
    count = out_ref.shape[0]
    base = 0
    if sending is not None:
        side = lax.axis_index("col")
        base = (1 - side if sending else side) * count
    totals = added_ref[...]
    for i in range(sums_ref.shape[0]):
        totals = totals + sums_ref[i].astype(jnp.float32)
    inverse_ref[...] = (1.0 / totals)[:, None, :]

    def gather(row, slot):
        col = cols_ref[row, slot]
        scale = jnp.where(slot < counts_ref[row], inverse_ref[col], 0.0)
        scale = jnp.broadcast_to(scale, (16, size)).astype(jnp.bfloat16)
        coef = (blocks_ref[row, slot].reshape(size // 16, 16, size) * scale).reshape(size, size)
        coef_ref[row, slot] = coef
        return coef, demand_ref[col]

    rows = [base + b for b in range(count)]
    multiply_rows(rows, counts_ref, slots, lambda b: 0.0, gather, acc_ref)
    out_ref[...] = acc_ref[...].astype(out_ref.dtype)


def second_rows(first_row, place, cols_ref, counts_ref, coef_ref, source_ref, start, out_ref, acc_ref):
    slots = coef_ref.shape[1]

    def gather(row, slot):
        return coef_ref[row, slot], source_ref[place(cols_ref[row, slot])]

    rows = [first_row + b for b in range(out_ref.shape[0])]
    multiply_rows(rows, counts_ref, slots, start, gather, acc_ref)
    out_ref[...] = acc_ref[...].astype(out_ref.dtype)


def exact_scale(count, part):
    scale = -(-(1 << 16) // part)
    assert all((i * scale) >> 16 == i // part for i in range(count))
    return scale


GATHERED = (
    ((0, 0, 0), (0, 1, 0), (1, 0, 0), (1, 1, 0)),
    ((0, 0, 1), (0, 1, 1), (1, 0, 1), (1, 1, 1)),
)


def second_part_kernel(which, cols_ref, counts_ref, coef_ref, own_ref, *rest):
    part = own_ref.shape[0]
    if which == 0:
        pieces, (out_ref, source_ref, acc_ref) = rest[:-3], rest[-3:]
        for number, array in enumerate(pieces):
            core = number // len(GATHERED)
            for i, (z, y, away) in enumerate(GATHERED[number % len(GATHERED)]):
                at = ((z * 4 + y * 2 + core) * 2 + away) * part
                source_ref[at : at + part] = array[i * part : (i + 1) * part]
    else:
        source_ref, out_ref, acc_ref = rest
    side = lax.axis_index("col")
    near = lax.rem(lax.axis_index("row"), 8) * 2 + side
    scale = exact_scale(source_ref.shape[0], part)

    def place(col):
        piece = lax.shift_right_logical(col * scale, 16)
        return col + part * ((piece ^ near) - piece)

    def start(b):
        return jnp.where(side == which, own_ref[b].astype(jnp.float32), 0.0)

    second_rows(which * part, place, cols_ref, counts_ref, coef_ref, source_ref, start, out_ref, acc_ref)


def second_kernel(cols_ref, counts_ref, coef_ref, own_ref, source_ref, out_ref, acc_ref):
    first = lax.axis_index("col") == 0

    def start(b):
        return jnp.where(first, own_ref[b].astype(jnp.float32), 0.0)

    second_rows(0, lambda col: col, cols_ref, counts_ref, coef_ref, source_ref, start, out_ref, acc_ref)


def choose_kernel(own_ref, crossed_ref, home_ref, away_ref):
    owner = lax.div(lax.axis_index("row"), 8) == lax.axis_index("col")

    @pl.when(owner)
    def _():
        home_ref[...] = own_ref[...]
        away_ref[...] = crossed_ref[...]

    @pl.when(jnp.logical_not(owner))
    def _():
        home_ref[...] = crossed_ref[...]
        away_ref[...] = own_ref[...]


def join_kernel(*refs):
    pieces, joined_ref = refs[:-1], refs[-1]
    part = pieces[0].shape[0]
    for i, piece in enumerate(pieces):
        joined_ref[i * part : (i + 1) * part] = piece[...]


def result_kernel(first_row, mine_ref, other_ref, *rest):
    out_ref, sum_ref, sem = rest[-3:]
    sum_ref[...] = (mine_ref[...].astype(jnp.float32) + other_ref[...].astype(jnp.float32)).astype(sum_ref.dtype)
    copy = pltpu.make_async_copy(sum_ref, out_ref.at[pl.ds(first_row, sum_ref.shape[0])], sem)
    copy.start()
    copy.wait()


SMEM = pl.BlockSpec(memory_space=pltpu.SMEM)
VMEM = pl.BlockSpec(memory_space=pltpu.VMEM)
PARAMS = pltpu.CompilerParams(vmem_limit_bytes=VMEM_LIMIT)


def cost(flops, bytes_accessed):
    return pl.CostEstimate(flops=flops, bytes_accessed=bytes_accessed, transcendentals=0)


def in_vmem(array):
    return pltpu.with_memory_space_constraint(array, pltpu.VMEM)


def body(n_row, n_col, blocks, slot_cols, counts, demand, value_added):
    rows, slots, size, _ = blocks.shape
    width = demand.shape[1]
    groups = demand.shape[0] // size
    group_devices = n_row // n_col
    paired = n_col == 2 and n_row == 16 and rows % 2 == 0
    half = rows // 2
    counts = counts.reshape(rows)

    sums, held = pl.pallas_call(
        sums_kernel,
        name="column_sums",
        out_shape=(
            jax.ShapeDtypeStruct((4, groups, size) if paired else (groups, size), jnp.bfloat16 if paired else jnp.float32),
            pltpu.VMEM(blocks.shape, blocks.dtype),
        ),
        in_specs=[pl.BlockSpec(memory_space=pltpu.HBM)] * 3,
        out_specs=(VMEM, VMEM),
        scratch_shapes=[
            pltpu.VMEM((groups + 1, 8, size), jnp.float32),
            pltpu.SMEM(slot_cols.shape, jnp.int32),
            pltpu.SMEM(counts.shape, jnp.int32),
            pltpu.SemaphoreType.DMA((2,)),
            pltpu.SemaphoreType.DMA((rows, 2)),
        ],
        compiler_params=PARAMS,
        cost_estimate=cost(0, 4 * rows * size * size * slots),
    )(*[pltpu.with_memory_space_constraint(array, pltpu.HBM) for array in (slot_cols, counts, blocks)])

    def flip(array, mask):
        return lax.ppermute(array, "row", [(i, i ^ mask) for i in range(n_row)])

    def swap(array):
        return lax.ppermute(array, "col", [(0, 1), (1, 0)])

    if paired:
        squares = [[i * 4 + j for j in range(4)] for i in range(4)]
        lines = [[i + j * 4 for j in range(4)] for i in range(4)]
        sums = lax.all_to_all(sums, "row", 0, 0, axis_index_groups=squares)
        sums = pl.pallas_call(
            add_kernel,
            name="own_sums",
            out_shape=jax.ShapeDtypeStruct(sums.shape, sums.dtype),
            in_specs=[VMEM],
            out_specs=VMEM,
            compiler_params=PARAMS,
        )(sums)
        sums = lax.all_to_all(sums, "row", 0, 0, axis_index_groups=lines)
    else:
        sums = lax.psum(sums, "row")[None]

    def layer_cost(count):
        return cost(2 * count * slots * size * size * width, count * slots * size * size * 2)

    def first_layer(sending, count, dtype, held):
        return pl.pallas_call(
            functools.partial(first_kernel, sending),
            name="first_layer",
            out_shape=(
                jax.ShapeDtypeStruct((count, size, width), dtype),
                pltpu.VMEM(blocks.shape, blocks.dtype),
            ),
            in_specs=[SMEM, SMEM, VMEM, VMEM, VMEM, VMEM],
            out_specs=(VMEM, VMEM),
            scratch_shapes=[
                pltpu.VMEM((groups, 1, size), jnp.float32),
                pltpu.VMEM((count, size, width), jnp.float32),
            ],
            input_output_aliases={5: 1},
            compiler_params=PARAMS,
            cost_estimate=layer_cost(count),
        )(
            slot_cols,
            counts,
            sums,
            value_added.reshape(groups, size),
            demand.reshape(groups, size, width),
            in_vmem(held),
        )

    def second_call(kernel, count, coefs, own, sources, keep_sources):
        dtype = jnp.bfloat16 if paired else jnp.float32
        out = jax.ShapeDtypeStruct((count, size, width), dtype)
        return pl.pallas_call(
            kernel,
            name="second_layer",
            out_shape=(out, jax.ShapeDtypeStruct((groups, size, width), jnp.bfloat16)) if keep_sources else out,
            in_specs=[SMEM, SMEM] + [VMEM] * (2 + len(sources)),
            out_specs=(VMEM, VMEM) if keep_sources else VMEM,
            scratch_shapes=[pltpu.VMEM((count, size, width), jnp.float32)],
            compiler_params=PARAMS,
            cost_estimate=layer_cost(count),
        )(slot_cols, counts, in_vmem(coefs), own, *sources)

    if not paired:
        group = lax.axis_index("col")
        partial, coefs = first_layer(None, rows, jnp.float32, held)
        layer_one = lax.psum(partial, "col").astype(jnp.bfloat16)
        gathered = lax.all_gather(layer_one, "row", axis=0, tiled=True)
        source = lax.dynamic_slice_in_dim(gathered, group * groups, groups, 0)
        partial = second_call(second_kernel, rows, coefs, layer_one, [source], False)
        return lax.psum(partial, "col").astype(jnp.bfloat16).reshape(rows * size, width)

    sent, coefs = first_layer(True, half, jnp.bfloat16, held)
    arrived = swap(sent)
    kept, coefs = first_layer(False, half, jnp.float32, coefs)
    own = (kept + arrived.astype(jnp.float32)).astype(jnp.bfloat16)

    piece = jax.ShapeDtypeStruct(own.shape, own.dtype)
    home, away = pl.pallas_call(
        choose_kernel,
        name="home_and_away",
        out_shape=(piece, piece),
        in_specs=[VMEM] * 2,
        out_specs=(VMEM, VMEM),
        compiler_params=PARAMS,
    )(own, flip(own, group_devices))

    def join(pieces):
        return pl.pallas_call(
            join_kernel,
            name="own_joined",
            out_shape=jax.ShapeDtypeStruct((len(pieces) * half, size, width), own.dtype),
            in_specs=[VMEM] * len(pieces),
            out_specs=VMEM,
            compiler_params=PARAMS,
        )(*pieces)

    away = swap(away)
    gathered = [join([part] + [flip(part, mask) for mask in (2, 4, 6)]) for part in (home, away)]
    pieces = gathered + [flip(part, 1) for part in gathered]

    part_a, source = second_call(functools.partial(second_part_kernel, 0), half, coefs, own, pieces, True)
    other_a = swap(part_a)
    part_b = second_call(functools.partial(second_part_kernel, 1), half, coefs, own, [source], False)
    other_b = swap(part_b)

    def result(first_row, inputs):
        return pl.pallas_call(
            functools.partial(result_kernel, first_row),
            name="result",
            out_shape=jax.ShapeDtypeStruct((rows, size, width), jnp.bfloat16),
            in_specs=[VMEM, VMEM] + [pl.BlockSpec(memory_space=pltpu.HBM)] * (len(inputs) - 2),
            out_specs=pl.BlockSpec(memory_space=pltpu.HBM),
            scratch_shapes=[pltpu.VMEM(piece.shape, piece.dtype), pltpu.SemaphoreType.DMA],
            input_output_aliases={2: 0} if len(inputs) > 2 else {},
            compiler_params=PARAMS,
        )(*inputs)

    out = result(0, [part_a, other_a])
    return result(half, [part_b, other_b, out]).reshape(rows * size, width)


def solution(mesh):
    return jax.shard_map(
        functools.partial(body, mesh.shape["row"], mesh.shape["col"]),
        mesh=mesh,
        in_specs=(
            P("row", "col", None, None),
            P("row", "col"),
            P("row", "col"),
            P("col", None),
            P("col"),
        ),
        out_specs=P("row", None),
        check_vma=False,
    )
```

```python
import functools

import jax
import jax.numpy as jnp
from jax import lax
from jax.experimental import pallas as pl
from jax.experimental.pallas import tpu as pltpu
from jax.sharding import PartitionSpec as P

VMEM_LIMIT = 12 * 1024 * 1024


def slot_ranges(slots):
    first = min(12, slots)
    return [range(first)] + ([range(first, slots)] if slots > first else [])


def sums_kernel(cols_hbm, counts_hbm, blocks_ref, sums_ref, held_ref, acc_ref, cols_ref, counts_ref, list_sems, sems):
    rows, slots, size, _ = blocks_ref.shape
    groups = acc_ref.shape[0] - 1
    first, *others = slot_ranges(slots)

    def fetch(b, part):
        span = pl.ds(part.start, len(part))
        return pltpu.make_async_copy(blocks_ref.at[b, span], held_ref.at[b, span], sems.at[b, min(part.start, 1)])

    counts_copy = pltpu.make_async_copy(counts_hbm, counts_ref, list_sems.at[0])
    cols_copy = pltpu.make_async_copy(cols_hbm, cols_ref, list_sems.at[1])
    counts_copy.start()
    cols_copy.start()
    for b in range(rows):
        fetch(b, first).start()
    acc_ref[...] = jnp.zeros_like(acc_ref)
    counts_copy.wait()
    cols_copy.wait()
    for b in range(rows):
        for part in others:

            @pl.when(counts_ref[b] > part.start)
            def _(b=b, part=part):
                fetch(b, part).start()

    def add(b, part):
        fetch(b, part).wait()
        for slot in part:
            col = jnp.where(slot < counts_ref[b], cols_ref[b, slot], groups)
            block = held_ref[b, slot]
            for _ in range(2):
                middle = block.shape[0] // 2
                block = block[:middle] + block[middle:]
            block = block.astype(jnp.float32).reshape(block.shape[0] // 8, 8, size)
            acc_ref[col] += jnp.sum(block, axis=0)

    for b in range(rows):
        add(b, first)
    for b in range(rows):
        for part in others:

            @pl.when(counts_ref[b] > part.start)
            def _(b=b, part=part):
                add(b, part)

    sums_ref[...] = jnp.sum(acc_ref[:groups], axis=1)


def multiply_rows(rows, counts_ref, slots, start, gather, acc_ref):
    first, *others = slot_ranges(slots)

    def product(row, part):
        left, right = zip(*[gather(row, slot) for slot in part])
        return jnp.dot(jnp.concatenate(left, axis=1), jnp.concatenate(right, axis=0), preferred_element_type=jnp.float32)

    for b, row in enumerate(rows):
        acc_ref[b] = start(b) + product(row, first)
    for b, row in enumerate(rows):
        for part in others:

            @pl.when(counts_ref[row] > part.start)
            def _(b=b, row=row, part=part):
                acc_ref[b] += product(row, part)


def first_kernel(sending, cols_ref, counts_ref, sums_ref, added_ref, demand_ref, blocks_ref, out_ref, coef_ref, inverse_ref, acc_ref):
    slots, size = blocks_ref.shape[1:3]
    count = out_ref.shape[0]
    base = 0
    if sending is not None:
        side = lax.axis_index("col")
        base = (1 - side if sending else side) * count
    inverse_ref[...] = (1.0 / (sums_ref[...] + added_ref[...]))[:, None, :]

    def gather(row, slot):
        col = cols_ref[row, slot]
        scale = jnp.where(slot < counts_ref[row], inverse_ref[col], 0.0)
        scale = jnp.broadcast_to(scale, (16, size)).astype(jnp.bfloat16)
        coef = (blocks_ref[row, slot].reshape(size // 16, 16, size) * scale).reshape(size, size)
        coef_ref[row, slot] = coef
        return coef, demand_ref[col]

    rows = [base + b for b in range(count)]
    multiply_rows(rows, counts_ref, slots, lambda b: 0.0, gather, acc_ref)
    out_ref[...] = acc_ref[...].astype(out_ref.dtype)


def second_rows(first_row, place, cols_ref, counts_ref, coef_ref, source_ref, start, out_ref, acc_ref):
    slots = coef_ref.shape[1]

    def gather(row, slot):
        return coef_ref[row, slot], source_ref[place(cols_ref[row, slot])]

    rows = [first_row + b for b in range(out_ref.shape[0])]
    multiply_rows(rows, counts_ref, slots, start, gather, acc_ref)
    out_ref[...] = acc_ref[...].astype(out_ref.dtype)


def exact_scale(count, part):
    scale = -(-(1 << 16) // part)
    assert all((i * scale) >> 16 == i // part for i in range(count))
    return scale


HOME = ((0, 0, 0), (0, 1, 0), (1, 0, 0), (1, 1, 0))
AWAY = ((0, 0, 1), (0, 1, 1), (1, 0, 1), (1, 1, 1))


def collect(array, places, core, source_ref):
    part = array.shape[0] // len(places)
    for i, (z, y, away) in enumerate(places):
        at = ((z * 4 + y * 2 + core) * 2 + away) * part
        source_ref[at : at + part] = array[i * part : (i + 1) * part]


def collect_kernel(home_ref, away_ref, home_core_ref, source_ref):
    collect(home_ref, HOME, 0, source_ref)
    collect(away_ref, AWAY, 0, source_ref)
    collect(home_core_ref, HOME, 1, source_ref)


def second_part_kernel(which, cols_ref, counts_ref, coef_ref, own_ref, *rest):
    part = own_ref.shape[0]
    if which == 0:
        _, away_core_ref, out_ref, source_ref, acc_ref = rest
        collect(away_core_ref, AWAY, 1, source_ref)
    else:
        source_ref, out_ref, acc_ref = rest
    side = lax.axis_index("col")
    near = lax.rem(lax.axis_index("row"), 8) * 2 + side
    scale = exact_scale(source_ref.shape[0], part)

    def place(col):
        piece = lax.shift_right_logical(col * scale, 16)
        return col + part * ((piece ^ near) - piece)

    def start(b):
        return jnp.where(side == which, own_ref[b].astype(jnp.float32), 0.0)

    second_rows(which * part, place, cols_ref, counts_ref, coef_ref, source_ref, start, out_ref, acc_ref)


def second_kernel(cols_ref, counts_ref, coef_ref, own_ref, source_ref, out_ref, acc_ref):
    first = lax.axis_index("col") == 0

    def start(b):
        return jnp.where(first, own_ref[b].astype(jnp.float32), 0.0)

    second_rows(0, lambda col: col, cols_ref, counts_ref, coef_ref, source_ref, start, out_ref, acc_ref)


def choose_kernel(own_ref, crossed_ref, home_ref, away_ref):
    owner = lax.div(lax.axis_index("row"), 8) == lax.axis_index("col")

    @pl.when(owner)
    def _():
        home_ref[...] = own_ref[...]
        away_ref[...] = crossed_ref[...]

    @pl.when(jnp.logical_not(owner))
    def _():
        home_ref[...] = crossed_ref[...]
        away_ref[...] = own_ref[...]


def join_kernel(*refs):
    pieces, joined_ref = refs[:-1], refs[-1]
    part = pieces[0].shape[0]
    for i, piece in enumerate(pieces):
        joined_ref[i * part : (i + 1) * part] = piece[...]


def result_kernel(first_row, mine_ref, other_ref, *rest):
    out_ref, sum_ref, sem = rest[-3:]
    sum_ref[...] = (mine_ref[...].astype(jnp.float32) + other_ref[...].astype(jnp.float32)).astype(sum_ref.dtype)
    copy = pltpu.make_async_copy(sum_ref, out_ref.at[pl.ds(first_row, sum_ref.shape[0])], sem)
    copy.start()
    copy.wait()


SMEM = pl.BlockSpec(memory_space=pltpu.SMEM)
VMEM = pl.BlockSpec(memory_space=pltpu.VMEM)
PARAMS = pltpu.CompilerParams(vmem_limit_bytes=VMEM_LIMIT)


def cost(flops, bytes_accessed):
    return pl.CostEstimate(flops=flops, bytes_accessed=bytes_accessed, transcendentals=0)


def in_vmem(array):
    return pltpu.with_memory_space_constraint(array, pltpu.VMEM)


def body(n_row, n_col, blocks, slot_cols, counts, demand, value_added):
    rows, slots, size, _ = blocks.shape
    width = demand.shape[1]
    groups = demand.shape[0] // size
    group_devices = n_row // n_col
    paired = n_col == 2 and n_row == 16 and rows % 2 == 0
    half = rows // 2
    counts = counts.reshape(rows)

    sums, held = pl.pallas_call(
        sums_kernel,
        name="column_sums",
        out_shape=(
            jax.ShapeDtypeStruct((groups, size), jnp.float32),
            pltpu.VMEM(blocks.shape, blocks.dtype),
        ),
        in_specs=[pl.BlockSpec(memory_space=pltpu.HBM)] * 3,
        out_specs=(VMEM, VMEM),
        scratch_shapes=[
            pltpu.VMEM((groups + 1, 8, size), jnp.float32),
            pltpu.SMEM(slot_cols.shape, jnp.int32),
            pltpu.SMEM(counts.shape, jnp.int32),
            pltpu.SemaphoreType.DMA((2,)),
            pltpu.SemaphoreType.DMA((rows, 2)),
        ],
        compiler_params=PARAMS,
        cost_estimate=cost(0, 4 * rows * size * size * slots),
    )(*[pltpu.with_memory_space_constraint(array, pltpu.HBM) for array in (slot_cols, counts, blocks)])

    def flip(array, mask):
        return lax.ppermute(array, "row", [(i, i ^ mask) for i in range(n_row)])

    def swap(array):
        return lax.ppermute(array, "col", [(0, 1), (1, 0)])

    if paired:
        for masks in ((1, 2, 3), (4, 8, 12)):
            sums = sums.astype(jnp.bfloat16)
            parts = [sums] + [flip(sums, m) for m in masks]
            sums = functools.reduce(jnp.add, [part.astype(jnp.float32) for part in parts])
    else:
        sums = lax.psum(sums, "row")

    def layer_cost(count):
        return cost(2 * count * slots * size * size * width, count * slots * size * size * 2)

    def first_layer(sending, count, dtype, held):
        return pl.pallas_call(
            functools.partial(first_kernel, sending),
            name="first_layer",
            out_shape=(
                jax.ShapeDtypeStruct((count, size, width), dtype),
                pltpu.VMEM(blocks.shape, blocks.dtype),
            ),
            in_specs=[SMEM, SMEM, VMEM, VMEM, VMEM, VMEM],
            out_specs=(VMEM, VMEM),
            scratch_shapes=[
                pltpu.VMEM((groups, 1, size), jnp.float32),
                pltpu.VMEM((count, size, width), jnp.float32),
            ],
            input_output_aliases={5: 1},
            compiler_params=PARAMS,
            cost_estimate=layer_cost(count),
        )(
            slot_cols,
            counts,
            sums,
            value_added.reshape(groups, size),
            demand.reshape(groups, size, width),
            in_vmem(held),
        )

    def second_call(kernel, count, coefs, own, sources, keep_sources):
        dtype = jnp.bfloat16 if paired else jnp.float32
        out = jax.ShapeDtypeStruct((count, size, width), dtype)
        return pl.pallas_call(
            kernel,
            name="second_layer",
            out_shape=(out, pltpu.VMEM((groups, size, width), jnp.bfloat16)) if keep_sources else out,
            input_output_aliases={4: 1} if keep_sources else {},
            in_specs=[SMEM, SMEM] + [VMEM] * (2 + len(sources)),
            out_specs=(VMEM, VMEM) if keep_sources else VMEM,
            scratch_shapes=[pltpu.VMEM((count, size, width), jnp.float32)],
            compiler_params=PARAMS,
            cost_estimate=layer_cost(count),
        )(slot_cols, counts, in_vmem(coefs), own, *sources)

    if not paired:
        group = lax.axis_index("col")
        partial, coefs = first_layer(None, rows, jnp.float32, held)
        layer_one = lax.psum(partial, "col").astype(jnp.bfloat16)
        gathered = lax.all_gather(layer_one, "row", axis=0, tiled=True)
        source = lax.dynamic_slice_in_dim(gathered, group * groups, groups, 0)
        partial = second_call(second_kernel, rows, coefs, layer_one, [source], False)
        return lax.psum(partial, "col").astype(jnp.bfloat16).reshape(rows * size, width)

    sent, coefs = first_layer(True, half, jnp.bfloat16, held)
    arrived = swap(sent)
    kept, coefs = first_layer(False, half, jnp.float32, coefs)
    own = (kept + arrived.astype(jnp.float32)).astype(jnp.bfloat16)

    piece = jax.ShapeDtypeStruct(own.shape, own.dtype)
    home, away = pl.pallas_call(
        choose_kernel,
        name="home_and_away",
        out_shape=(piece, piece),
        in_specs=[VMEM] * 2,
        out_specs=(VMEM, VMEM),
        compiler_params=PARAMS,
    )(own, flip(own, group_devices))

    def join(pieces):
        return pl.pallas_call(
            join_kernel,
            name="own_joined",
            out_shape=jax.ShapeDtypeStruct((len(pieces) * half, size, width), own.dtype),
            in_specs=[VMEM] * len(pieces),
            out_specs=VMEM,
            compiler_params=PARAMS,
        )(*pieces)

    away = swap(away)
    home, away = [join([part] + [flip(part, mask) for mask in (2, 4, 6)]) for part in (home, away)]
    home_core, away_core = flip(home, 1), flip(away, 1)
    source = pl.pallas_call(
        collect_kernel,
        name="own_collected",
        out_shape=pltpu.VMEM((groups, size, width), jnp.bfloat16),
        in_specs=[VMEM] * 3,
        out_specs=VMEM,
        compiler_params=PARAMS,
        cost_estimate=cost(0, 2 * groups * size * width * 2),
    )(home, away, home_core)

    part_a, source = second_call(
        functools.partial(second_part_kernel, 0), half, coefs, own, [in_vmem(source), away_core], True
    )
    other_a = swap(part_a)
    part_b = second_call(functools.partial(second_part_kernel, 1), half, coefs, own, [in_vmem(source)], False)
    other_b = swap(part_b)

    def result(first_row, inputs):
        return pl.pallas_call(
            functools.partial(result_kernel, first_row),
            name="result",
            out_shape=jax.ShapeDtypeStruct((rows, size, width), jnp.bfloat16),
            in_specs=[VMEM, VMEM] + [pl.BlockSpec(memory_space=pltpu.HBM)] * (len(inputs) - 2),
            out_specs=pl.BlockSpec(memory_space=pltpu.HBM),
            scratch_shapes=[pltpu.VMEM(piece.shape, piece.dtype), pltpu.SemaphoreType.DMA],
            input_output_aliases={2: 0} if len(inputs) > 2 else {},
            compiler_params=PARAMS,
        )(*inputs)

    out = result(0, [part_a, other_a])
    return result(half, [part_b, other_b, out]).reshape(rows * size, width)


def solution(mesh):
    return jax.shard_map(
        functools.partial(body, mesh.shape["row"], mesh.shape["col"]),
        mesh=mesh,
        in_specs=(
            P("row", "col", None, None),
            P("row", "col"),
            P("row", "col"),
            P("col", None),
            P("col"),
        ),
        out_specs=P("row", None),
        check_vma=False,
    )
```

```python
import functools

import jax
import jax.numpy as jnp
from jax import lax
from jax.experimental import pallas as pl
from jax.experimental.pallas import tpu as pltpu
from jax.sharding import PartitionSpec as P

VMEM_LIMIT = 12 * 1024 * 1024


def slot_ranges(slots):
    first = min(12, slots)
    return [range(first)] + ([range(first, slots)] if slots > first else [])


def sums_kernel(cols_hbm, counts_hbm, blocks_ref, sums_ref, held_ref, cols_ref, counts_ref, list_sems, sems, *acc_refs):
    rows, slots, size, _ = blocks_ref.shape
    groups = acc_refs[0].shape[0] - 1
    first, *others = slot_ranges(slots)

    def fetch(b, part):
        span = pl.ds(part.start, len(part))
        return pltpu.make_async_copy(blocks_ref.at[b, span], held_ref.at[b, span], sems.at[b, min(part.start, 1)])

    counts_copy = pltpu.make_async_copy(counts_hbm, counts_ref, list_sems.at[0])
    cols_copy = pltpu.make_async_copy(cols_hbm, cols_ref, list_sems.at[1])
    counts_copy.start()
    cols_copy.start()
    for b in range(rows):
        fetch(b, first).start()
    for acc_ref in acc_refs:
        acc_ref[...] = jnp.zeros_like(acc_ref)
    counts_copy.wait()
    cols_copy.wait()
    for b in range(rows):
        for part in others:

            @pl.when(counts_ref[b] > part.start)
            def _(b=b, part=part):
                fetch(b, part).start()

    def add(b, part):
        fetch(b, part).wait()
        for slot in part:
            col = jnp.where(slot < counts_ref[b], cols_ref[b, slot], groups)
            block = held_ref[b, slot]
            for _ in range(2):
                middle = block.shape[0] // 2
                block = block[:middle] + block[middle:]
            block = block.astype(jnp.float32).reshape(block.shape[0] // 8, 8, size)
            acc_refs[slot % len(acc_refs)][col] += jnp.sum(block, axis=0)

    for b in range(rows):
        add(b, first)
    for b in range(rows):
        for part in others:

            @pl.when(counts_ref[b] > part.start)
            def _(b=b, part=part):
                add(b, part)

    sums_ref[...] = jnp.sum(functools.reduce(jnp.add, [acc_ref[:groups] for acc_ref in acc_refs]), axis=1)


def multiply_rows(rows, counts_ref, slots, start, gather, acc_ref):
    first, *others = slot_ranges(slots)

    def product(row, part):
        left, right = zip(*[gather(row, slot) for slot in part])
        return jnp.dot(jnp.concatenate(left, axis=1), jnp.concatenate(right, axis=0), preferred_element_type=jnp.float32)

    for b, row in enumerate(rows):
        acc_ref[b] = start(b) + product(row, first)
    for b, row in enumerate(rows):
        for part in others:

            @pl.when(counts_ref[row] > part.start)
            def _(b=b, row=row, part=part):
                acc_ref[b] += product(row, part)


def first_kernel(sending, cols_ref, counts_ref, sums_ref, added_ref, demand_ref, blocks_ref, out_ref, coef_ref, inverse_ref, acc_ref):
    slots, size = blocks_ref.shape[1:3]
    count = out_ref.shape[0]
    base = 0
    if sending is not None:
        side = lax.axis_index("col")
        base = (1 - side if sending else side) * count
    inverse_ref[...] = (1.0 / (sums_ref[...] + added_ref[...]))[:, None, :]

    def gather(row, slot):
        col = cols_ref[row, slot]
        scale = jnp.where(slot < counts_ref[row], inverse_ref[col], 0.0)
        scale = jnp.broadcast_to(scale, (16, size)).astype(jnp.bfloat16)
        coef = (blocks_ref[row, slot].reshape(size // 16, 16, size) * scale).reshape(size, size)
        coef_ref[row, slot] = coef
        return coef, demand_ref[col]

    rows = [base + b for b in range(count)]
    multiply_rows(rows, counts_ref, slots, lambda b: 0.0, gather, acc_ref)
    out_ref[...] = acc_ref[...].astype(out_ref.dtype)


def second_rows(first_row, place, cols_ref, counts_ref, coef_ref, source_ref, start, out_ref, acc_ref):
    slots = coef_ref.shape[1]

    def gather(row, slot):
        return coef_ref[row, slot], source_ref[place(cols_ref[row, slot])]

    rows = [first_row + b for b in range(out_ref.shape[0])]
    multiply_rows(rows, counts_ref, slots, start, gather, acc_ref)
    out_ref[...] = acc_ref[...].astype(out_ref.dtype)


def exact_scale(count, part):
    scale = -(-(1 << 16) // part)
    assert all((i * scale) >> 16 == i // part for i in range(count))
    return scale


HOME = ((0, 0, 0), (0, 1, 0), (1, 0, 0), (1, 1, 0))
AWAY = ((0, 0, 1), (0, 1, 1), (1, 0, 1), (1, 1, 1))


def collect(array, places, core, source_ref):
    part = array.shape[0] // len(places)
    for i, (z, y, away) in enumerate(places):
        at = ((z * 4 + y * 2 + core) * 2 + away) * part
        source_ref[at : at + part] = array[i * part : (i + 1) * part]


def collect_kernel(home_ref, away_ref, home_core_ref, source_ref):
    collect(home_ref, HOME, 0, source_ref)
    collect(away_ref, AWAY, 0, source_ref)
    collect(home_core_ref, HOME, 1, source_ref)


def second_part_kernel(which, cols_ref, counts_ref, coef_ref, own_ref, *rest):
    part = own_ref.shape[0]
    if which == 0:
        _, away_core_ref, out_ref, source_ref, acc_ref = rest
        collect(away_core_ref, AWAY, 1, source_ref)
    else:
        source_ref, out_ref, acc_ref = rest
    side = lax.axis_index("col")
    near = lax.rem(lax.axis_index("row"), 8) * 2 + side
    scale = exact_scale(source_ref.shape[0], part)

    def place(col):
        piece = lax.shift_right_logical(col * scale, 16)
        return col + part * ((piece ^ near) - piece)

    def start(b):
        return jnp.where(side == which, own_ref[b].astype(jnp.float32), 0.0)

    second_rows(which * part, place, cols_ref, counts_ref, coef_ref, source_ref, start, out_ref, acc_ref)


def second_kernel(cols_ref, counts_ref, coef_ref, own_ref, source_ref, out_ref, acc_ref):
    first = lax.axis_index("col") == 0

    def start(b):
        return jnp.where(first, own_ref[b].astype(jnp.float32), 0.0)

    second_rows(0, lambda col: col, cols_ref, counts_ref, coef_ref, source_ref, start, out_ref, acc_ref)


def choose_kernel(own_ref, crossed_ref, home_ref, away_ref):
    owner = lax.div(lax.axis_index("row"), 8) == lax.axis_index("col")

    @pl.when(owner)
    def _():
        home_ref[...] = own_ref[...]
        away_ref[...] = crossed_ref[...]

    @pl.when(jnp.logical_not(owner))
    def _():
        home_ref[...] = crossed_ref[...]
        away_ref[...] = own_ref[...]


def join_kernel(*refs):
    pieces, joined_ref = refs[:-1], refs[-1]
    part = pieces[0].shape[0]
    for i, piece in enumerate(pieces):
        joined_ref[i * part : (i + 1) * part] = piece[...]


def result_kernel(first_row, mine_ref, other_ref, *rest):
    out_ref, sum_ref, sem = rest[-3:]
    sum_ref[...] = (mine_ref[...].astype(jnp.float32) + other_ref[...].astype(jnp.float32)).astype(sum_ref.dtype)
    copy = pltpu.make_async_copy(sum_ref, out_ref.at[pl.ds(first_row, sum_ref.shape[0])], sem)
    copy.start()
    copy.wait()


SMEM = pl.BlockSpec(memory_space=pltpu.SMEM)
VMEM = pl.BlockSpec(memory_space=pltpu.VMEM)
PARAMS = pltpu.CompilerParams(vmem_limit_bytes=VMEM_LIMIT)


def cost(flops, bytes_accessed):
    return pl.CostEstimate(flops=flops, bytes_accessed=bytes_accessed, transcendentals=0)


def in_vmem(array):
    return pltpu.with_memory_space_constraint(array, pltpu.VMEM)


def body(n_row, n_col, blocks, slot_cols, counts, demand, value_added):
    rows, slots, size, _ = blocks.shape
    width = demand.shape[1]
    groups = demand.shape[0] // size
    group_devices = n_row // n_col
    paired = n_col == 2 and n_row == 16 and rows % 2 == 0
    half = rows // 2
    counts = counts.reshape(rows)

    sums, held = pl.pallas_call(
        sums_kernel,
        name="column_sums",
        out_shape=(
            jax.ShapeDtypeStruct((groups, size), jnp.float32),
            pltpu.VMEM(blocks.shape, blocks.dtype),
        ),
        in_specs=[pl.BlockSpec(memory_space=pltpu.HBM)] * 3,
        out_specs=(VMEM, VMEM),
        scratch_shapes=[
            pltpu.SMEM(slot_cols.shape, jnp.int32),
            pltpu.SMEM(counts.shape, jnp.int32),
            pltpu.SemaphoreType.DMA((2,)),
            pltpu.SemaphoreType.DMA((rows, 2)),
        ]
        + [pltpu.VMEM((groups + 1, 8, size), jnp.float32)] * 4,
        compiler_params=PARAMS,
        cost_estimate=cost(0, 4 * rows * size * size * slots),
    )(*[pltpu.with_memory_space_constraint(array, pltpu.HBM) for array in (slot_cols, counts, blocks)])

    def flip(array, mask):
        return lax.ppermute(array, "row", [(i, i ^ mask) for i in range(n_row)])

    def swap(array):
        return lax.ppermute(array, "col", [(0, 1), (1, 0)])

    if paired:
        sums = sums + flip(sums.astype(jnp.bfloat16), 1).astype(jnp.float32)
        shared = sums.astype(jnp.bfloat16)
        parts = []
        for masks in ((0, 8), (2, 10), (4, 12), (6, 14)):
            parts.append(lax.ppermute(shared, "row", [(i, i ^ masks[i % 2]) for i in range(n_row)]))
        sums = functools.reduce(jnp.add, [part.astype(jnp.float32) for part in parts])
        sums = sums + flip(sums.astype(jnp.bfloat16), 1).astype(jnp.float32)
    else:
        sums = lax.psum(sums, "row")

    def layer_cost(count):
        return cost(2 * count * slots * size * size * width, count * slots * size * size * 2)

    def first_layer(sending, count, dtype, held):
        return pl.pallas_call(
            functools.partial(first_kernel, sending),
            name="first_layer",
            out_shape=(
                jax.ShapeDtypeStruct((count, size, width), dtype),
                pltpu.VMEM(blocks.shape, blocks.dtype),
            ),
            in_specs=[SMEM, SMEM, VMEM, VMEM, VMEM, VMEM],
            out_specs=(VMEM, VMEM),
            scratch_shapes=[
                pltpu.VMEM((groups, 1, size), jnp.float32),
                pltpu.VMEM((count, size, width), jnp.float32),
            ],
            input_output_aliases={5: 1},
            compiler_params=PARAMS,
            cost_estimate=layer_cost(count),
        )(
            slot_cols,
            counts,
            sums,
            value_added.reshape(groups, size),
            demand.reshape(groups, size, width),
            in_vmem(held),
        )

    def second_call(kernel, count, coefs, own, sources, keep_sources):
        dtype = jnp.bfloat16 if paired else jnp.float32
        out = jax.ShapeDtypeStruct((count, size, width), dtype)
        return pl.pallas_call(
            kernel,
            name="second_layer",
            out_shape=(out, pltpu.VMEM((groups, size, width), jnp.bfloat16)) if keep_sources else out,
            input_output_aliases={4: 1} if keep_sources else {},
            in_specs=[SMEM, SMEM] + [VMEM] * (2 + len(sources)),
            out_specs=(VMEM, VMEM) if keep_sources else VMEM,
            scratch_shapes=[pltpu.VMEM((count, size, width), jnp.float32)],
            compiler_params=PARAMS,
            cost_estimate=layer_cost(count),
        )(slot_cols, counts, in_vmem(coefs), own, *sources)

    if not paired:
        group = lax.axis_index("col")
        partial, coefs = first_layer(None, rows, jnp.float32, held)
        layer_one = lax.psum(partial, "col").astype(jnp.bfloat16)
        gathered = lax.all_gather(layer_one, "row", axis=0, tiled=True)
        source = lax.dynamic_slice_in_dim(gathered, group * groups, groups, 0)
        partial = second_call(second_kernel, rows, coefs, layer_one, [source], False)
        return lax.psum(partial, "col").astype(jnp.bfloat16).reshape(rows * size, width)

    sent, coefs = first_layer(True, half, jnp.bfloat16, held)
    arrived = swap(sent)
    kept, coefs = first_layer(False, half, jnp.float32, coefs)
    own = (kept + arrived.astype(jnp.float32)).astype(jnp.bfloat16)

    piece = jax.ShapeDtypeStruct(own.shape, own.dtype)
    home, away = pl.pallas_call(
        choose_kernel,
        name="home_and_away",
        out_shape=(piece, piece),
        in_specs=[VMEM] * 2,
        out_specs=(VMEM, VMEM),
        compiler_params=PARAMS,
    )(own, flip(own, group_devices))

    def join(pieces):
        return pl.pallas_call(
            join_kernel,
            name="own_joined",
            out_shape=jax.ShapeDtypeStruct((len(pieces) * half, size, width), own.dtype),
            in_specs=[VMEM] * len(pieces),
            out_specs=VMEM,
            compiler_params=PARAMS,
        )(*pieces)

    away = swap(away)
    home, away = [join([part] + [flip(part, mask) for mask in (2, 4, 6)]) for part in (home, away)]
    home_core, away_core = flip(home, 1), flip(away, 1)
    source = pl.pallas_call(
        collect_kernel,
        name="own_collected",
        out_shape=pltpu.VMEM((groups, size, width), jnp.bfloat16),
        in_specs=[VMEM] * 3,
        out_specs=VMEM,
        compiler_params=PARAMS,
        cost_estimate=cost(0, 2 * groups * size * width * 2),
    )(home, away, home_core)

    part_a, source = second_call(
        functools.partial(second_part_kernel, 0), half, coefs, own, [in_vmem(source), away_core], True
    )
    other_a = swap(part_a)
    part_b = second_call(functools.partial(second_part_kernel, 1), half, coefs, own, [in_vmem(source)], False)
    other_b = swap(part_b)

    def result(first_row, inputs):
        return pl.pallas_call(
            functools.partial(result_kernel, first_row),
            name="result",
            out_shape=jax.ShapeDtypeStruct((rows, size, width), jnp.bfloat16),
            in_specs=[VMEM, VMEM] + [pl.BlockSpec(memory_space=pltpu.HBM)] * (len(inputs) - 2),
            out_specs=pl.BlockSpec(memory_space=pltpu.HBM),
            scratch_shapes=[pltpu.VMEM(piece.shape, piece.dtype), pltpu.SemaphoreType.DMA],
            input_output_aliases={2: 0} if len(inputs) > 2 else {},
            compiler_params=PARAMS,
        )(*inputs)

    out = result(0, [part_a, other_a])
    return result(half, [part_b, other_b, out]).reshape(rows * size, width)


def solution(mesh):
    return jax.shard_map(
        functools.partial(body, mesh.shape["row"], mesh.shape["col"]),
        mesh=mesh,
        in_specs=(
            P("row", "col", None, None),
            P("row", "col"),
            P("row", "col"),
            P("col", None),
            P("col"),
        ),
        out_specs=P("row", None),
        check_vma=False,
    )
```

```python
import functools

import jax
import jax.numpy as jnp
from jax import lax
from jax.experimental import pallas as pl
from jax.experimental.pallas import tpu as pltpu
from jax.sharding import PartitionSpec as P

VMEM_LIMIT = 12 * 1024 * 1024


def slot_ranges(slots):
    first = min(12, slots)
    return [range(first)] + ([range(first, slots)] if slots > first else [])


def sums_kernel(cols_hbm, counts_hbm, blocks_ref, sums_ref, held_ref, acc_ref, cols_ref, counts_ref, list_sems, sems):
    rows, slots, size, _ = blocks_ref.shape
    groups = acc_ref.shape[0] - 1
    first, *others = slot_ranges(slots)
    spans = [range(start, min(start + 4, len(first))) for start in range(0, len(first), 4)] + others

    def fetch(b, i):
        span = pl.ds(spans[i].start, len(spans[i]))
        return pltpu.make_async_copy(blocks_ref.at[b, span], held_ref.at[b, span], sems.at[b, i])

    def when_live(b, i, action):
        if i == 0:
            action()
        else:
            pl.when(counts_ref[b] > spans[i].start)(action)

    counts_copy = pltpu.make_async_copy(counts_hbm, counts_ref, list_sems.at[0])
    cols_copy = pltpu.make_async_copy(cols_hbm, cols_ref, list_sems.at[1])
    counts_copy.start()
    cols_copy.start()
    for b in range(rows):
        fetch(b, 0).start()
    acc_ref[...] = jnp.zeros_like(acc_ref)
    counts_copy.wait()
    cols_copy.wait()
    for b in range(rows):
        for i in range(1, len(spans)):
            when_live(b, i, lambda b=b, i=i: fetch(b, i).start())

    def add(b, part):
        for slot in part:
            col = jnp.where(slot < counts_ref[b], cols_ref[b, slot], groups)
            block = held_ref[b, slot].astype(jnp.float32)
            acc_ref[col] += jnp.sum(block.reshape(size // 8, 8, size), axis=0)

    for b in range(rows):
        for i in range(len(spans) - len(others)):
            when_live(b, i, lambda b=b, i=i: fetch(b, i).wait())
        add(b, first)
    for b in range(rows):
        for i in range(len(spans) - len(others), len(spans)):

            def finish(b=b, i=i):
                fetch(b, i).wait()
                add(b, spans[i])

            when_live(b, i, finish)

    sums_ref[...] = jnp.sum(acc_ref[:groups], axis=1)


def multiply_rows(rows, counts_ref, slots, start, gather, acc_ref):
    first, *others = slot_ranges(slots)

    def product(row, part):
        left, right = zip(*[gather(row, slot) for slot in part])
        return jnp.dot(jnp.concatenate(left, axis=1), jnp.concatenate(right, axis=0), preferred_element_type=jnp.float32)

    for b, row in enumerate(rows):
        acc_ref[b] = start(b) + product(row, first)
    for b, row in enumerate(rows):
        for part in others:

            @pl.when(counts_ref[row] > part.start)
            def _(b=b, row=row, part=part):
                acc_ref[b] += product(row, part)


def first_kernel(sending, cols_ref, counts_ref, sums_ref, added_ref, demand_ref, blocks_ref, out_ref, coef_ref, inverse_ref, acc_ref):
    slots, size = blocks_ref.shape[1:3]
    count = out_ref.shape[0]
    base = 0
    if sending is not None:
        side = lax.axis_index("col")
        base = (1 - side if sending else side) * count
    inverse_ref[...] = (1.0 / (sums_ref[...] + added_ref[...]))[:, None, :]

    def gather(row, slot):
        col = cols_ref[row, slot]
        live = slot < counts_ref[row]
        scale = jnp.where(live, inverse_ref[col], 0.0)
        scale = jnp.broadcast_to(scale, (16, size)).astype(jnp.bfloat16)
        coef = (blocks_ref[row, jnp.where(live, slot, 0)].reshape(size // 16, 16, size) * scale).reshape(size, size)
        coef_ref[row, slot] = coef
        return coef, demand_ref[col]

    rows = [base + b for b in range(count)]
    multiply_rows(rows, counts_ref, slots, lambda b: 0.0, gather, acc_ref)
    out_ref[...] = acc_ref[...].astype(out_ref.dtype)


def second_rows(first_row, place, cols_ref, counts_ref, coef_ref, source_ref, start, out_ref, acc_ref):
    slots = coef_ref.shape[1]

    def gather(row, slot):
        return coef_ref[row, slot], source_ref[place(cols_ref[row, slot])]

    rows = [first_row + b for b in range(out_ref.shape[0])]
    multiply_rows(rows, counts_ref, slots, start, gather, acc_ref)
    out_ref[...] = acc_ref[...].astype(out_ref.dtype)


def exact_scale(count, part):
    scale = -(-(1 << 16) // part)
    assert all((i * scale) >> 16 == i // part for i in range(count))
    return scale


HOME = ((0, 0, 0), (0, 1, 0), (1, 0, 0), (1, 1, 0))
AWAY = ((0, 0, 1), (0, 1, 1), (1, 0, 1), (1, 1, 1))


def collect(array, places, core, source_ref):
    part = array.shape[0] // len(places)
    for i, (z, y, away) in enumerate(places):
        at = ((z * 4 + y * 2 + core) * 2 + away) * part
        source_ref[at : at + part] = array[i * part : (i + 1) * part]


def collect_kernel(home_ref, away_ref, home_core_ref, source_ref):
    collect(home_ref, HOME, 0, source_ref)
    collect(away_ref, AWAY, 0, source_ref)
    collect(home_core_ref, HOME, 1, source_ref)


def second_part_kernel(which, cols_ref, counts_ref, coef_ref, own_ref, *rest):
    part = own_ref.shape[0]
    if which == 0:
        _, away_core_ref, out_ref, source_ref, acc_ref = rest
        collect(away_core_ref, AWAY, 1, source_ref)
    else:
        source_ref, out_ref, acc_ref = rest
    side = lax.axis_index("col")
    near = lax.rem(lax.axis_index("row"), 8) * 2 + side
    scale = exact_scale(source_ref.shape[0], part)

    def place(col):
        piece = lax.shift_right_logical(col * scale, 16)
        return col + part * ((piece ^ near) - piece)

    def start(b):
        return jnp.where(side == which, own_ref[b].astype(jnp.float32), 0.0)

    second_rows(which * part, place, cols_ref, counts_ref, coef_ref, source_ref, start, out_ref, acc_ref)


def second_kernel(cols_ref, counts_ref, coef_ref, own_ref, source_ref, out_ref, acc_ref):
    first = lax.axis_index("col") == 0

    def start(b):
        return jnp.where(first, own_ref[b].astype(jnp.float32), 0.0)

    second_rows(0, lambda col: col, cols_ref, counts_ref, coef_ref, source_ref, start, out_ref, acc_ref)


def choose_kernel(own_ref, crossed_ref, home_ref, away_ref):
    owner = lax.div(lax.axis_index("row"), 8) == lax.axis_index("col")

    @pl.when(owner)
    def _():
        home_ref[...] = own_ref[...]
        away_ref[...] = crossed_ref[...]

    @pl.when(jnp.logical_not(owner))
    def _():
        home_ref[...] = crossed_ref[...]
        away_ref[...] = own_ref[...]


def join_kernel(*refs):
    pieces, joined_ref = refs[:-1], refs[-1]
    part = pieces[0].shape[0]
    for i, piece in enumerate(pieces):
        joined_ref[i * part : (i + 1) * part] = piece[...]


def result_kernel(first_row, mine_ref, other_ref, *rest):
    out_ref, sum_ref, sem = rest[-3:]
    sum_ref[...] = (mine_ref[...].astype(jnp.float32) + other_ref[...].astype(jnp.float32)).astype(sum_ref.dtype)
    copy = pltpu.make_async_copy(sum_ref, out_ref.at[pl.ds(first_row, sum_ref.shape[0])], sem)
    copy.start()
    copy.wait()


SMEM = pl.BlockSpec(memory_space=pltpu.SMEM)
VMEM = pl.BlockSpec(memory_space=pltpu.VMEM)
PARAMS = pltpu.CompilerParams(vmem_limit_bytes=VMEM_LIMIT)


def cost(flops, bytes_accessed):
    return pl.CostEstimate(flops=flops, bytes_accessed=bytes_accessed, transcendentals=0)


def in_vmem(array):
    return pltpu.with_memory_space_constraint(array, pltpu.VMEM)


def body(n_row, n_col, blocks, slot_cols, counts, demand, value_added):
    rows, slots, size, _ = blocks.shape
    width = demand.shape[1]
    groups = demand.shape[0] // size
    group_devices = n_row // n_col
    paired = n_col == 2 and n_row == 16 and rows % 2 == 0
    half = rows // 2
    counts = counts.reshape(rows)

    sums, held = pl.pallas_call(
        sums_kernel,
        name="column_sums",
        out_shape=(
            jax.ShapeDtypeStruct((groups, size), jnp.float32),
            pltpu.VMEM(blocks.shape, blocks.dtype),
        ),
        in_specs=[pl.BlockSpec(memory_space=pltpu.HBM)] * 3,
        out_specs=(VMEM, VMEM),
        scratch_shapes=[
            pltpu.VMEM((groups + 1, 8, size), jnp.float32),
            pltpu.SMEM(slot_cols.shape, jnp.int32),
            pltpu.SMEM(counts.shape, jnp.int32),
            pltpu.SemaphoreType.DMA((2,)),
            pltpu.SemaphoreType.DMA((rows, 4)),
        ],
        compiler_params=PARAMS,
        cost_estimate=cost(0, 4 * rows * size * size * slots),
    )(*[pltpu.with_memory_space_constraint(array, pltpu.HBM) for array in (slot_cols, counts, blocks)])

    def flip(array, mask):
        return lax.ppermute(array, "row", [(i, i ^ mask) for i in range(n_row)])

    def swap(array):
        return lax.ppermute(array, "col", [(0, 1), (1, 0)])

    if paired:
        for masks in ((1, 2, 3), (4, 8, 12)):
            sums = sums.astype(jnp.bfloat16)
            parts = [sums] + [flip(sums, m) for m in masks]
            sums = functools.reduce(jnp.add, [part.astype(jnp.float32) for part in parts])
    else:
        sums = lax.psum(sums, "row")

    def layer_cost(count):
        return cost(2 * count * slots * size * size * width, count * slots * size * size * 2)

    def first_layer(sending, count, dtype, held):
        return pl.pallas_call(
            functools.partial(first_kernel, sending),
            name="first_layer",
            out_shape=(
                jax.ShapeDtypeStruct((count, size, width), dtype),
                pltpu.VMEM(blocks.shape, blocks.dtype),
            ),
            in_specs=[SMEM, SMEM, VMEM, VMEM, VMEM, VMEM],
            out_specs=(VMEM, VMEM),
            scratch_shapes=[
                pltpu.VMEM((groups, 1, size), jnp.float32),
                pltpu.VMEM((count, size, width), jnp.float32),
            ],
            input_output_aliases={5: 1},
            compiler_params=PARAMS,
            cost_estimate=layer_cost(count),
        )(
            slot_cols,
            counts,
            sums,
            value_added.reshape(groups, size),
            demand.reshape(groups, size, width),
            in_vmem(held),
        )

    def second_call(kernel, count, coefs, own, sources, keep_sources):
        dtype = jnp.bfloat16 if paired else jnp.float32
        out = jax.ShapeDtypeStruct((count, size, width), dtype)
        return pl.pallas_call(
            kernel,
            name="second_layer",
            out_shape=(out, pltpu.VMEM((groups, size, width), jnp.bfloat16)) if keep_sources else out,
            input_output_aliases={4: 1} if keep_sources else {},
            in_specs=[SMEM, SMEM] + [VMEM] * (2 + len(sources)),
            out_specs=(VMEM, VMEM) if keep_sources else VMEM,
            scratch_shapes=[pltpu.VMEM((count, size, width), jnp.float32)],
            compiler_params=PARAMS,
            cost_estimate=layer_cost(count),
        )(slot_cols, counts, in_vmem(coefs), own, *sources)

    if not paired:
        group = lax.axis_index("col")
        partial, coefs = first_layer(None, rows, jnp.float32, held)
        layer_one = lax.psum(partial, "col").astype(jnp.bfloat16)
        gathered = lax.all_gather(layer_one, "row", axis=0, tiled=True)
        source = lax.dynamic_slice_in_dim(gathered, group * groups, groups, 0)
        partial = second_call(second_kernel, rows, coefs, layer_one, [source], False)
        return lax.psum(partial, "col").astype(jnp.bfloat16).reshape(rows * size, width)

    sent, coefs = first_layer(True, half, jnp.bfloat16, held)
    arrived = swap(sent)
    kept, coefs = first_layer(False, half, jnp.float32, coefs)
    own = (kept + arrived.astype(jnp.float32)).astype(jnp.bfloat16)

    piece = jax.ShapeDtypeStruct(own.shape, own.dtype)
    home, away = pl.pallas_call(
        choose_kernel,
        name="home_and_away",
        out_shape=(piece, piece),
        in_specs=[VMEM] * 2,
        out_specs=(VMEM, VMEM),
        compiler_params=PARAMS,
    )(own, flip(own, group_devices))

    def join(pieces):
        return pl.pallas_call(
            join_kernel,
            name="own_joined",
            out_shape=jax.ShapeDtypeStruct((len(pieces) * half, size, width), own.dtype),
            in_specs=[VMEM] * len(pieces),
            out_specs=VMEM,
            compiler_params=PARAMS,
        )(*pieces)

    away = swap(away)
    home, away = [join([part] + [flip(part, mask) for mask in (2, 4, 6)]) for part in (home, away)]
    home_core, away_core = flip(home, 1), flip(away, 1)
    source = pl.pallas_call(
        collect_kernel,
        name="own_collected",
        out_shape=pltpu.VMEM((groups, size, width), jnp.bfloat16),
        in_specs=[VMEM] * 3,
        out_specs=VMEM,
        compiler_params=PARAMS,
        cost_estimate=cost(0, 2 * groups * size * width * 2),
    )(home, away, home_core)

    part_a, source = second_call(
        functools.partial(second_part_kernel, 0), half, coefs, own, [in_vmem(source), away_core], True
    )
    other_a = swap(part_a)
    part_b = second_call(functools.partial(second_part_kernel, 1), half, coefs, own, [in_vmem(source)], False)
    other_b = swap(part_b)

    def result(first_row, inputs):
        return pl.pallas_call(
            functools.partial(result_kernel, first_row),
            name="result",
            out_shape=jax.ShapeDtypeStruct((rows, size, width), jnp.bfloat16),
            in_specs=[VMEM, VMEM] + [pl.BlockSpec(memory_space=pltpu.HBM)] * (len(inputs) - 2),
            out_specs=pl.BlockSpec(memory_space=pltpu.HBM),
            scratch_shapes=[pltpu.VMEM(piece.shape, piece.dtype), pltpu.SemaphoreType.DMA],
            input_output_aliases={2: 0} if len(inputs) > 2 else {},
            compiler_params=PARAMS,
        )(*inputs)

    out = result(0, [part_a, other_a])
    return result(half, [part_b, other_b, out]).reshape(rows * size, width)


def solution(mesh):
    return jax.shard_map(
        functools.partial(body, mesh.shape["row"], mesh.shape["col"]),
        mesh=mesh,
        in_specs=(
            P("row", "col", None, None),
            P("row", "col"),
            P("row", "col"),
            P("col", None),
            P("col"),
        ),
        out_specs=P("row", None),
        check_vma=False,
    )
```

```python
import functools

import jax
import jax.numpy as jnp
from jax import lax
from jax.experimental import pallas as pl
from jax.experimental.pallas import tpu as pltpu
from jax.sharding import PartitionSpec as P

VMEM_LIMIT = 12 * 1024 * 1024


def slot_ranges(slots):
    first = min(12, slots)
    return [range(first)] + ([range(first, slots)] if slots > first else [])


def sums_kernel(cols_hbm, counts_hbm, blocks_ref, sums_ref, held_ref, acc_ref, cols_ref, counts_ref, list_sems, sems):
    rows, slots, size, _ = blocks_ref.shape
    groups = acc_ref.shape[0] - 1
    first, *others = slot_ranges(slots)

    def fetch(b, part):
        span = pl.ds(part.start, len(part))
        return pltpu.make_async_copy(blocks_ref.at[b, span], held_ref.at[b, span], sems.at[b, min(part.start, 1)])

    counts_copy = pltpu.make_async_copy(counts_hbm, counts_ref, list_sems.at[0])
    cols_copy = pltpu.make_async_copy(cols_hbm, cols_ref, list_sems.at[1])
    counts_copy.start()
    cols_copy.start()
    for b in range(rows):
        fetch(b, first).start()
    acc_ref[...] = jnp.zeros_like(acc_ref)
    counts_copy.wait()
    cols_copy.wait()
    for b in range(rows):
        for part in others:

            @pl.when(counts_ref[b] > part.start)
            def _(b=b, part=part):
                fetch(b, part).start()

    def add(b, part):
        fetch(b, part).wait()
        for slot in part:
            col = jnp.where(slot < counts_ref[b], cols_ref[b, slot], groups)
            block = held_ref[b, slot].astype(jnp.float32)
            acc_ref[col] += jnp.sum(block.reshape(size // 8, 8, size), axis=0)

    for b in range(rows):
        add(b, first)
    for b in range(rows):
        for part in others:

            @pl.when(counts_ref[b] > part.start)
            def _(b=b, part=part):
                add(b, part)

    sums_ref[...] = jnp.sum(acc_ref[:groups], axis=1)


def multiply_rows(rows, counts_ref, slots, start, gather, acc_ref):
    first, *others = slot_ranges(slots)

    def product(row, part):
        left, right = zip(*[gather(row, slot) for slot in part])
        return jnp.dot(jnp.concatenate(left, axis=1), jnp.concatenate(right, axis=0), preferred_element_type=jnp.float32)

    for b, row in enumerate(rows):
        acc_ref[b] = start(b) + product(row, first)
    for b, row in enumerate(rows):
        for part in others:

            @pl.when(counts_ref[row] > part.start)
            def _(b=b, row=row, part=part):
                acc_ref[b] += product(row, part)


def scaled_block(row, slot, cols_ref, counts_ref, inverse_ref, blocks_ref):
    size = blocks_ref.shape[2]
    scale = jnp.where(slot < counts_ref[row], inverse_ref[pl.ds(cols_ref[row, slot], 1), :], 0.0)
    scale = jnp.broadcast_to(scale, (16, size)).astype(jnp.bfloat16)
    return (blocks_ref[row, slot].reshape(size // 16, 16, size) * scale).reshape(size, size)


def first_row(sending, count):
    if sending is None:
        return 0
    side = lax.axis_index("col")
    return (1 - side if sending else side) * count


def first_kernel(sending, cols_ref, counts_ref, sums_ref, added_ref, demand_ref, blocks_ref, *rest):
    inverse_ref, acc_ref = rest[-2:]
    if sending:
        out_ref, coef_ref = rest[-3], None
    else:
        out_ref, coef_ref = rest[-4:-2]
    slots = blocks_ref.shape[1]
    count = out_ref.shape[0]
    inverse_ref[...] = 1.0 / (sums_ref[...] + added_ref[...])

    def gather(row, slot):
        coef = scaled_block(row, slot, cols_ref, counts_ref, inverse_ref, blocks_ref)
        if coef_ref is not None:
            coef_ref[row, slot] = coef
        return coef, demand_ref[cols_ref[row, slot]]

    rows = [first_row(sending, count) + b for b in range(count)]
    multiply_rows(rows, counts_ref, slots, lambda b: 0.0, gather, acc_ref)
    out_ref[...] = acc_ref[...].astype(out_ref.dtype)


def scale_kernel(count, cols_ref, counts_ref, sums_ref, added_ref, blocks_ref, coef_ref, inverse_ref):
    first, *others = slot_ranges(blocks_ref.shape[1])
    inverse_ref[...] = 1.0 / (sums_ref[...] + added_ref[...])

    def scale(row, part):
        for slot in part:
            coef_ref[row, slot] = scaled_block(row, slot, cols_ref, counts_ref, inverse_ref, blocks_ref)

    rows = [first_row(True, count) + b for b in range(count)]
    for row in rows:
        scale(row, first)
    for row in rows:
        for part in others:

            @pl.when(counts_ref[row] > part.start)
            def _(row=row, part=part):
                scale(row, part)


def fetch_kernel(demand_hbm, _, demand_ref, sem):
    copy = pltpu.make_async_copy(demand_hbm, demand_ref, sem)
    copy.start()
    copy.wait()


def second_rows(first_row, place, cols_ref, counts_ref, coef_ref, source_ref, start, out_ref, acc_ref):
    slots = coef_ref.shape[1]

    def gather(row, slot):
        return coef_ref[row, slot], source_ref[place(cols_ref[row, slot])]

    rows = [first_row + b for b in range(out_ref.shape[0])]
    multiply_rows(rows, counts_ref, slots, start, gather, acc_ref)
    out_ref[...] = acc_ref[...].astype(out_ref.dtype)


def exact_scale(count, part):
    scale = -(-(1 << 16) // part)
    assert all((i * scale) >> 16 == i // part for i in range(count))
    return scale


HOME = ((0, 0, 0), (0, 1, 0), (1, 0, 0), (1, 1, 0))
AWAY = ((0, 0, 1), (0, 1, 1), (1, 0, 1), (1, 1, 1))


def collect(array, places, core, source_ref):
    part = array.shape[0] // len(places)
    for i, (z, y, away) in enumerate(places):
        at = ((z * 4 + y * 2 + core) * 2 + away) * part
        source_ref[at : at + part] = array[i * part : (i + 1) * part]


def collect_kernel(home_ref, away_ref, home_core_ref, source_ref):
    collect(home_ref, HOME, 0, source_ref)
    collect(away_ref, AWAY, 0, source_ref)
    collect(home_core_ref, HOME, 1, source_ref)


def second_part_kernel(which, cols_ref, counts_ref, coef_ref, own_ref, *rest):
    part = own_ref.shape[0]
    if which == 0:
        _, away_core_ref, out_ref, source_ref, acc_ref = rest
        collect(away_core_ref, AWAY, 1, source_ref)
    else:
        source_ref, out_ref, acc_ref = rest
    side = lax.axis_index("col")
    near = lax.rem(lax.axis_index("row"), 8) * 2 + side
    scale = exact_scale(source_ref.shape[0], part)

    def place(col):
        piece = lax.shift_right_logical(col * scale, 16)
        return col + part * ((piece ^ near) - piece)

    def start(b):
        return jnp.where(side == which, own_ref[b].astype(jnp.float32), 0.0)

    second_rows(which * part, place, cols_ref, counts_ref, coef_ref, source_ref, start, out_ref, acc_ref)


def second_kernel(cols_ref, counts_ref, coef_ref, own_ref, source_ref, out_ref, acc_ref):
    first = lax.axis_index("col") == 0

    def start(b):
        return jnp.where(first, own_ref[b].astype(jnp.float32), 0.0)

    second_rows(0, lambda col: col, cols_ref, counts_ref, coef_ref, source_ref, start, out_ref, acc_ref)


def choose_kernel(own_ref, crossed_ref, _, home_ref, away_ref):
    owner = lax.div(lax.axis_index("row"), 8) == lax.axis_index("col")

    @pl.when(owner)
    def _():
        home_ref[...] = own_ref[...]
        away_ref[...] = crossed_ref[...]

    @pl.when(jnp.logical_not(owner))
    def _():
        home_ref[...] = crossed_ref[...]
        away_ref[...] = own_ref[...]


def join_kernel(*refs):
    pieces, joined_ref = refs[:-1], refs[-1]
    part = pieces[0].shape[0]
    for i, piece in enumerate(pieces):
        joined_ref[i * part : (i + 1) * part] = piece[...]


def result_kernel(first_row, mine_ref, other_ref, *rest):
    out_ref, sum_ref, sem = rest[-3:]
    sum_ref[...] = (mine_ref[...].astype(jnp.float32) + other_ref[...].astype(jnp.float32)).astype(sum_ref.dtype)
    copy = pltpu.make_async_copy(sum_ref, out_ref.at[pl.ds(first_row, sum_ref.shape[0])], sem)
    copy.start()
    copy.wait()


SMEM = pl.BlockSpec(memory_space=pltpu.SMEM)
VMEM = pl.BlockSpec(memory_space=pltpu.VMEM)
PARAMS = pltpu.CompilerParams(vmem_limit_bytes=VMEM_LIMIT)


def cost(flops, bytes_accessed):
    return pl.CostEstimate(flops=flops, bytes_accessed=bytes_accessed, transcendentals=0)


def in_vmem(array):
    return pltpu.with_memory_space_constraint(array, pltpu.VMEM)


def body(n_row, n_col, blocks, slot_cols, counts, demand, value_added):
    rows, slots, size, _ = blocks.shape
    width = demand.shape[1]
    groups = demand.shape[0] // size
    group_devices = n_row // n_col
    paired = n_col == 2 and n_row == 16 and rows % 2 == 0
    half = rows // 2
    counts = counts.reshape(rows)

    sums, held = pl.pallas_call(
        sums_kernel,
        name="column_sums",
        out_shape=(
            jax.ShapeDtypeStruct((groups, size), jnp.float32),
            pltpu.VMEM(blocks.shape, blocks.dtype),
        ),
        in_specs=[pl.BlockSpec(memory_space=pltpu.HBM)] * 3,
        out_specs=(VMEM, VMEM),
        scratch_shapes=[
            pltpu.VMEM((groups + 1, 8, size), jnp.float32),
            pltpu.SMEM(slot_cols.shape, jnp.int32),
            pltpu.SMEM(counts.shape, jnp.int32),
            pltpu.SemaphoreType.DMA((2,)),
            pltpu.SemaphoreType.DMA((rows, 2)),
        ],
        compiler_params=PARAMS,
        cost_estimate=cost(0, 4 * rows * size * size * slots),
    )(*[pltpu.with_memory_space_constraint(array, pltpu.HBM) for array in (slot_cols, counts, blocks)])

    def flip(array, mask):
        return lax.ppermute(array, "row", [(i, i ^ mask) for i in range(n_row)])

    def swap(array):
        return lax.ppermute(array, "col", [(0, 1), (1, 0)])

    if paired:
        for masks in ((1, 2, 3), (4, 8, 12)):
            sums = sums.astype(jnp.bfloat16)
            parts = [sums] + [flip(sums, m) for m in masks]
            if masks[0] == 4:
                demand = pl.pallas_call(
                    fetch_kernel,
                    name="own_demand",
                    out_shape=pltpu.VMEM(demand.shape, demand.dtype),
                    in_specs=[pl.BlockSpec(memory_space=pltpu.HBM), pl.BlockSpec(memory_space=pl.ANY)],
                    out_specs=VMEM,
                    scratch_shapes=[pltpu.SemaphoreType.DMA],
                    compiler_params=PARAMS,
                    cost_estimate=cost(0, 3 * demand.size * 2),
                )(pltpu.with_memory_space_constraint(demand, pltpu.HBM), sums)
            sums = functools.reduce(jnp.add, [part.astype(jnp.float32) for part in parts])
    else:
        sums = lax.psum(sums, "row")

    def layer_cost(count):
        return cost(2 * count * slots * size * size * width, count * slots * size * size * 2)

    def first_layer(sending, count, dtype, held, earlier=()):
        out = jax.ShapeDtypeStruct((count, size, width), dtype)
        return pl.pallas_call(
            functools.partial(first_kernel, sending),
            name="first_layer",
            out_shape=out if sending else (out, pltpu.VMEM(blocks.shape, blocks.dtype)),
            in_specs=[SMEM, SMEM, VMEM, VMEM, VMEM, VMEM] + [pl.BlockSpec(memory_space=pl.ANY)] * len(earlier),
            out_specs=VMEM if sending else (VMEM, VMEM),
            scratch_shapes=[
                pltpu.VMEM((groups, size), jnp.float32),
                pltpu.VMEM((count, size, width), jnp.float32),
            ],
            input_output_aliases={} if sending else {5: 1},
            compiler_params=PARAMS,
            cost_estimate=layer_cost(count),
        )(
            slot_cols,
            counts,
            sums,
            value_added.reshape(groups, size),
            demand.reshape(groups, size, width),
            in_vmem(held),
            *earlier,
        )

    def second_call(kernel, count, coefs, own, sources, keep_sources):
        dtype = jnp.bfloat16 if paired else jnp.float32
        out = jax.ShapeDtypeStruct((count, size, width), dtype)
        return pl.pallas_call(
            kernel,
            name="second_layer",
            out_shape=(out, pltpu.VMEM((groups, size, width), jnp.bfloat16)) if keep_sources else out,
            input_output_aliases={4: 1} if keep_sources else {},
            in_specs=[SMEM, SMEM] + [VMEM] * (2 + len(sources)),
            out_specs=(VMEM, VMEM) if keep_sources else VMEM,
            scratch_shapes=[pltpu.VMEM((count, size, width), jnp.float32)],
            compiler_params=PARAMS,
            cost_estimate=layer_cost(count),
        )(slot_cols, counts, in_vmem(coefs), own, *sources)

    if not paired:
        group = lax.axis_index("col")
        partial, coefs = first_layer(None, rows, jnp.float32, held)
        layer_one = lax.psum(partial, "col").astype(jnp.bfloat16)
        gathered = lax.all_gather(layer_one, "row", axis=0, tiled=True)
        source = lax.dynamic_slice_in_dim(gathered, group * groups, groups, 0)
        partial = second_call(second_kernel, rows, coefs, layer_one, [source], False)
        return lax.psum(partial, "col").astype(jnp.bfloat16).reshape(rows * size, width)

    sent = first_layer(True, half, jnp.bfloat16, held)
    arrived = swap(sent)
    kept, coefs = first_layer(False, half, jnp.float32, held, [sent])
    coefs = pl.pallas_call(
        functools.partial(scale_kernel, half),
        name="own_coefficients",
        out_shape=pltpu.VMEM(blocks.shape, blocks.dtype),
        in_specs=[SMEM, SMEM, VMEM, VMEM, VMEM],
        out_specs=VMEM,
        scratch_shapes=[pltpu.VMEM((groups, size), jnp.float32)],
        input_output_aliases={4: 0},
        compiler_params=PARAMS,
        cost_estimate=layer_cost(half),
    )(slot_cols, counts, sums, value_added.reshape(groups, size), in_vmem(coefs))
    own = (kept + arrived.astype(jnp.float32)).astype(jnp.bfloat16)

    piece = jax.ShapeDtypeStruct(own.shape, own.dtype)
    home, away = pl.pallas_call(
        choose_kernel,
        name="home_and_away",
        out_shape=(piece, piece),
        in_specs=[VMEM] * 2 + [pl.BlockSpec(memory_space=pl.ANY)],
        out_specs=(VMEM, VMEM),
        compiler_params=PARAMS,
    )(own, flip(own, group_devices), in_vmem(coefs))

    def join(pieces):
        return pl.pallas_call(
            join_kernel,
            name="own_joined",
            out_shape=jax.ShapeDtypeStruct((len(pieces) * half, size, width), own.dtype),
            in_specs=[VMEM] * len(pieces),
            out_specs=VMEM,
            compiler_params=PARAMS,
        )(*pieces)

    away = swap(away)
    home, away = [join([part] + [flip(part, mask) for mask in (2, 4, 6)]) for part in (home, away)]
    home_core, away_core = flip(home, 1), flip(away, 1)
    source = pl.pallas_call(
        collect_kernel,
        name="own_collected",
        out_shape=pltpu.VMEM((groups, size, width), jnp.bfloat16),
        in_specs=[VMEM] * 3,
        out_specs=VMEM,
        compiler_params=PARAMS,
        cost_estimate=cost(0, 2 * groups * size * width * 2),
    )(home, away, home_core)

    part_a, source = second_call(
        functools.partial(second_part_kernel, 0), half, coefs, own, [in_vmem(source), away_core], True
    )
    other_a = swap(part_a)
    part_b = second_call(functools.partial(second_part_kernel, 1), half, coefs, own, [in_vmem(source)], False)
    other_b = swap(part_b)

    def result(first_row, inputs):
        return pl.pallas_call(
            functools.partial(result_kernel, first_row),
            name="result",
            out_shape=jax.ShapeDtypeStruct((rows, size, width), jnp.bfloat16),
            in_specs=[VMEM, VMEM] + [pl.BlockSpec(memory_space=pltpu.HBM)] * (len(inputs) - 2),
            out_specs=pl.BlockSpec(memory_space=pltpu.HBM),
            scratch_shapes=[pltpu.VMEM(piece.shape, piece.dtype), pltpu.SemaphoreType.DMA],
            input_output_aliases={2: 0} if len(inputs) > 2 else {},
            compiler_params=PARAMS,
        )(*inputs)

    out = result(0, [part_a, other_a])
    return result(half, [part_b, other_b, out]).reshape(rows * size, width)


def solution(mesh):
    return jax.shard_map(
        functools.partial(body, mesh.shape["row"], mesh.shape["col"]),
        mesh=mesh,
        in_specs=(
            P("row", "col", None, None),
            P("row", "col"),
            P("row", "col"),
            P("col", None),
            P("col"),
        ),
        out_specs=P("row", None),
        check_vma=False,
    )
```

```python
import functools

import jax
import jax.numpy as jnp
from jax import lax
from jax.experimental import pallas as pl
from jax.experimental.pallas import tpu as pltpu
from jax.sharding import PartitionSpec as P

VMEM_LIMIT = 12 * 1024 * 1024


def slot_ranges(slots):
    first = min(12, slots)
    return [range(first)] + ([range(first, slots)] if slots > first else [])


def sums_kernel(cols_hbm, counts_hbm, blocks_ref, sums_ref, held_ref, acc_ref, cols_ref, counts_ref, list_sems, sems):
    rows, slots, size, _ = blocks_ref.shape
    groups = acc_ref.shape[0] - 1
    first, *others = slot_ranges(slots)
    others = [range(start, min(start + 12, slots)) for other in others for start in range(other.start, slots, 12)]

    def fetch(b, part):
        span = pl.ds(part.start, len(part))
        return pltpu.make_async_copy(blocks_ref.at[b, span], held_ref.at[b, span], sems.at[b, part.start // 12])

    counts_copy = pltpu.make_async_copy(counts_hbm, counts_ref, list_sems.at[0])
    cols_copy = pltpu.make_async_copy(cols_hbm, cols_ref, list_sems.at[1])
    counts_copy.start()
    cols_copy.start()
    for b in range(rows):
        fetch(b, first).start()
    acc_ref[...] = jnp.zeros_like(acc_ref)
    counts_copy.wait()
    cols_copy.wait()
    for b in range(rows):
        for part in others:

            @pl.when(counts_ref[b] > len(first))
            def _(b=b, part=part):
                fetch(b, part).start()

    def add(b, part):
        fetch(b, part).wait()
        for slot in part:
            col = jnp.where(slot < counts_ref[b], cols_ref[b, slot], groups)
            block = held_ref[b, slot].astype(jnp.float32)
            acc_ref[col] += jnp.sum(block.reshape(size // 8, 8, size), axis=0)

    for b in range(rows):
        add(b, first)
    for b in range(rows):
        for part in others:

            @pl.when(counts_ref[b] > len(first))
            def _(b=b, part=part):
                add(b, part)

    sums_ref[...] = jnp.sum(acc_ref[:groups], axis=1)


def multiply_rows(rows, counts_ref, slots, start, gather, acc_ref):
    first, *others = slot_ranges(slots)

    def product(row, part):
        left, right = zip(*[gather(row, slot) for slot in part])
        return jnp.dot(jnp.concatenate(left, axis=1), jnp.concatenate(right, axis=0), preferred_element_type=jnp.float32)

    for b, row in enumerate(rows):
        acc_ref[b] = start(b) + product(row, first)
    for b, row in enumerate(rows):
        for part in others:

            @pl.when(counts_ref[row] > part.start)
            def _(b=b, row=row, part=part):
                acc_ref[b] += product(row, part)


def scaled_block(row, slot, cols_ref, counts_ref, inverse_ref, blocks_ref):
    size = blocks_ref.shape[2]
    scale = jnp.where(slot < counts_ref[row], inverse_ref[pl.ds(cols_ref[row, slot], 1), :], 0.0)
    scale = jnp.broadcast_to(scale, (16, size)).astype(jnp.bfloat16)
    return (blocks_ref[row, slot].reshape(size // 16, 16, size) * scale).reshape(size, size)


def first_row(sending, count):
    if sending is None:
        return 0
    side = lax.axis_index("col")
    return (1 - side if sending else side) * count


def first_kernel(sending, cols_ref, counts_ref, sums_ref, added_ref, demand_ref, blocks_ref, *rest):
    inverse_ref, acc_ref = rest[-2:]
    if sending:
        out_ref, coef_ref = rest[-3], None
    else:
        out_ref, coef_ref = rest[-4:-2]
    slots = blocks_ref.shape[1]
    count = out_ref.shape[0]
    inverse_ref[...] = 1.0 / (sums_ref[...] + added_ref[...])

    def gather(row, slot):
        coef = scaled_block(row, slot, cols_ref, counts_ref, inverse_ref, blocks_ref)
        if coef_ref is not None:
            coef_ref[row, slot] = coef
        return coef, demand_ref[cols_ref[row, slot]]

    rows = [first_row(sending, count) + b for b in range(count)]
    multiply_rows(rows, counts_ref, slots, lambda b: 0.0, gather, acc_ref)
    out_ref[...] = acc_ref[...].astype(out_ref.dtype)


def scale_kernel(count, cols_ref, counts_ref, sums_ref, added_ref, blocks_ref, coef_ref, token_ref, inverse_ref):
    first, *others = slot_ranges(blocks_ref.shape[1])
    inverse_ref[...] = 1.0 / (sums_ref[...] + added_ref[...])
    token_ref[...] = inverse_ref[:8]

    def scale(row, part):
        for slot in part:
            coef_ref[row, slot] = scaled_block(row, slot, cols_ref, counts_ref, inverse_ref, blocks_ref)

    rows = [first_row(True, count) + b for b in range(count)]
    for row in rows:
        scale(row, first)
    for row in rows:
        for part in others:

            @pl.when(counts_ref[row] > part.start)
            def _(row=row, part=part):
                scale(row, part)


def fetch_kernel(demand_hbm, _, demand_ref, sem):
    copy = pltpu.make_async_copy(demand_hbm, demand_ref, sem)
    copy.start()
    copy.wait()


def second_rows(first_row, place, cols_ref, counts_ref, coef_ref, source_ref, start, out_ref, acc_ref):
    slots = coef_ref.shape[1]

    def gather(row, slot):
        return coef_ref[row, slot], source_ref[place(cols_ref[row, slot])]

    rows = [first_row + b for b in range(out_ref.shape[0])]
    multiply_rows(rows, counts_ref, slots, start, gather, acc_ref)
    out_ref[...] = acc_ref[...].astype(out_ref.dtype)


def exact_scale(count, part):
    scale = -(-(1 << 16) // part)
    assert all((i * scale) >> 16 == i // part for i in range(count))
    return scale


HOME = ((0, 0, 0), (0, 1, 0), (1, 0, 0), (1, 1, 0))
AWAY = ((0, 0, 1), (0, 1, 1), (1, 0, 1), (1, 1, 1))


def collect(array, places, core, source_ref):
    part = array.shape[0] // len(places)
    for i, (z, y, away) in enumerate(places):
        at = ((z * 4 + y * 2 + core) * 2 + away) * part
        source_ref[at : at + part] = array[i * part : (i + 1) * part]


def collect_kernel(home_ref, away_ref, home_core_ref, source_ref):
    collect(home_ref, HOME, 0, source_ref)
    collect(away_ref, AWAY, 0, source_ref)
    collect(home_core_ref, HOME, 1, source_ref)


def second_part_kernel(which, cols_ref, counts_ref, coef_ref, own_ref, *rest):
    part = own_ref.shape[0]
    if which == 0:
        _, away_core_ref, out_ref, source_ref, acc_ref = rest
        collect(away_core_ref, AWAY, 1, source_ref)
    else:
        source_ref, out_ref, acc_ref = rest
    side = lax.axis_index("col")
    near = lax.rem(lax.axis_index("row"), 8) * 2 + side
    scale = exact_scale(source_ref.shape[0], part)

    def place(col):
        piece = lax.shift_right_logical(col * scale, 16)
        return col + part * ((piece ^ near) - piece)

    def start(b):
        return jnp.where(side == which, own_ref[b].astype(jnp.float32), 0.0)

    second_rows(which * part, place, cols_ref, counts_ref, coef_ref, source_ref, start, out_ref, acc_ref)


def second_kernel(cols_ref, counts_ref, coef_ref, own_ref, source_ref, out_ref, acc_ref):
    first = lax.axis_index("col") == 0

    def start(b):
        return jnp.where(first, own_ref[b].astype(jnp.float32), 0.0)

    second_rows(0, lambda col: col, cols_ref, counts_ref, coef_ref, source_ref, start, out_ref, acc_ref)


def choose_kernel(own_ref, crossed_ref, _, home_ref, away_ref):
    owner = lax.div(lax.axis_index("row"), 8) == lax.axis_index("col")

    @pl.when(owner)
    def _():
        home_ref[...] = own_ref[...]
        away_ref[...] = crossed_ref[...]

    @pl.when(jnp.logical_not(owner))
    def _():
        home_ref[...] = crossed_ref[...]
        away_ref[...] = own_ref[...]


def join_kernel(*refs):
    pieces, joined_ref = refs[:-1], refs[-1]
    part = pieces[0].shape[0]
    for i, piece in enumerate(pieces):
        joined_ref[i * part : (i + 1) * part] = piece[...]


def result_kernel(first_row, mine_ref, other_ref, *rest):
    out_ref, sum_ref, sem = rest[-3:]
    sum_ref[...] = (mine_ref[...].astype(jnp.float32) + other_ref[...].astype(jnp.float32)).astype(sum_ref.dtype)
    copy = pltpu.make_async_copy(sum_ref, out_ref.at[pl.ds(first_row, sum_ref.shape[0])], sem)
    copy.start()
    copy.wait()


SMEM = pl.BlockSpec(memory_space=pltpu.SMEM)
VMEM = pl.BlockSpec(memory_space=pltpu.VMEM)
PARAMS = pltpu.CompilerParams(vmem_limit_bytes=VMEM_LIMIT)


def cost(flops, bytes_accessed):
    return pl.CostEstimate(flops=flops, bytes_accessed=bytes_accessed, transcendentals=0)


def in_vmem(array):
    return pltpu.with_memory_space_constraint(array, pltpu.VMEM)


def body(n_row, n_col, blocks, slot_cols, counts, demand, value_added):
    rows, slots, size, _ = blocks.shape
    width = demand.shape[1]
    groups = demand.shape[0] // size
    group_devices = n_row // n_col
    paired = n_col == 2 and n_row == 16 and rows % 2 == 0
    half = rows // 2
    counts = counts.reshape(rows)

    sums, held = pl.pallas_call(
        sums_kernel,
        name="column_sums",
        out_shape=(
            jax.ShapeDtypeStruct((groups, size), jnp.float32),
            pltpu.VMEM(blocks.shape, blocks.dtype),
        ),
        in_specs=[pl.BlockSpec(memory_space=pltpu.HBM)] * 3,
        out_specs=(VMEM, VMEM),
        scratch_shapes=[
            pltpu.VMEM((groups + 1, 8, size), jnp.float32),
            pltpu.SMEM(slot_cols.shape, jnp.int32),
            pltpu.SMEM(counts.shape, jnp.int32),
            pltpu.SemaphoreType.DMA((2,)),
            pltpu.SemaphoreType.DMA((rows, -(-slots // 12))),
        ],
        compiler_params=PARAMS,
        cost_estimate=cost(0, 4 * rows * size * size * slots),
    )(*[pltpu.with_memory_space_constraint(array, pltpu.HBM) for array in (slot_cols, counts, blocks)])

    def flip(array, mask):
        return lax.ppermute(array, "row", [(i, i ^ mask) for i in range(n_row)])

    def swap(array):
        return lax.ppermute(array, "col", [(0, 1), (1, 0)])

    if paired:
        for masks in ((1, 2, 3), (4, 8, 12)):
            sums = sums.astype(jnp.bfloat16)
            parts = [sums] + [flip(sums, m) for m in masks]
            if masks[0] == 4:
                demand = pl.pallas_call(
                    fetch_kernel,
                    name="own_demand",
                    out_shape=pltpu.VMEM(demand.shape, demand.dtype),
                    in_specs=[pl.BlockSpec(memory_space=pltpu.HBM), pl.BlockSpec(memory_space=pl.ANY)],
                    out_specs=VMEM,
                    scratch_shapes=[pltpu.SemaphoreType.DMA],
                    compiler_params=PARAMS,
                    cost_estimate=cost(0, 3 * demand.size * 2),
                )(pltpu.with_memory_space_constraint(demand, pltpu.HBM), sums)
            sums = functools.reduce(jnp.add, [part.astype(jnp.float32) for part in parts])
    else:
        sums = lax.psum(sums, "row")

    def layer_cost(count):
        return cost(2 * count * slots * size * size * width, count * slots * size * size * 2)

    def first_layer(sending, count, dtype, held, earlier=()):
        out = jax.ShapeDtypeStruct((count, size, width), dtype)
        return pl.pallas_call(
            functools.partial(first_kernel, sending),
            name="first_layer",
            out_shape=out if sending else (out, pltpu.VMEM(blocks.shape, blocks.dtype)),
            in_specs=[SMEM, SMEM, VMEM, VMEM, VMEM, VMEM] + [pl.BlockSpec(memory_space=pl.ANY)] * len(earlier),
            out_specs=VMEM if sending else (VMEM, VMEM),
            scratch_shapes=[
                pltpu.VMEM((groups, size), jnp.float32),
                pltpu.VMEM((count, size, width), jnp.float32),
            ],
            input_output_aliases={} if sending else {5: 1},
            compiler_params=PARAMS,
            cost_estimate=layer_cost(count),
        )(
            slot_cols,
            counts,
            sums,
            value_added.reshape(groups, size),
            demand.reshape(groups, size, width),
            in_vmem(held),
            *earlier,
        )

    def second_call(kernel, count, coefs, own, sources, keep_sources):
        dtype = jnp.bfloat16 if paired else jnp.float32
        out = jax.ShapeDtypeStruct((count, size, width), dtype)
        return pl.pallas_call(
            kernel,
            name="second_layer",
            out_shape=(out, pltpu.VMEM((groups, size, width), jnp.bfloat16)) if keep_sources else out,
            input_output_aliases={4: 1} if keep_sources else {},
            in_specs=[SMEM, SMEM] + [VMEM] * (2 + len(sources)),
            out_specs=(VMEM, VMEM) if keep_sources else VMEM,
            scratch_shapes=[pltpu.VMEM((count, size, width), jnp.float32)],
            compiler_params=PARAMS,
            cost_estimate=layer_cost(count),
        )(slot_cols, counts, in_vmem(coefs), own, *sources)

    if not paired:
        group = lax.axis_index("col")
        partial, coefs = first_layer(None, rows, jnp.float32, held)
        layer_one = lax.psum(partial, "col").astype(jnp.bfloat16)
        gathered = lax.all_gather(layer_one, "row", axis=0, tiled=True)
        source = lax.dynamic_slice_in_dim(gathered, group * groups, groups, 0)
        partial = second_call(second_kernel, rows, coefs, layer_one, [source], False)
        return lax.psum(partial, "col").astype(jnp.bfloat16).reshape(rows * size, width)

    sent = first_layer(True, half, jnp.bfloat16, held)
    arrived = swap(sent)
    kept, coefs = first_layer(False, half, jnp.float32, held, [sent])
    coefs, token = pl.pallas_call(
        functools.partial(scale_kernel, half),
        name="own_coefficients",
        out_shape=(pltpu.VMEM(blocks.shape, blocks.dtype), jax.ShapeDtypeStruct((8, size), jnp.float32)),
        in_specs=[SMEM, SMEM, VMEM, VMEM, VMEM],
        out_specs=(VMEM, VMEM),
        scratch_shapes=[pltpu.VMEM((groups, size), jnp.float32)],
        input_output_aliases={4: 0},
        compiler_params=PARAMS,
        cost_estimate=layer_cost(half),
    )(slot_cols, counts, sums, value_added.reshape(groups, size), in_vmem(coefs))
    own = (kept + arrived.astype(jnp.float32)).astype(jnp.bfloat16)

    piece = jax.ShapeDtypeStruct(own.shape, own.dtype)
    home, away = pl.pallas_call(
        choose_kernel,
        name="home_and_away",
        out_shape=(piece, piece),
        in_specs=[VMEM] * 3,
        out_specs=(VMEM, VMEM),
        compiler_params=PARAMS,
    )(own, flip(own, group_devices), token)

    def join(pieces):
        return pl.pallas_call(
            join_kernel,
            name="own_joined",
            out_shape=jax.ShapeDtypeStruct((len(pieces) * half, size, width), own.dtype),
            in_specs=[VMEM] * len(pieces),
            out_specs=VMEM,
            compiler_params=PARAMS,
        )(*pieces)

    away = swap(away)
    home, away = [join([part] + [flip(part, mask) for mask in (2, 4, 6)]) for part in (home, away)]
    home_core, away_core = flip(home, 1), flip(away, 1)
    source = pl.pallas_call(
        collect_kernel,
        name="own_collected",
        out_shape=pltpu.VMEM((groups, size, width), jnp.bfloat16),
        in_specs=[VMEM] * 3,
        out_specs=VMEM,
        compiler_params=PARAMS,
        cost_estimate=cost(0, 2 * groups * size * width * 2),
    )(home, away, home_core)

    part_a, source = second_call(
        functools.partial(second_part_kernel, 0), half, coefs, own, [in_vmem(source), away_core], True
    )
    other_a = swap(part_a)
    part_b = second_call(functools.partial(second_part_kernel, 1), half, coefs, own, [in_vmem(source)], False)
    other_b = swap(part_b)

    def result(first_row, inputs):
        return pl.pallas_call(
            functools.partial(result_kernel, first_row),
            name="result",
            out_shape=jax.ShapeDtypeStruct((rows, size, width), jnp.bfloat16),
            in_specs=[VMEM, VMEM] + [pl.BlockSpec(memory_space=pltpu.HBM)] * (len(inputs) - 2),
            out_specs=pl.BlockSpec(memory_space=pltpu.HBM),
            scratch_shapes=[pltpu.VMEM(piece.shape, piece.dtype), pltpu.SemaphoreType.DMA],
            input_output_aliases={2: 0} if len(inputs) > 2 else {},
            compiler_params=PARAMS,
        )(*inputs)

    out = result(0, [part_a, other_a])
    return result(half, [part_b, other_b, out]).reshape(rows * size, width)


def solution(mesh):
    return jax.shard_map(
        functools.partial(body, mesh.shape["row"], mesh.shape["col"]),
        mesh=mesh,
        in_specs=(
            P("row", "col", None, None),
            P("row", "col"),
            P("row", "col"),
            P("col", None),
            P("col"),
        ),
        out_specs=P("row", None),
        check_vma=False,
    )
```

```python
import functools

import jax
import jax.numpy as jnp
from jax import lax
from jax.experimental import pallas as pl
from jax.experimental.pallas import tpu as pltpu
from jax.sharding import PartitionSpec as P

VMEM_LIMIT = 12 * 1024 * 1024


def slot_ranges(slots):
    first = min(12, slots)
    return [range(first)] + ([range(first, slots)] if slots > first else [])


def sums_kernel(cols_hbm, counts_hbm, blocks_ref, sums_ref, held_ref, acc_ref, cols_ref, counts_ref, list_sems, sems):
    rows, slots, size, _ = blocks_ref.shape
    groups = acc_ref.shape[0] - 1
    first, *others = slot_ranges(slots)
    others = [range(start, min(start + 12, slots)) for other in others for start in range(other.start, slots, 12)]

    def fetch(b, part):
        span = pl.ds(part.start, len(part))
        return pltpu.make_async_copy(blocks_ref.at[b, span], held_ref.at[b, span], sems.at[b, part.start // 12])

    counts_copy = pltpu.make_async_copy(counts_hbm, counts_ref, list_sems.at[0])
    cols_copy = pltpu.make_async_copy(cols_hbm, cols_ref, list_sems.at[1])
    counts_copy.start()
    cols_copy.start()
    for b in range(rows):
        fetch(b, first).start()
    acc_ref[...] = jnp.zeros_like(acc_ref)
    counts_copy.wait()
    cols_copy.wait()
    def for_heavy_rows(action):
        def one_row(b, carry):
            @pl.when(counts_ref[b] > len(first))
            def _():
                for part in others:
                    action(b, part)

            return carry

        if others:
            lax.fori_loop(0, rows, one_row, 0)

    def add(b, part):
        fetch(b, part).wait()
        for slot in part:
            col = jnp.where(slot < counts_ref[b], cols_ref[b, slot], groups)
            block = held_ref[b, slot].astype(jnp.float32)
            acc_ref[col] += jnp.sum(block.reshape(size // 8, 8, size), axis=0)

    def add_first(b, carry):
        add(b, first)
        return carry

    for_heavy_rows(lambda b, part: fetch(b, part).start())
    lax.fori_loop(0, rows, add_first, 0)
    for_heavy_rows(add)
    sums_ref[...] = jnp.sum(acc_ref[:groups], axis=1)


def multiply_rows(rows, counts_ref, slots, start, gather, acc_ref):
    first, *others = slot_ranges(slots)

    def product(row, part):
        left, right = zip(*[gather(row, slot) for slot in part])
        return jnp.dot(jnp.concatenate(left, axis=1), jnp.concatenate(right, axis=0), preferred_element_type=jnp.float32)

    for b, row in enumerate(rows):
        acc_ref[b] = start(b) + product(row, first)
    def one_row(b, carry):
        row = rows[0] + b
        for part in others:

            @pl.when(counts_ref[row] > part.start)
            def _():
                acc_ref[b] += product(row, part)

        return carry

    if others:
        lax.fori_loop(0, len(rows), one_row, 0)


def scaled_block(row, slot, cols_ref, counts_ref, inverse_ref, blocks_ref):
    size = blocks_ref.shape[2]
    scale = jnp.where(slot < counts_ref[row], inverse_ref[pl.ds(cols_ref[row, slot], 1), :], 0.0)
    scale = jnp.broadcast_to(scale, (16, size)).astype(jnp.bfloat16)
    return (blocks_ref[row, slot].reshape(size // 16, 16, size) * scale).reshape(size, size)


def first_row(sending, count):
    if sending is None:
        return 0
    side = lax.axis_index("col")
    return (1 - side if sending else side) * count


def first_kernel(sending, cols_ref, counts_ref, sums_ref, added_ref, demand_ref, blocks_ref, *rest):
    inverse_ref, acc_ref = rest[-2:]
    if sending:
        out_ref, coef_ref = rest[-3], None
    else:
        out_ref, coef_ref = rest[-4:-2]
    slots = blocks_ref.shape[1]
    count = out_ref.shape[0]
    inverse_ref[...] = 1.0 / (sums_ref[...] + added_ref[...])

    def gather(row, slot):
        coef = scaled_block(row, slot, cols_ref, counts_ref, inverse_ref, blocks_ref)
        if coef_ref is not None:
            coef_ref[row, slot] = coef
        return coef, demand_ref[cols_ref[row, slot]]

    rows = [first_row(sending, count) + b for b in range(count)]
    multiply_rows(rows, counts_ref, slots, lambda b: 0.0, gather, acc_ref)
    out_ref[...] = acc_ref[...].astype(out_ref.dtype)


def scale_kernel(count, cols_ref, counts_ref, sums_ref, added_ref, blocks_ref, coef_ref, token_ref, inverse_ref):
    first, *others = slot_ranges(blocks_ref.shape[1])
    inverse_ref[...] = 1.0 / (sums_ref[...] + added_ref[...])
    token_ref[...] = inverse_ref[:8]

    def scale(row, part):
        for slot in part:
            coef_ref[row, slot] = scaled_block(row, slot, cols_ref, counts_ref, inverse_ref, blocks_ref)

    rows = [first_row(True, count) + b for b in range(count)]
    for row in rows:
        scale(row, first)
    def one_row(b, carry):
        row = rows[0] + b
        for part in others:

            @pl.when(counts_ref[row] > part.start)
            def _():
                scale(row, part)

        return carry

    if others:
        lax.fori_loop(0, len(rows), one_row, 0)


def fetch_kernel(demand_hbm, _, demand_ref, sem):
    copy = pltpu.make_async_copy(demand_hbm, demand_ref, sem)
    copy.start()
    copy.wait()


def second_rows(first_row, place, cols_ref, counts_ref, coef_ref, source_ref, start, out_ref, acc_ref):
    slots = coef_ref.shape[1]

    def gather(row, slot):
        return coef_ref[row, slot], source_ref[place(cols_ref[row, slot])]

    rows = [first_row + b for b in range(out_ref.shape[0])]
    multiply_rows(rows, counts_ref, slots, start, gather, acc_ref)
    out_ref[...] = acc_ref[...].astype(out_ref.dtype)


def exact_scale(count, part):
    scale = -(-(1 << 16) // part)
    assert all((i * scale) >> 16 == i // part for i in range(count))
    return scale


HOME = ((0, 0, 0), (0, 1, 0), (1, 0, 0), (1, 1, 0))
AWAY = ((0, 0, 1), (0, 1, 1), (1, 0, 1), (1, 1, 1))


def collect(array, places, core, source_ref):
    part = array.shape[0] // len(places)
    for i, (z, y, away) in enumerate(places):
        at = ((z * 4 + y * 2 + core) * 2 + away) * part
        source_ref[at : at + part] = array[i * part : (i + 1) * part]


def collect_kernel(home_ref, away_ref, home_core_ref, source_ref):
    collect(home_ref, HOME, 0, source_ref)
    collect(away_ref, AWAY, 0, source_ref)
    collect(home_core_ref, HOME, 1, source_ref)


def second_part_kernel(which, cols_ref, counts_ref, coef_ref, own_ref, *rest):
    part = own_ref.shape[0]
    if which == 0:
        _, away_core_ref, out_ref, source_ref, acc_ref = rest
        collect(away_core_ref, AWAY, 1, source_ref)
    else:
        source_ref, out_ref, acc_ref = rest
    side = lax.axis_index("col")
    near = lax.rem(lax.axis_index("row"), 8) * 2 + side
    scale = exact_scale(source_ref.shape[0], part)

    def place(col):
        piece = lax.shift_right_logical(col * scale, 16)
        return col + part * ((piece ^ near) - piece)

    def start(b):
        return jnp.where(side == which, own_ref[b].astype(jnp.float32), 0.0)

    second_rows(which * part, place, cols_ref, counts_ref, coef_ref, source_ref, start, out_ref, acc_ref)


def second_kernel(cols_ref, counts_ref, coef_ref, own_ref, source_ref, out_ref, acc_ref):
    first = lax.axis_index("col") == 0

    def start(b):
        return jnp.where(first, own_ref[b].astype(jnp.float32), 0.0)

    second_rows(0, lambda col: col, cols_ref, counts_ref, coef_ref, source_ref, start, out_ref, acc_ref)


def choose_kernel(own_ref, crossed_ref, _, home_ref, away_ref):
    owner = lax.div(lax.axis_index("row"), 8) == lax.axis_index("col")

    @pl.when(owner)
    def _():
        home_ref[...] = own_ref[...]
        away_ref[...] = crossed_ref[...]

    @pl.when(jnp.logical_not(owner))
    def _():
        home_ref[...] = crossed_ref[...]
        away_ref[...] = own_ref[...]


def join_kernel(*refs):
    pieces, joined_ref = refs[:-1], refs[-1]
    part = pieces[0].shape[0]
    for i, piece in enumerate(pieces):
        joined_ref[i * part : (i + 1) * part] = piece[...]


def result_kernel(first_row, mine_ref, other_ref, *rest):
    out_ref, sum_ref, sem = rest[-3:]
    sum_ref[...] = (mine_ref[...].astype(jnp.float32) + other_ref[...].astype(jnp.float32)).astype(sum_ref.dtype)
    copy = pltpu.make_async_copy(sum_ref, out_ref.at[pl.ds(first_row, sum_ref.shape[0])], sem)
    copy.start()
    copy.wait()


SMEM = pl.BlockSpec(memory_space=pltpu.SMEM)
VMEM = pl.BlockSpec(memory_space=pltpu.VMEM)
PARAMS = pltpu.CompilerParams(vmem_limit_bytes=VMEM_LIMIT)


def cost(flops, bytes_accessed):
    return pl.CostEstimate(flops=flops, bytes_accessed=bytes_accessed, transcendentals=0)


def in_vmem(array):
    return pltpu.with_memory_space_constraint(array, pltpu.VMEM)


def body(n_row, n_col, blocks, slot_cols, counts, demand, value_added):
    rows, slots, size, _ = blocks.shape
    width = demand.shape[1]
    groups = demand.shape[0] // size
    group_devices = n_row // n_col
    paired = n_col == 2 and n_row == 16 and rows % 2 == 0
    half = rows // 2
    counts = counts.reshape(rows)

    sums, held = pl.pallas_call(
        sums_kernel,
        name="column_sums",
        out_shape=(
            jax.ShapeDtypeStruct((groups, size), jnp.float32),
            pltpu.VMEM(blocks.shape, blocks.dtype),
        ),
        in_specs=[pl.BlockSpec(memory_space=pltpu.HBM)] * 3,
        out_specs=(VMEM, VMEM),
        scratch_shapes=[
            pltpu.VMEM((groups + 1, 8, size), jnp.float32),
            pltpu.SMEM(slot_cols.shape, jnp.int32),
            pltpu.SMEM(counts.shape, jnp.int32),
            pltpu.SemaphoreType.DMA((2,)),
            pltpu.SemaphoreType.DMA((rows, -(-slots // 12))),
        ],
        compiler_params=PARAMS,
        cost_estimate=cost(0, 4 * rows * size * size * slots),
    )(*[pltpu.with_memory_space_constraint(array, pltpu.HBM) for array in (slot_cols, counts, blocks)])

    def flip(array, mask):
        return lax.ppermute(array, "row", [(i, i ^ mask) for i in range(n_row)])

    def swap(array):
        return lax.ppermute(array, "col", [(0, 1), (1, 0)])

    if paired:
        for masks in ((1, 2, 3), (4, 8, 12)):
            sums = sums.astype(jnp.bfloat16)
            parts = [sums] + [flip(sums, m) for m in masks]
            if masks[0] == 4:
                demand = pl.pallas_call(
                    fetch_kernel,
                    name="own_demand",
                    out_shape=pltpu.VMEM(demand.shape, demand.dtype),
                    in_specs=[pl.BlockSpec(memory_space=pltpu.HBM), pl.BlockSpec(memory_space=pl.ANY)],
                    out_specs=VMEM,
                    scratch_shapes=[pltpu.SemaphoreType.DMA],
                    compiler_params=PARAMS,
                    cost_estimate=cost(0, 3 * demand.size * 2),
                )(pltpu.with_memory_space_constraint(demand, pltpu.HBM), sums)
            sums = functools.reduce(jnp.add, [part.astype(jnp.float32) for part in parts])
    else:
        sums = lax.psum(sums, "row")

    def layer_cost(count):
        return cost(2 * count * slots * size * size * width, count * slots * size * size * 2)

    def first_layer(sending, count, dtype, held, earlier=()):
        out = jax.ShapeDtypeStruct((count, size, width), dtype)
        return pl.pallas_call(
            functools.partial(first_kernel, sending),
            name="first_layer",
            out_shape=out if sending else (out, pltpu.VMEM(blocks.shape, blocks.dtype)),
            in_specs=[SMEM, SMEM, VMEM, VMEM, VMEM, VMEM] + [pl.BlockSpec(memory_space=pl.ANY)] * len(earlier),
            out_specs=VMEM if sending else (VMEM, VMEM),
            scratch_shapes=[
                pltpu.VMEM((groups, size), jnp.float32),
                pltpu.VMEM((count, size, width), jnp.float32),
            ],
            input_output_aliases={} if sending else {5: 1},
            compiler_params=PARAMS,
            cost_estimate=layer_cost(count),
        )(
            slot_cols,
            counts,
            sums,
            value_added.reshape(groups, size),
            demand.reshape(groups, size, width),
            in_vmem(held),
            *earlier,
        )

    def second_call(kernel, count, coefs, own, sources, keep_sources):
        dtype = jnp.bfloat16 if paired else jnp.float32
        out = jax.ShapeDtypeStruct((count, size, width), dtype)
        return pl.pallas_call(
            kernel,
            name="second_layer",
            out_shape=(out, pltpu.VMEM((groups, size, width), jnp.bfloat16)) if keep_sources else out,
            input_output_aliases={4: 1} if keep_sources else {},
            in_specs=[SMEM, SMEM] + [VMEM] * (2 + len(sources)),
            out_specs=(VMEM, VMEM) if keep_sources else VMEM,
            scratch_shapes=[pltpu.VMEM((count, size, width), jnp.float32)],
            compiler_params=PARAMS,
            cost_estimate=layer_cost(count),
        )(slot_cols, counts, in_vmem(coefs), own, *sources)

    if not paired:
        group = lax.axis_index("col")
        partial, coefs = first_layer(None, rows, jnp.float32, held)
        layer_one = lax.psum(partial, "col").astype(jnp.bfloat16)
        gathered = lax.all_gather(layer_one, "row", axis=0, tiled=True)
        source = lax.dynamic_slice_in_dim(gathered, group * groups, groups, 0)
        partial = second_call(second_kernel, rows, coefs, layer_one, [source], False)
        return lax.psum(partial, "col").astype(jnp.bfloat16).reshape(rows * size, width)

    sent = first_layer(True, half, jnp.bfloat16, held)
    arrived = swap(sent)
    kept, coefs = first_layer(False, half, jnp.float32, held, [sent])
    coefs, token = pl.pallas_call(
        functools.partial(scale_kernel, half),
        name="own_coefficients",
        out_shape=(pltpu.VMEM(blocks.shape, blocks.dtype), jax.ShapeDtypeStruct((8, size), jnp.float32)),
        in_specs=[SMEM, SMEM, VMEM, VMEM, VMEM],
        out_specs=(VMEM, VMEM),
        scratch_shapes=[pltpu.VMEM((groups, size), jnp.float32)],
        input_output_aliases={4: 0},
        compiler_params=PARAMS,
        cost_estimate=layer_cost(half),
    )(slot_cols, counts, sums, value_added.reshape(groups, size), in_vmem(coefs))
    own = (kept + arrived.astype(jnp.float32)).astype(jnp.bfloat16)

    piece = jax.ShapeDtypeStruct(own.shape, own.dtype)
    home, away = pl.pallas_call(
        choose_kernel,
        name="home_and_away",
        out_shape=(piece, piece),
        in_specs=[VMEM] * 3,
        out_specs=(VMEM, VMEM),
        compiler_params=PARAMS,
    )(own, flip(own, group_devices), token)

    def join(pieces):
        return pl.pallas_call(
            join_kernel,
            name="own_joined",
            out_shape=jax.ShapeDtypeStruct((len(pieces) * half, size, width), own.dtype),
            in_specs=[VMEM] * len(pieces),
            out_specs=VMEM,
            compiler_params=PARAMS,
        )(*pieces)

    away = swap(away)
    home, away = [join([part] + [flip(part, mask) for mask in (2, 4, 6)]) for part in (home, away)]
    home_core, away_core = flip(home, 1), flip(away, 1)
    source = pl.pallas_call(
        collect_kernel,
        name="own_collected",
        out_shape=pltpu.VMEM((groups, size, width), jnp.bfloat16),
        in_specs=[VMEM] * 3,
        out_specs=VMEM,
        compiler_params=PARAMS,
        cost_estimate=cost(0, 2 * groups * size * width * 2),
    )(home, away, home_core)

    part_a, source = second_call(
        functools.partial(second_part_kernel, 0), half, coefs, own, [in_vmem(source), away_core], True
    )
    other_a = swap(part_a)
    part_b = second_call(functools.partial(second_part_kernel, 1), half, coefs, own, [in_vmem(source)], False)
    other_b = swap(part_b)

    def result(first_row, inputs):
        return pl.pallas_call(
            functools.partial(result_kernel, first_row),
            name="result",
            out_shape=jax.ShapeDtypeStruct((rows, size, width), jnp.bfloat16),
            in_specs=[VMEM, VMEM] + [pl.BlockSpec(memory_space=pltpu.HBM)] * (len(inputs) - 2),
            out_specs=pl.BlockSpec(memory_space=pltpu.HBM),
            scratch_shapes=[pltpu.VMEM(piece.shape, piece.dtype), pltpu.SemaphoreType.DMA],
            input_output_aliases={2: 0} if len(inputs) > 2 else {},
            compiler_params=PARAMS,
        )(*inputs)

    out = result(0, [part_a, other_a])
    return result(half, [part_b, other_b, out]).reshape(rows * size, width)


def solution(mesh):
    return jax.shard_map(
        functools.partial(body, mesh.shape["row"], mesh.shape["col"]),
        mesh=mesh,
        in_specs=(
            P("row", "col", None, None),
            P("row", "col"),
            P("row", "col"),
            P("col", None),
            P("col"),
        ),
        out_specs=P("row", None),
        check_vma=False,
    )
```

```python
import functools

import jax
import jax.numpy as jnp
from jax import lax
from jax.experimental import pallas as pl
from jax.experimental.pallas import tpu as pltpu
from jax.sharding import PartitionSpec as P

VMEM_LIMIT = 12 * 1024 * 1024


def slot_ranges(slots):
    first = min(12, slots)
    return [range(first)] + ([range(first, slots)] if slots > first else [])


def sums_kernel(cols_hbm, counts_hbm, blocks_ref, sums_ref, held_ref, acc_ref, cols_ref, counts_ref, list_sems, sems):
    rows, slots, size, _ = blocks_ref.shape
    groups = acc_ref.shape[0] - 1
    first, *others = slot_ranges(slots)
    others = [range(start, min(start + 12, slots)) for other in others for start in range(other.start, slots, 12)]

    def fetch(b, part):
        span = pl.ds(part.start, len(part))
        return pltpu.make_async_copy(blocks_ref.at[b, span], held_ref.at[b, span], sems.at[b, part.start // 12])

    counts_copy = pltpu.make_async_copy(counts_hbm, counts_ref, list_sems.at[0])
    cols_copy = pltpu.make_async_copy(cols_hbm, cols_ref, list_sems.at[1])
    counts_copy.start()
    cols_copy.start()
    for b in range(rows):
        fetch(b, first).start()
    acc_ref[...] = jnp.zeros_like(acc_ref)
    counts_copy.wait()
    cols_copy.wait()
    def for_heavy_rows(action):
        def one_row(b, carry):
            @pl.when(counts_ref[b] > len(first))
            def _():
                for part in others:
                    action(b, part)

            return carry

        if others:
            lax.fori_loop(0, rows, one_row, 0)

    def add(b, part):
        fetch(b, part).wait()
        for slot in part:
            col = jnp.where(slot < counts_ref[b], cols_ref[b, slot], groups)
            block = held_ref[b, slot].astype(jnp.float32)
            acc_ref[col] += jnp.sum(block.reshape(size // 8, 8, size), axis=0)

    def add_first(b, carry):
        add(b, first)
        return carry

    for_heavy_rows(lambda b, part: fetch(b, part).start())
    lax.fori_loop(0, rows, add_first, 0)
    for_heavy_rows(add)
    sums_ref[...] = jnp.sum(acc_ref[:groups], axis=1)


def multiply_rows(rows, counts_ref, slots, start, gather, acc_ref):
    first, *others = slot_ranges(slots)

    def product(row, part):
        left, right = zip(*[gather(row, slot) for slot in part])
        return jnp.dot(jnp.concatenate(left, axis=1), jnp.concatenate(right, axis=0), preferred_element_type=jnp.float32)

    for b, row in enumerate(rows):
        acc_ref[b] = start(b) + product(row, first)
    def one_row(b, carry):
        row = rows[0] + b
        for part in others:

            @pl.when(counts_ref[row] > part.start)
            def _():
                acc_ref[b] += product(row, part)

        return carry

    if others:
        lax.fori_loop(0, len(rows), one_row, 0)


def scaled_block(row, slot, cols_ref, counts_ref, inverse_ref, blocks_ref):
    size = blocks_ref.shape[2]
    scale = jnp.where(slot < counts_ref[row], inverse_ref[pl.ds(cols_ref[row, slot], 1), :], 0.0)
    scale = jnp.broadcast_to(scale, (16, size)).astype(jnp.bfloat16)
    return (blocks_ref[row, slot].reshape(size // 16, 16, size) * scale).reshape(size, size)


def first_row(sending, count):
    if sending is None:
        return 0
    side = lax.axis_index("col")
    return (1 - side if sending else side) * count


def first_kernel(sending, cols_ref, counts_ref, sums_ref, added_ref, demand_ref, blocks_ref, *rest):
    inverse_ref, acc_ref = rest[-2:]
    if sending:
        out_ref, coef_ref = rest[-3], None
    else:
        out_ref, coef_ref = rest[-4:-2]
    slots = blocks_ref.shape[1]
    count = out_ref.shape[0]
    inverse_ref[...] = 1.0 / (sums_ref[...] + added_ref[...])

    def gather(row, slot):
        coef = scaled_block(row, slot, cols_ref, counts_ref, inverse_ref, blocks_ref)
        if coef_ref is not None:
            coef_ref[row, slot] = coef
        return coef, demand_ref[cols_ref[row, slot]]

    rows = [first_row(sending, count) + b for b in range(count)]
    multiply_rows(rows, counts_ref, slots, lambda b: 0.0, gather, acc_ref)
    out_ref[...] = acc_ref[...].astype(out_ref.dtype)


def scale_kernel(count, cols_ref, counts_ref, sums_ref, added_ref, blocks_ref, coef_ref, token_ref, inverse_ref):
    first, *others = slot_ranges(blocks_ref.shape[1])
    inverse_ref[...] = 1.0 / (sums_ref[...] + added_ref[...])
    token_ref[...] = inverse_ref[:8]

    def scale(row, part):
        for slot in part:
            coef_ref[row, slot] = scaled_block(row, slot, cols_ref, counts_ref, inverse_ref, blocks_ref)

    rows = [first_row(True, count) + b for b in range(count)]
    for row in rows:
        scale(row, first)
    def one_row(b, carry):
        row = rows[0] + b
        for part in others:

            @pl.when(counts_ref[row] > part.start)
            def _():
                scale(row, part)

        return carry

    if others:
        lax.fori_loop(0, len(rows), one_row, 0)


def fetch_kernel(demand_hbm, _, demand_ref, sem):
    copy = pltpu.make_async_copy(demand_hbm, demand_ref, sem)
    copy.start()
    copy.wait()


def second_rows(first_row, place, cols_ref, counts_ref, coef_ref, source_ref, start, out_ref, acc_ref):
    slots = coef_ref.shape[1]

    def gather(row, slot):
        return coef_ref[row, slot], source_ref[place(cols_ref[row, slot])]

    rows = [first_row + b for b in range(out_ref.shape[0])]
    multiply_rows(rows, counts_ref, slots, start, gather, acc_ref)
    out_ref[...] = acc_ref[...].astype(out_ref.dtype)


def exact_scale(count, part):
    scale = -(-(1 << 16) // part)
    assert all((i * scale) >> 16 == i // part for i in range(count))
    return scale


HOME = ((0, 0, 0), (0, 1, 0), (1, 0, 0), (1, 1, 0))
AWAY = ((0, 0, 1), (0, 1, 1), (1, 0, 1), (1, 1, 1))


def collect(array, places, core, source_ref):
    part = array.shape[0] // len(places)
    for i, (z, y, away) in enumerate(places):
        at = ((z * 4 + y * 2 + core) * 2 + away) * part
        source_ref[at : at + part] = array[i * part : (i + 1) * part]


def collect_kernel(home_ref, away_ref, home_core_ref, source_ref):
    collect(home_ref, HOME, 0, source_ref)
    collect(away_ref, AWAY, 0, source_ref)
    collect(home_core_ref, HOME, 1, source_ref)


def second_part_kernel(which, cols_ref, counts_ref, coef_ref, own_ref, *rest):
    part = own_ref.shape[0]
    if which == 0:
        _, away_core_ref, out_ref, source_ref, acc_ref = rest
        collect(away_core_ref, AWAY, 1, source_ref)
    else:
        source_ref, out_ref, acc_ref = rest
    side = lax.axis_index("col")
    near = lax.rem(lax.axis_index("row"), 8) * 2 + side
    scale = exact_scale(source_ref.shape[0], part)

    def place(col):
        piece = lax.shift_right_logical(col * scale, 16)
        return col + part * ((piece ^ near) - piece)

    def start(b):
        return jnp.where(side == which, own_ref[b].astype(jnp.float32), 0.0)

    second_rows(which * part, place, cols_ref, counts_ref, coef_ref, source_ref, start, out_ref, acc_ref)


def second_kernel(cols_ref, counts_ref, coef_ref, own_ref, source_ref, out_ref, acc_ref):
    first = lax.axis_index("col") == 0

    def start(b):
        return jnp.where(first, own_ref[b].astype(jnp.float32), 0.0)

    second_rows(0, lambda col: col, cols_ref, counts_ref, coef_ref, source_ref, start, out_ref, acc_ref)


def choose_kernel(own_ref, crossed_ref, _, home_ref, away_ref):
    owner = lax.div(lax.axis_index("row"), 8) == lax.axis_index("col")

    @pl.when(owner)
    def _():
        home_ref[...] = own_ref[...]
        away_ref[...] = crossed_ref[...]

    @pl.when(jnp.logical_not(owner))
    def _():
        home_ref[...] = crossed_ref[...]
        away_ref[...] = own_ref[...]


def join_kernel(*refs):
    pieces, joined_ref = refs[:-1], refs[-1]
    part = pieces[0].shape[0]
    for i, piece in enumerate(pieces):
        joined_ref[i * part : (i + 1) * part] = piece[...]


def result_kernel(first_row, mine_ref, other_ref, *rest):
    out_ref, sum_ref, sem = rest[-3:]
    sum_ref[...] = (mine_ref[...].astype(jnp.float32) + other_ref[...].astype(jnp.float32)).astype(sum_ref.dtype)
    copy = pltpu.make_async_copy(sum_ref, out_ref.at[pl.ds(first_row, sum_ref.shape[0])], sem)
    copy.start()
    copy.wait()


SMEM = pl.BlockSpec(memory_space=pltpu.SMEM)
VMEM = pl.BlockSpec(memory_space=pltpu.VMEM)
PARAMS = pltpu.CompilerParams(vmem_limit_bytes=VMEM_LIMIT)


def cost(flops, bytes_accessed):
    return pl.CostEstimate(flops=flops, bytes_accessed=bytes_accessed, transcendentals=0)


def in_vmem(array):
    return pltpu.with_memory_space_constraint(array, pltpu.VMEM)


def body(n_row, n_col, blocks, slot_cols, counts, demand, value_added):
    rows, slots, size, _ = blocks.shape
    width = demand.shape[1]
    groups = demand.shape[0] // size
    group_devices = n_row // n_col
    paired = n_col == 2 and n_row == 16 and rows % 2 == 0
    half = rows // 2
    counts = counts.reshape(rows)

    sums, held = pl.pallas_call(
        sums_kernel,
        name="column_sums",
        out_shape=(
            jax.ShapeDtypeStruct((groups, size), jnp.float32),
            pltpu.VMEM(blocks.shape, blocks.dtype),
        ),
        in_specs=[pl.BlockSpec(memory_space=pltpu.HBM)] * 3,
        out_specs=(VMEM, VMEM),
        scratch_shapes=[
            pltpu.VMEM((groups + 1, 8, size), jnp.float32),
            pltpu.SMEM(slot_cols.shape, jnp.int32),
            pltpu.SMEM(counts.shape, jnp.int32),
            pltpu.SemaphoreType.DMA((2,)),
            pltpu.SemaphoreType.DMA((rows, -(-slots // 12))),
        ],
        compiler_params=PARAMS,
        cost_estimate=cost(0, 4 * rows * size * size * slots),
    )(*[pltpu.with_memory_space_constraint(array, pltpu.HBM) for array in (slot_cols, counts, blocks)])

    def flip(array, mask):
        return lax.ppermute(array, "row", [(i, i ^ mask) for i in range(n_row)])

    def swap(array):
        return lax.ppermute(array, "col", [(0, 1), (1, 0)])

    if paired:
        for masks in ((1, 2, 3), (4, 12, 8)):
            sums = sums.astype(jnp.bfloat16)
            parts = [sums] + [flip(sums, m) for m in masks]
            if masks[0] == 4:
                demand = pl.pallas_call(
                    fetch_kernel,
                    name="own_demand",
                    out_shape=pltpu.VMEM(demand.shape, demand.dtype),
                    in_specs=[pl.BlockSpec(memory_space=pltpu.HBM), pl.BlockSpec(memory_space=pl.ANY)],
                    out_specs=VMEM,
                    scratch_shapes=[pltpu.SemaphoreType.DMA],
                    compiler_params=PARAMS,
                    cost_estimate=cost(0, 3 * demand.size * 2),
                )(pltpu.with_memory_space_constraint(demand, pltpu.HBM), sums)
            sums = functools.reduce(jnp.add, [part.astype(jnp.float32) for part in parts])
    else:
        sums = lax.psum(sums, "row")

    def layer_cost(count):
        return cost(2 * count * slots * size * size * width, count * slots * size * size * 2)

    def first_layer(sending, count, dtype, held, earlier=()):
        out = jax.ShapeDtypeStruct((count, size, width), dtype)
        return pl.pallas_call(
            functools.partial(first_kernel, sending),
            name="first_layer",
            out_shape=out if sending else (out, pltpu.VMEM(blocks.shape, blocks.dtype)),
            in_specs=[SMEM, SMEM, VMEM, VMEM, VMEM, VMEM] + [pl.BlockSpec(memory_space=pl.ANY)] * len(earlier),
            out_specs=VMEM if sending else (VMEM, VMEM),
            scratch_shapes=[
                pltpu.VMEM((groups, size), jnp.float32),
                pltpu.VMEM((count, size, width), jnp.float32),
            ],
            input_output_aliases={} if sending else {5: 1},
            compiler_params=PARAMS,
            cost_estimate=layer_cost(count),
        )(
            slot_cols,
            counts,
            sums,
            value_added.reshape(groups, size),
            demand.reshape(groups, size, width),
            in_vmem(held),
            *earlier,
        )

    def second_call(kernel, count, coefs, own, sources, keep_sources):
        dtype = jnp.bfloat16 if paired else jnp.float32
        out = jax.ShapeDtypeStruct((count, size, width), dtype)
        return pl.pallas_call(
            kernel,
            name="second_layer",
            out_shape=(out, pltpu.VMEM((groups, size, width), jnp.bfloat16)) if keep_sources else out,
            input_output_aliases={4: 1} if keep_sources else {},
            in_specs=[SMEM, SMEM] + [VMEM] * (2 + len(sources)),
            out_specs=(VMEM, VMEM) if keep_sources else VMEM,
            scratch_shapes=[pltpu.VMEM((count, size, width), jnp.float32)],
            compiler_params=PARAMS,
            cost_estimate=layer_cost(count),
        )(slot_cols, counts, in_vmem(coefs), own, *sources)

    if not paired:
        group = lax.axis_index("col")
        partial, coefs = first_layer(None, rows, jnp.float32, held)
        layer_one = lax.psum(partial, "col").astype(jnp.bfloat16)
        gathered = lax.all_gather(layer_one, "row", axis=0, tiled=True)
        source = lax.dynamic_slice_in_dim(gathered, group * groups, groups, 0)
        partial = second_call(second_kernel, rows, coefs, layer_one, [source], False)
        return lax.psum(partial, "col").astype(jnp.bfloat16).reshape(rows * size, width)

    sent = first_layer(True, half, jnp.bfloat16, held)
    arrived = swap(sent)
    kept, coefs = first_layer(False, half, jnp.float32, held, [sent])
    coefs, token = pl.pallas_call(
        functools.partial(scale_kernel, half),
        name="own_coefficients",
        out_shape=(pltpu.VMEM(blocks.shape, blocks.dtype), jax.ShapeDtypeStruct((8, size), jnp.float32)),
        in_specs=[SMEM, SMEM, VMEM, VMEM, VMEM],
        out_specs=(VMEM, VMEM),
        scratch_shapes=[pltpu.VMEM((groups, size), jnp.float32)],
        input_output_aliases={4: 0},
        compiler_params=PARAMS,
        cost_estimate=layer_cost(half),
    )(slot_cols, counts, sums, value_added.reshape(groups, size), in_vmem(coefs))
    own = (kept + arrived.astype(jnp.float32)).astype(jnp.bfloat16)

    piece = jax.ShapeDtypeStruct(own.shape, own.dtype)
    home, away = pl.pallas_call(
        choose_kernel,
        name="home_and_away",
        out_shape=(piece, piece),
        in_specs=[VMEM] * 3,
        out_specs=(VMEM, VMEM),
        compiler_params=PARAMS,
    )(own, flip(own, group_devices), token)

    def join(pieces):
        return pl.pallas_call(
            join_kernel,
            name="own_joined",
            out_shape=jax.ShapeDtypeStruct((len(pieces) * half, size, width), own.dtype),
            in_specs=[VMEM] * len(pieces),
            out_specs=VMEM,
            compiler_params=PARAMS,
        )(*pieces)

    away = swap(away)
    home, away = [join([part] + [flip(part, mask) for mask in (2, 4, 6)]) for part in (home, away)]
    home_core, away_core = flip(home, 1), flip(away, 1)
    source = pl.pallas_call(
        collect_kernel,
        name="own_collected",
        out_shape=pltpu.VMEM((groups, size, width), jnp.bfloat16),
        in_specs=[VMEM] * 3,
        out_specs=VMEM,
        compiler_params=PARAMS,
        cost_estimate=cost(0, 2 * groups * size * width * 2),
    )(home, away, home_core)

    part_a, source = second_call(
        functools.partial(second_part_kernel, 0), half, coefs, own, [in_vmem(source), away_core], True
    )
    other_a = swap(part_a)
    part_b = second_call(functools.partial(second_part_kernel, 1), half, coefs, own, [in_vmem(source)], False)
    other_b = swap(part_b)

    def result(first_row, inputs):
        return pl.pallas_call(
            functools.partial(result_kernel, first_row),
            name="result",
            out_shape=jax.ShapeDtypeStruct((rows, size, width), jnp.bfloat16),
            in_specs=[VMEM, VMEM] + [pl.BlockSpec(memory_space=pltpu.HBM)] * (len(inputs) - 2),
            out_specs=pl.BlockSpec(memory_space=pltpu.HBM),
            scratch_shapes=[pltpu.VMEM(piece.shape, piece.dtype), pltpu.SemaphoreType.DMA],
            input_output_aliases={2: 0} if len(inputs) > 2 else {},
            compiler_params=PARAMS,
        )(*inputs)

    out = result(0, [part_a, other_a])
    return result(half, [part_b, other_b, out]).reshape(rows * size, width)


def solution(mesh):
    return jax.shard_map(
        functools.partial(body, mesh.shape["row"], mesh.shape["col"]),
        mesh=mesh,
        in_specs=(
            P("row", "col", None, None),
            P("row", "col"),
            P("row", "col"),
            P("col", None),
            P("col"),
        ),
        out_specs=P("row", None),
        check_vma=False,
    )
```

```python
import functools

import jax
import jax.numpy as jnp
from jax import lax
from jax.experimental import pallas as pl
from jax.experimental.pallas import tpu as pltpu
from jax.sharding import PartitionSpec as P

VMEM_LIMIT = 12 * 1024 * 1024


def slot_ranges(slots):
    first = min(12, slots)
    return [range(first)] + ([range(first, slots)] if slots > first else [])


def sums_kernel(cols_hbm, counts_hbm, blocks_ref, sums_ref, held_ref, acc_ref, cols_ref, counts_ref, list_sems, sems):
    rows, slots, size, _ = blocks_ref.shape
    groups = acc_ref.shape[0] - 1
    first, *others = slot_ranges(slots)
    others = [range(start, min(start + 12, slots)) for other in others for start in range(other.start, slots, 12)]

    def fetch(b, part):
        span = pl.ds(part.start, len(part))
        return pltpu.make_async_copy(blocks_ref.at[b, span], held_ref.at[b, span], sems.at[b, part.start // 12])

    counts_copy = pltpu.make_async_copy(counts_hbm, counts_ref, list_sems.at[0])
    cols_copy = pltpu.make_async_copy(cols_hbm, cols_ref, list_sems.at[1])
    counts_copy.start()
    cols_copy.start()
    for b in range(rows):
        fetch(b, first).start()
    acc_ref[...] = jnp.zeros_like(acc_ref)
    counts_copy.wait()
    cols_copy.wait()
    def for_heavy_rows(action):
        def one_row(b, carry):
            @pl.when(counts_ref[b] > len(first))
            def _():
                for part in others:
                    action(b, part)

            return carry

        if others:
            lax.fori_loop(0, rows, one_row, 0)

    def add(b, part):
        fetch(b, part).wait()
        for slot in part:
            col = jnp.where(slot < counts_ref[b], cols_ref[b, slot], groups)
            block = held_ref[b, slot].astype(jnp.float32)
            acc_ref[col] += jnp.sum(block.reshape(size // 8, 8, size), axis=0)

    def add_first(b, carry):
        add(b, first)
        return carry

    for_heavy_rows(lambda b, part: fetch(b, part).start())
    lax.fori_loop(0, rows, add_first, 0)
    for_heavy_rows(add)
    sums_ref[...] = jnp.sum(acc_ref[:groups], axis=1)


def multiply_rows(rows, counts_ref, slots, start, gather, acc_ref):
    first, *others = slot_ranges(slots)

    def product(row, part):
        left, right = zip(*[gather(row, slot) for slot in part])
        return jnp.dot(jnp.concatenate(left, axis=1), jnp.concatenate(right, axis=0), preferred_element_type=jnp.float32)

    for b, row in enumerate(rows):
        acc_ref[b] = start(b) + product(row, first)
    def one_row(b, carry):
        row = rows[0] + b
        for part in others:

            @pl.when(counts_ref[row] > part.start)
            def _():
                acc_ref[b] += product(row, part)

        return carry

    if others:
        lax.fori_loop(0, len(rows), one_row, 0)


def scaled_block(row, slot, cols_ref, counts_ref, inverse_ref, blocks_ref):
    size = blocks_ref.shape[2]
    scale = jnp.where(slot < counts_ref[row], inverse_ref[pl.ds(cols_ref[row, slot], 1), :], 0.0)
    scale = jnp.broadcast_to(scale, (16, size)).astype(jnp.bfloat16)
    return (blocks_ref[row, slot].reshape(size // 16, 16, size) * scale).reshape(size, size)


def first_row(sending, count):
    if sending is None:
        return 0
    side = lax.axis_index("col")
    return (1 - side if sending else side) * count


def first_kernel(sending, cols_ref, counts_ref, sums_ref, added_ref, demand_ref, blocks_ref, *rest):
    inverse_ref, acc_ref = rest[-2:]
    if sending:
        out_ref, coef_ref = rest[-3], None
    else:
        out_ref, coef_ref = rest[-4:-2]
    slots = blocks_ref.shape[1]
    count = out_ref.shape[0]
    inverse_ref[...] = 1.0 / (sums_ref[...] + added_ref[...])

    def gather(row, slot):
        coef = scaled_block(row, slot, cols_ref, counts_ref, inverse_ref, blocks_ref)
        if coef_ref is not None:
            coef_ref[row, slot] = coef
        return coef, demand_ref[cols_ref[row, slot]]

    rows = [first_row(sending, count) + b for b in range(count)]
    multiply_rows(rows, counts_ref, slots, lambda b: 0.0, gather, acc_ref)
    out_ref[...] = acc_ref[...].astype(out_ref.dtype)


def scale_kernel(count, cols_ref, counts_ref, sums_ref, added_ref, blocks_ref, coef_ref, token_ref, inverse_ref):
    first, *others = slot_ranges(blocks_ref.shape[1])
    inverse_ref[...] = 1.0 / (sums_ref[...] + added_ref[...])
    token_ref[...] = inverse_ref[:8]

    def scale(row, part):
        for slot in part:
            coef_ref[row, slot] = scaled_block(row, slot, cols_ref, counts_ref, inverse_ref, blocks_ref)

    rows = [first_row(True, count) + b for b in range(count)]
    def one_row(b, carry):
        row = rows[0] + b
        scale(row, first)
        for part in others:

            @pl.when(counts_ref[row] > part.start)
            def _():
                scale(row, part)

        return carry

    lax.fori_loop(0, len(rows), one_row, 0)


def fetch_kernel(demand_hbm, _, demand_ref, sem):
    copy = pltpu.make_async_copy(demand_hbm, demand_ref, sem)
    copy.start()
    copy.wait()


def second_rows(first_row, place, cols_ref, counts_ref, coef_ref, source_ref, start, out_ref, acc_ref):
    slots = coef_ref.shape[1]

    def gather(row, slot):
        return coef_ref[row, slot], source_ref[place(cols_ref[row, slot])]

    rows = [first_row + b for b in range(out_ref.shape[0])]
    multiply_rows(rows, counts_ref, slots, start, gather, acc_ref)
    out_ref[...] = acc_ref[...].astype(out_ref.dtype)


def exact_scale(count, part):
    scale = -(-(1 << 16) // part)
    assert all((i * scale) >> 16 == i // part for i in range(count))
    return scale


HOME = ((0, 0, 0), (0, 1, 0), (1, 0, 0), (1, 1, 0))
AWAY = ((0, 0, 1), (0, 1, 1), (1, 0, 1), (1, 1, 1))


def collect(array, places, core, source_ref):
    part = array.shape[0] // len(places)
    for i, (z, y, away) in enumerate(places):
        at = ((z * 4 + y * 2 + core) * 2 + away) * part
        source_ref[at : at + part] = array[i * part : (i + 1) * part]


def collect_kernel(home_ref, away_ref, home_core_ref, source_ref):
    collect(home_ref, HOME, 0, source_ref)
    collect(away_ref, AWAY, 0, source_ref)
    collect(home_core_ref, HOME, 1, source_ref)


def second_part_kernel(which, cols_ref, counts_ref, coef_ref, own_ref, *rest):
    part = own_ref.shape[0]
    if which == 0:
        _, away_core_ref, out_ref, source_ref, acc_ref = rest
        collect(away_core_ref, AWAY, 1, source_ref)
    else:
        source_ref, out_ref, acc_ref = rest
    side = lax.axis_index("col")
    near = lax.rem(lax.axis_index("row"), 8) * 2 + side
    scale = exact_scale(source_ref.shape[0], part)

    def place(col):
        piece = lax.shift_right_logical(col * scale, 16)
        return col + part * ((piece ^ near) - piece)

    def start(b):
        return jnp.where(side == which, own_ref[b].astype(jnp.float32), 0.0)

    second_rows(which * part, place, cols_ref, counts_ref, coef_ref, source_ref, start, out_ref, acc_ref)


def second_kernel(cols_ref, counts_ref, coef_ref, own_ref, source_ref, out_ref, acc_ref):
    first = lax.axis_index("col") == 0

    def start(b):
        return jnp.where(first, own_ref[b].astype(jnp.float32), 0.0)

    second_rows(0, lambda col: col, cols_ref, counts_ref, coef_ref, source_ref, start, out_ref, acc_ref)


def choose_kernel(own_ref, crossed_ref, home_ref, away_ref):
    owner = lax.div(lax.axis_index("row"), 8) == lax.axis_index("col")

    @pl.when(owner)
    def _():
        home_ref[...] = own_ref[...]
        away_ref[...] = crossed_ref[...]

    @pl.when(jnp.logical_not(owner))
    def _():
        home_ref[...] = crossed_ref[...]
        away_ref[...] = own_ref[...]


def join_kernel(*refs):
    pieces, joined_ref = refs[:4], refs[-1]
    part = pieces[0].shape[0]
    for i, piece in enumerate(pieces):
        joined_ref[i * part : (i + 1) * part] = piece[...]


def result_kernel(first_row, mine_ref, other_ref, *rest):
    out_ref, sum_ref, sem = rest[-3:]
    sum_ref[...] = (mine_ref[...].astype(jnp.float32) + other_ref[...].astype(jnp.float32)).astype(sum_ref.dtype)
    copy = pltpu.make_async_copy(sum_ref, out_ref.at[pl.ds(first_row, sum_ref.shape[0])], sem)
    copy.start()
    copy.wait()


SMEM = pl.BlockSpec(memory_space=pltpu.SMEM)
VMEM = pl.BlockSpec(memory_space=pltpu.VMEM)
PARAMS = pltpu.CompilerParams(vmem_limit_bytes=VMEM_LIMIT)


def cost(flops, bytes_accessed):
    return pl.CostEstimate(flops=flops, bytes_accessed=bytes_accessed, transcendentals=0)


def in_vmem(array):
    return pltpu.with_memory_space_constraint(array, pltpu.VMEM)


def body(n_row, n_col, blocks, slot_cols, counts, demand, value_added):
    rows, slots, size, _ = blocks.shape
    width = demand.shape[1]
    groups = demand.shape[0] // size
    group_devices = n_row // n_col
    paired = n_col == 2 and n_row == 16 and rows % 2 == 0
    half = rows // 2
    counts = counts.reshape(rows)

    sums, held = pl.pallas_call(
        sums_kernel,
        name="column_sums",
        out_shape=(
            jax.ShapeDtypeStruct((groups, size), jnp.float32),
            pltpu.VMEM(blocks.shape, blocks.dtype),
        ),
        in_specs=[pl.BlockSpec(memory_space=pltpu.HBM)] * 3,
        out_specs=(VMEM, VMEM),
        scratch_shapes=[
            pltpu.VMEM((groups + 1, 8, size), jnp.float32),
            pltpu.SMEM(slot_cols.shape, jnp.int32),
            pltpu.SMEM(counts.shape, jnp.int32),
            pltpu.SemaphoreType.DMA((2,)),
            pltpu.SemaphoreType.DMA((rows, -(-slots // 12))),
        ],
        compiler_params=PARAMS,
        cost_estimate=cost(0, 4 * rows * size * size * slots),
    )(*[pltpu.with_memory_space_constraint(array, pltpu.HBM) for array in (slot_cols, counts, blocks)])

    def flip(array, mask):
        return lax.ppermute(array, "row", [(i, i ^ mask) for i in range(n_row)])

    def swap(array):
        return lax.ppermute(array, "col", [(0, 1), (1, 0)])

    if paired:
        for masks in ((1, 2, 3), (4, 12, 8)):
            sums = sums.astype(jnp.bfloat16)
            parts = [sums] + [flip(sums, m) for m in masks]
            if masks[0] == 4:
                demand = pl.pallas_call(
                    fetch_kernel,
                    name="own_demand",
                    out_shape=pltpu.VMEM(demand.shape, demand.dtype),
                    in_specs=[pl.BlockSpec(memory_space=pltpu.HBM), pl.BlockSpec(memory_space=pl.ANY)],
                    out_specs=VMEM,
                    scratch_shapes=[pltpu.SemaphoreType.DMA],
                    compiler_params=PARAMS,
                    cost_estimate=cost(0, 3 * demand.size * 2),
                )(pltpu.with_memory_space_constraint(demand, pltpu.HBM), sums)
            sums = functools.reduce(jnp.add, [part.astype(jnp.float32) for part in parts])
    else:
        sums = lax.psum(sums, "row")

    def layer_cost(count):
        return cost(2 * count * slots * size * size * width, count * slots * size * size * 2)

    def first_layer(sending, count, dtype, held, earlier=()):
        out = jax.ShapeDtypeStruct((count, size, width), dtype)
        return pl.pallas_call(
            functools.partial(first_kernel, sending),
            name="first_layer",
            out_shape=out if sending else (out, pltpu.VMEM(blocks.shape, blocks.dtype)),
            in_specs=[SMEM, SMEM, VMEM, VMEM, VMEM, VMEM] + [pl.BlockSpec(memory_space=pl.ANY)] * len(earlier),
            out_specs=VMEM if sending else (VMEM, VMEM),
            scratch_shapes=[
                pltpu.VMEM((groups, size), jnp.float32),
                pltpu.VMEM((count, size, width), jnp.float32),
            ],
            input_output_aliases={} if sending else {5: 1},
            compiler_params=PARAMS,
            cost_estimate=layer_cost(count),
        )(
            slot_cols,
            counts,
            sums,
            value_added.reshape(groups, size),
            demand.reshape(groups, size, width),
            in_vmem(held),
            *earlier,
        )

    def second_call(kernel, count, coefs, own, sources, keep_sources):
        dtype = jnp.bfloat16 if paired else jnp.float32
        out = jax.ShapeDtypeStruct((count, size, width), dtype)
        return pl.pallas_call(
            kernel,
            name="second_layer",
            out_shape=(out, pltpu.VMEM((groups, size, width), jnp.bfloat16)) if keep_sources else out,
            input_output_aliases={4: 1} if keep_sources else {},
            in_specs=[SMEM, SMEM] + [VMEM] * (2 + len(sources)),
            out_specs=(VMEM, VMEM) if keep_sources else VMEM,
            scratch_shapes=[pltpu.VMEM((count, size, width), jnp.float32)],
            compiler_params=PARAMS,
            cost_estimate=layer_cost(count),
        )(slot_cols, counts, in_vmem(coefs), own, *sources)

    if not paired:
        group = lax.axis_index("col")
        partial, coefs = first_layer(None, rows, jnp.float32, held)
        layer_one = lax.psum(partial, "col").astype(jnp.bfloat16)
        gathered = lax.all_gather(layer_one, "row", axis=0, tiled=True)
        source = lax.dynamic_slice_in_dim(gathered, group * groups, groups, 0)
        partial = second_call(second_kernel, rows, coefs, layer_one, [source], False)
        return lax.psum(partial, "col").astype(jnp.bfloat16).reshape(rows * size, width)

    sent = first_layer(True, half, jnp.bfloat16, held)
    arrived = swap(sent)
    kept, coefs = first_layer(False, half, jnp.float32, held, [sent])
    coefs, token = pl.pallas_call(
        functools.partial(scale_kernel, half),
        name="own_coefficients",
        out_shape=(pltpu.VMEM(blocks.shape, blocks.dtype), jax.ShapeDtypeStruct((8, size), jnp.float32)),
        in_specs=[SMEM, SMEM, VMEM, VMEM, VMEM],
        out_specs=(VMEM, VMEM),
        scratch_shapes=[pltpu.VMEM((groups, size), jnp.float32)],
        input_output_aliases={4: 0},
        compiler_params=PARAMS,
        cost_estimate=layer_cost(half),
    )(slot_cols, counts, sums, value_added.reshape(groups, size), in_vmem(coefs))
    own = (kept + arrived.astype(jnp.float32)).astype(jnp.bfloat16)

    piece = jax.ShapeDtypeStruct(own.shape, own.dtype)
    home, away = pl.pallas_call(
        choose_kernel,
        name="home_and_away",
        out_shape=(piece, piece),
        in_specs=[VMEM] * 2,
        out_specs=(VMEM, VMEM),
        compiler_params=PARAMS,
    )(own, flip(own, group_devices))

    def join(pieces, earlier):
        return pl.pallas_call(
            join_kernel,
            name="own_joined",
            out_shape=jax.ShapeDtypeStruct((len(pieces) * half, size, width), own.dtype),
            in_specs=[VMEM] * (len(pieces) + len(earlier)),
            out_specs=VMEM,
            compiler_params=PARAMS,
        )(*pieces, *earlier)

    away = swap(away)
    home, away = [
        join([part] + [flip(part, mask) for mask in (2, 4, 6)], earlier)
        for part, earlier in ((home, [token]), (away, []))
    ]
    home_core, away_core = flip(home, 1), flip(away, 1)
    source = pl.pallas_call(
        collect_kernel,
        name="own_collected",
        out_shape=pltpu.VMEM((groups, size, width), jnp.bfloat16),
        in_specs=[VMEM] * 3,
        out_specs=VMEM,
        compiler_params=PARAMS,
        cost_estimate=cost(0, 2 * groups * size * width * 2),
    )(home, away, home_core)

    part_a, source = second_call(
        functools.partial(second_part_kernel, 0), half, coefs, own, [in_vmem(source), away_core], True
    )
    other_a = swap(part_a)
    part_b = second_call(functools.partial(second_part_kernel, 1), half, coefs, own, [in_vmem(source)], False)
    other_b = swap(part_b)

    def result(first_row, inputs):
        return pl.pallas_call(
            functools.partial(result_kernel, first_row),
            name="result",
            out_shape=jax.ShapeDtypeStruct((rows, size, width), jnp.bfloat16),
            in_specs=[VMEM, VMEM] + [pl.BlockSpec(memory_space=pltpu.HBM)] * (len(inputs) - 2),
            out_specs=pl.BlockSpec(memory_space=pltpu.HBM),
            scratch_shapes=[pltpu.VMEM(piece.shape, piece.dtype), pltpu.SemaphoreType.DMA],
            input_output_aliases={2: 0} if len(inputs) > 2 else {},
            compiler_params=PARAMS,
        )(*inputs)

    out = result(0, [part_a, other_a])
    return result(half, [part_b, other_b, out]).reshape(rows * size, width)


def solution(mesh):
    return jax.shard_map(
        functools.partial(body, mesh.shape["row"], mesh.shape["col"]),
        mesh=mesh,
        in_specs=(
            P("row", "col", None, None),
            P("row", "col"),
            P("row", "col"),
            P("col", None),
            P("col"),
        ),
        out_specs=P("row", None),
        check_vma=False,
    )
```

```python
import functools

import jax
import jax.numpy as jnp
from jax import lax
from jax.experimental import pallas as pl
from jax.experimental.pallas import tpu as pltpu
from jax.sharding import PartitionSpec as P

VMEM_LIMIT = 12 * 1024 * 1024


def slot_ranges(slots):
    first = min(12, slots)
    return [range(first)] + ([range(first, slots)] if slots > first else [])


def sums_kernel(cols_hbm, counts_hbm, blocks_ref, sums_ref, held_ref, acc_ref, cols_ref, counts_ref, list_sems, sems):
    rows, slots, size, _ = blocks_ref.shape
    groups = acc_ref.shape[0] - 1
    first, *others = slot_ranges(slots)
    others = [range(start, min(start + 12, slots)) for other in others for start in range(other.start, slots, 12)]

    def fetch(b, part):
        span = pl.ds(part.start, len(part))
        return pltpu.make_async_copy(blocks_ref.at[b, span], held_ref.at[b, span], sems.at[b, part.start // 12])

    counts_copy = pltpu.make_async_copy(counts_hbm, counts_ref, list_sems.at[0])
    cols_copy = pltpu.make_async_copy(cols_hbm, cols_ref, list_sems.at[1])
    counts_copy.start()
    cols_copy.start()
    for b in range(rows):
        fetch(b, first).start()
    acc_ref[...] = jnp.zeros_like(acc_ref)
    counts_copy.wait()
    cols_copy.wait()
    def for_heavy_rows(action):
        def one_row(b, carry):
            @pl.when(counts_ref[b] > len(first))
            def _():
                for part in others:
                    action(b, part)

            return carry

        if others:
            lax.fori_loop(0, rows, one_row, 0)

    def add(b, part):
        fetch(b, part).wait()
        for slot in part:
            col = jnp.where(slot < counts_ref[b], cols_ref[b, slot], groups)
            block = held_ref[b, slot].astype(jnp.float32)
            acc_ref[col] += jnp.sum(block.reshape(size // 8, 8, size), axis=0)

    def add_first(b, carry):
        add(b, first)
        return carry

    for_heavy_rows(lambda b, part: fetch(b, part).start())
    lax.fori_loop(0, rows, add_first, 0)
    for_heavy_rows(add)
    sums_ref[...] = jnp.sum(acc_ref[:groups], axis=1)


def multiply_rows(rows, counts_ref, slots, start, gather, acc_ref):
    first, *others = slot_ranges(slots)

    def product(row, part):
        left, right = zip(*[gather(row, slot) for slot in part])
        return jnp.dot(jnp.concatenate(left, axis=1), jnp.concatenate(right, axis=0), preferred_element_type=jnp.float32)

    for b, row in enumerate(rows):
        acc_ref[b] = start(b) + product(row, first)
    def one_row(b, carry):
        row = rows[0] + b
        for part in others:

            @pl.when(counts_ref[row] > part.start)
            def _():
                acc_ref[b] += product(row, part)

        return carry

    if others:
        lax.fori_loop(0, len(rows), one_row, 0)


def scaled_block(row, slot, cols_ref, counts_ref, inverse_ref, blocks_ref):
    size = blocks_ref.shape[2]
    scale = jnp.where(slot < counts_ref[row], inverse_ref[pl.ds(cols_ref[row, slot], 1), :], 0.0)
    scale = jnp.broadcast_to(scale, (16, size)).astype(jnp.bfloat16)
    return (blocks_ref[row, slot].reshape(size // 16, 16, size) * scale).reshape(size, size)


def first_row(sending, count):
    if sending is None:
        return 0
    side = lax.axis_index("col")
    return (1 - side if sending else side) * count


def first_kernel(sending, cols_ref, counts_ref, sums_ref, added_ref, demand_ref, blocks_ref, *rest):
    inverse_ref, acc_ref = rest[-2:]
    if sending:
        out_ref, coef_ref = rest[-3], None
    else:
        out_ref, coef_ref = rest[-4:-2]
    slots = blocks_ref.shape[1]
    count = out_ref.shape[0]
    inverse_ref[...] = 1.0 / (sums_ref[...] + added_ref[...])

    def gather(row, slot):
        coef = scaled_block(row, slot, cols_ref, counts_ref, inverse_ref, blocks_ref)
        if coef_ref is not None:
            coef_ref[row, slot] = coef
        return coef, demand_ref[cols_ref[row, slot]]

    rows = [first_row(sending, count) + b for b in range(count)]
    multiply_rows(rows, counts_ref, slots, lambda b: 0.0, gather, acc_ref)
    out_ref[...] = acc_ref[...].astype(out_ref.dtype)


def scale_kernel(count, cols_ref, counts_ref, sums_ref, added_ref, blocks_ref, coef_ref, token_ref, inverse_ref):
    first, *others = slot_ranges(blocks_ref.shape[1])
    inverse_ref[...] = 1.0 / (sums_ref[...] + added_ref[...])
    token_ref[...] = inverse_ref[:8]

    def scale(row, part):
        for slot in part:
            coef_ref[row, slot] = scaled_block(row, slot, cols_ref, counts_ref, inverse_ref, blocks_ref)

    rows = [first_row(True, count) + b for b in range(count)]

    def one_row(b, carry):
        row = rows[0] + b
        scale(row, first)
        for part in others:

            @pl.when(counts_ref[row] > part.start)
            def _():
                scale(row, part)

        return carry

    lax.fori_loop(0, len(rows), one_row, 0)


def fetch_kernel(demand_hbm, _, demand_ref, sem):
    copy = pltpu.make_async_copy(demand_hbm, demand_ref, sem)
    copy.start()
    copy.wait()


def second_rows(first_row, place, cols_ref, counts_ref, coef_ref, source_ref, start, out_ref, acc_ref):
    slots = coef_ref.shape[1]

    def gather(row, slot):
        return coef_ref[row, slot], source_ref[place(cols_ref[row, slot])]

    rows = [first_row + b for b in range(out_ref.shape[0])]
    multiply_rows(rows, counts_ref, slots, start, gather, acc_ref)
    out_ref[...] = acc_ref[...].astype(out_ref.dtype)


def exact_scale(count, part):
    scale = -(-(1 << 16) // part)
    assert all((i * scale) >> 16 == i // part for i in range(count))
    return scale


HOME = ((0, 0, 0), (0, 1, 0), (1, 0, 0), (1, 1, 0))
AWAY = ((0, 0, 1), (0, 1, 1), (1, 0, 1), (1, 1, 1))


def collect(array, places, core, source_ref):
    part = array.shape[0] // len(places)
    for i, (z, y, away) in enumerate(places):
        at = ((z * 4 + y * 2 + core) * 2 + away) * part
        source_ref[at : at + part] = array[i * part : (i + 1) * part]


def collect_kernel(home_ref, away_ref, home_core_ref, source_ref):
    collect(home_ref, HOME, 0, source_ref)
    collect(away_ref, AWAY, 0, source_ref)
    collect(home_core_ref, HOME, 1, source_ref)


def second_part_kernel(which, cols_ref, counts_ref, coef_ref, own_ref, *rest):
    part = own_ref.shape[0]
    if which == 0:
        _, away_core_ref, out_ref, source_ref, acc_ref = rest
        collect(away_core_ref, AWAY, 1, source_ref)
    else:
        source_ref, out_ref, acc_ref = rest
    side = lax.axis_index("col")
    near = lax.rem(lax.axis_index("row"), 8) * 2 + side
    scale = exact_scale(source_ref.shape[0], part)

    def place(col):
        piece = lax.shift_right_logical(col * scale, 16)
        return col + part * ((piece ^ near) - piece)

    def start(b):
        return jnp.where(side == which, own_ref[b].astype(jnp.float32), 0.0)

    second_rows(which * part, place, cols_ref, counts_ref, coef_ref, source_ref, start, out_ref, acc_ref)


def second_kernel(cols_ref, counts_ref, coef_ref, own_ref, source_ref, out_ref, acc_ref):
    first = lax.axis_index("col") == 0

    def start(b):
        return jnp.where(first, own_ref[b].astype(jnp.float32), 0.0)

    second_rows(0, lambda col: col, cols_ref, counts_ref, coef_ref, source_ref, start, out_ref, acc_ref)


def choose_kernel(own_ref, crossed_ref, _, home_ref, away_ref):
    owner = lax.div(lax.axis_index("row"), 8) == lax.axis_index("col")

    @pl.when(owner)
    def _():
        home_ref[...] = own_ref[...]
        away_ref[...] = crossed_ref[...]

    @pl.when(jnp.logical_not(owner))
    def _():
        home_ref[...] = crossed_ref[...]
        away_ref[...] = own_ref[...]


def join_kernel(*refs):
    pieces, joined_ref = refs[:-1], refs[-1]
    part = pieces[0].shape[0]
    for i, piece in enumerate(pieces):
        joined_ref[i * part : (i + 1) * part] = piece[...]


def result_kernel(first_row, mine_ref, other_ref, *rest):
    out_ref, sum_ref, sem = rest[-3:]
    sum_ref[...] = (mine_ref[...].astype(jnp.float32) + other_ref[...].astype(jnp.float32)).astype(sum_ref.dtype)
    copy = pltpu.make_async_copy(sum_ref, out_ref.at[pl.ds(first_row, sum_ref.shape[0])], sem)
    copy.start()
    copy.wait()


SMEM = pl.BlockSpec(memory_space=pltpu.SMEM)
VMEM = pl.BlockSpec(memory_space=pltpu.VMEM)
PARAMS = pltpu.CompilerParams(vmem_limit_bytes=VMEM_LIMIT)


def cost(flops, bytes_accessed):
    return pl.CostEstimate(flops=flops, bytes_accessed=bytes_accessed, transcendentals=0)


def in_vmem(array):
    return pltpu.with_memory_space_constraint(array, pltpu.VMEM)


def body(n_row, n_col, blocks, slot_cols, counts, demand, value_added):
    rows, slots, size, _ = blocks.shape
    width = demand.shape[1]
    groups = demand.shape[0] // size
    group_devices = n_row // n_col
    paired = n_col == 2 and n_row == 16 and rows % 2 == 0
    half = rows // 2
    counts = counts.reshape(rows)

    sums, held = pl.pallas_call(
        sums_kernel,
        name="column_sums",
        out_shape=(
            jax.ShapeDtypeStruct((groups, size), jnp.float32),
            pltpu.VMEM(blocks.shape, blocks.dtype),
        ),
        in_specs=[pl.BlockSpec(memory_space=pltpu.HBM)] * 3,
        out_specs=(VMEM, VMEM),
        scratch_shapes=[
            pltpu.VMEM((groups + 1, 8, size), jnp.float32),
            pltpu.SMEM(slot_cols.shape, jnp.int32),
            pltpu.SMEM(counts.shape, jnp.int32),
            pltpu.SemaphoreType.DMA((2,)),
            pltpu.SemaphoreType.DMA((rows, -(-slots // 12))),
        ],
        compiler_params=PARAMS,
        cost_estimate=cost(0, 4 * rows * size * size * slots),
    )(*[pltpu.with_memory_space_constraint(array, pltpu.HBM) for array in (slot_cols, counts, blocks)])

    def flip(array, mask):
        return lax.ppermute(array, "row", [(i, i ^ mask) for i in range(n_row)])

    def swap(array):
        return lax.ppermute(array, "col", [(0, 1), (1, 0)])

    if paired:
        for masks in ((1, 2, 3), (4, 12, 8)):
            sums = sums.astype(jnp.bfloat16)
            parts = [sums] + [flip(sums, m) for m in masks]
            if masks[0] == 4:
                demand = pl.pallas_call(
                    fetch_kernel,
                    name="own_demand",
                    out_shape=pltpu.VMEM(demand.shape, demand.dtype),
                    in_specs=[pl.BlockSpec(memory_space=pltpu.HBM), pl.BlockSpec(memory_space=pl.ANY)],
                    out_specs=VMEM,
                    scratch_shapes=[pltpu.SemaphoreType.DMA],
                    compiler_params=PARAMS,
                    cost_estimate=cost(0, 3 * demand.size * 2),
                )(pltpu.with_memory_space_constraint(demand, pltpu.HBM), sums)
            sums = functools.reduce(jnp.add, [part.astype(jnp.float32) for part in parts])
    else:
        sums = lax.psum(sums, "row")

    def layer_cost(count):
        return cost(2 * count * slots * size * size * width, count * slots * size * size * 2)

    def first_layer(sending, count, dtype, held, earlier=()):
        out = jax.ShapeDtypeStruct((count, size, width), dtype)
        return pl.pallas_call(
            functools.partial(first_kernel, sending),
            name="first_layer",
            out_shape=out if sending else (out, pltpu.VMEM(blocks.shape, blocks.dtype)),
            in_specs=[SMEM, SMEM, VMEM, VMEM, VMEM, VMEM] + [pl.BlockSpec(memory_space=pl.ANY)] * len(earlier),
            out_specs=VMEM if sending else (VMEM, VMEM),
            scratch_shapes=[
                pltpu.VMEM((groups, size), jnp.float32),
                pltpu.VMEM((count, size, width), jnp.float32),
            ],
            input_output_aliases={} if sending else {5: 1},
            compiler_params=PARAMS,
            cost_estimate=layer_cost(count),
        )(
            slot_cols,
            counts,
            sums,
            value_added.reshape(groups, size),
            demand.reshape(groups, size, width),
            in_vmem(held),
            *earlier,
        )

    def second_call(kernel, count, coefs, own, sources, keep_sources):
        dtype = jnp.bfloat16 if paired else jnp.float32
        out = jax.ShapeDtypeStruct((count, size, width), dtype)
        return pl.pallas_call(
            kernel,
            name="second_layer",
            out_shape=(out, pltpu.VMEM((groups, size, width), jnp.bfloat16)) if keep_sources else out,
            input_output_aliases={4: 1} if keep_sources else {},
            in_specs=[SMEM, SMEM] + [VMEM] * (2 + len(sources)),
            out_specs=(VMEM, VMEM) if keep_sources else VMEM,
            scratch_shapes=[pltpu.VMEM((count, size, width), jnp.float32)],
            compiler_params=PARAMS,
            cost_estimate=layer_cost(count),
        )(slot_cols, counts, in_vmem(coefs), own, *sources)

    if not paired:
        group = lax.axis_index("col")
        partial, coefs = first_layer(None, rows, jnp.float32, held)
        layer_one = lax.psum(partial, "col").astype(jnp.bfloat16)
        gathered = lax.all_gather(layer_one, "row", axis=0, tiled=True)
        source = lax.dynamic_slice_in_dim(gathered, group * groups, groups, 0)
        partial = second_call(second_kernel, rows, coefs, layer_one, [source], False)
        return lax.psum(partial, "col").astype(jnp.bfloat16).reshape(rows * size, width)

    sent = first_layer(True, half, jnp.bfloat16, held)
    arrived = swap(sent)
    kept, coefs = first_layer(False, half, jnp.float32, held, [sent])
    coefs, token = pl.pallas_call(
        functools.partial(scale_kernel, half),
        name="own_coefficients",
        out_shape=(pltpu.VMEM(blocks.shape, blocks.dtype), jax.ShapeDtypeStruct((8, size), jnp.float32)),
        in_specs=[SMEM, SMEM, VMEM, VMEM, VMEM],
        out_specs=(VMEM, VMEM),
        scratch_shapes=[pltpu.VMEM((groups, size), jnp.float32)],
        input_output_aliases={4: 0},
        compiler_params=PARAMS,
        cost_estimate=layer_cost(half),
    )(slot_cols, counts, sums, value_added.reshape(groups, size), in_vmem(coefs))
    own = (kept + arrived.astype(jnp.float32)).astype(jnp.bfloat16)

    piece = jax.ShapeDtypeStruct(own.shape, own.dtype)
    home, away = pl.pallas_call(
        choose_kernel,
        name="home_and_away",
        out_shape=(piece, piece),
        in_specs=[VMEM] * 3,
        out_specs=(VMEM, VMEM),
        compiler_params=PARAMS,
    )(own, flip(own, group_devices), token)

    def join(pieces):
        return pl.pallas_call(
            join_kernel,
            name="own_joined",
            out_shape=jax.ShapeDtypeStruct((len(pieces) * half, size, width), own.dtype),
            in_specs=[VMEM] * len(pieces),
            out_specs=VMEM,
            compiler_params=PARAMS,
        )(*pieces)

    away = swap(away)
    home, away = [join([part] + [flip(part, mask) for mask in (2, 4, 6)]) for part in (home, away)]
    home_core, away_core = flip(home, 1), flip(away, 1)
    source = pl.pallas_call(
        collect_kernel,
        name="own_collected",
        out_shape=pltpu.VMEM((groups, size, width), jnp.bfloat16),
        in_specs=[VMEM] * 3,
        out_specs=VMEM,
        compiler_params=PARAMS,
        cost_estimate=cost(0, 2 * groups * size * width * 2),
    )(home, away, home_core)

    part_a, source = second_call(
        functools.partial(second_part_kernel, 0), half, coefs, own, [in_vmem(source), away_core], True
    )
    other_a = swap(part_a)
    part_b = second_call(functools.partial(second_part_kernel, 1), half, coefs, own, [in_vmem(source)], False)
    other_b = swap(part_b)

    def result(first_row, inputs):
        return pl.pallas_call(
            functools.partial(result_kernel, first_row),
            name="result",
            out_shape=jax.ShapeDtypeStruct((rows, size, width), jnp.bfloat16),
            in_specs=[VMEM, VMEM] + [pl.BlockSpec(memory_space=pltpu.HBM)] * (len(inputs) - 2),
            out_specs=pl.BlockSpec(memory_space=pltpu.HBM),
            scratch_shapes=[pltpu.VMEM(piece.shape, piece.dtype), pltpu.SemaphoreType.DMA],
            input_output_aliases={2: 0} if len(inputs) > 2 else {},
            compiler_params=PARAMS,
        )(*inputs)

    out = result(0, [part_a, other_a])
    return result(half, [part_b, other_b, out]).reshape(rows * size, width)


def solution(mesh):
    return jax.shard_map(
        functools.partial(body, mesh.shape["row"], mesh.shape["col"]),
        mesh=mesh,
        in_specs=(
            P("row", "col", None, None),
            P("row", "col"),
            P("row", "col"),
            P("col", None),
            P("col"),
        ),
        out_specs=P("row", None),
        check_vma=False,
    )
```
